32 devices in a mesh: batch: 4 (over x, core), row: 4 (over z), col: 2 (over y).
Axes of the slice: x: 2, y: 2, z: 4, core: 2. Of those that a mesh axis runs over, the one named last changes fastest.
Arguments:
- tokens: bfloat16 [16, 112, 56, 256], P('batch', 'row', 'col'), may hold values from -6 to 6
- heights: int32 [16], P('batch'), may hold values from 57 to 112, as said below
- widths: int32 [16], P('batch'), may hold values from 29 to 56, as said below
- keep_flags: int32 [16, 2], P('batch'), may hold values from 0 to 1, as said below
- out_grad: bfloat16 [16, 112, 56, 256], P('batch', 'row', 'col'), may hold values from -6 to 6
- first_gain: float32 [256], replicated, may hold values from 0.5 to 1.5
- first_shift: float32 [256], replicated, may hold values from -2 to 2
- triple_weight: bfloat16 [256, 768], replicated, may hold values from -0.375 to 0.375
- query_value_bias: float32 [2, 256], replicated, may hold values from -3 to 3
- position_kernel: float32 [3, 3, 256], replicated, may hold values from -1 to 1
- position_bias: float32 [256], replicated, may hold values from -2 to 2
- mixing_weight: bfloat16 [256, 256], replicated, may hold values from -1.5 to 1.5
- mixing_bias: float32 [256], replicated, may hold values from -2 to 2
- second_gain: float32 [256], replicated, may hold values from 0.5 to 1.5
- second_shift: float32 [256], replicated, may hold values from -2 to 2
- expand_weight: bfloat16 [256, 1024], replicated, may hold values from -0.375 to 0.375
- expand_bias: float32 [1024], replicated, may hold values from -3 to 3
- reduce_weight: bfloat16 [1024, 256], replicated, may hold values from -0.1875 to 0.1875
- reduce_bias: float32 [256], replicated, may hold values from -2 to 2
Outputs:
- output: bfloat16 [16, 112, 56, 256], P('batch', 'row', 'col')
- tokens_grad: bfloat16 [16, 112, 56, 256], P('batch', 'row', 'col')
- first_gain_grad: float32 [256], replicated
- first_shift_grad: float32 [256], replicated
- triple_weight_grad: float32 [256, 768], replicated
- query_value_bias_grad: float32 [2, 256], replicated
- position_kernel_grad: float32 [3, 3, 256], replicated
- position_bias_grad: float32 [256], replicated
- mixing_weight_grad: float32 [256, 256], replicated
- mixing_bias_grad: float32 [256], replicated
- second_gain_grad: float32 [256], replicated
- second_shift_grad: float32 [256], replicated
- expand_weight_grad: float32 [256, 1024], replicated
- expand_bias_grad: float32 [1024], replicated
- reduce_weight_grad: float32 [1024, 256], replicated
- reduce_bias_grad: float32 [256], replicated
The draws below stay inside these ranges and needn't reach their ends.
Inputs may be any that keep to these rules, and one draw needn't show every extreme that they name: `heights`: in every group of 4 consecutive images one image has the full height 112 and the full width 56. `widths`: the image of full height is also of full width 56. `keep_flags`: the image of full size in each group of 4 consecutive images is kept in both columns.
All inputs are finite; a program needn't handle non-finite values.
Results may differ from the reference program's by a relative error of at most 0.012.
Values may be sent and summed in bfloat16 or wider, within the bound.
No kernel may reach another device: no remote copies, remote signals or barrier semaphores. Data moves between devices by JAX's collectives and lax.ppermute only.
A program may use at most 256 MiB of HBM per device.

```python
import jax
import jax.numpy as jnp
from jax import lax

DIM = 256
HEADS = 8
HIDDEN_SIZE = 1024
STRIPE = 7
IMG_DEV = 4
GRID_H = 112
GRID_W = 56
IMAGES = 16


def chosen_images(key):
    groups = IMAGES // IMG_DEV
    picked = jax.random.randint(jax.random.fold_in(key, 99), (groups,), 0, IMG_DEV)
    return jnp.arange(IMAGES) % IMG_DEV == jnp.repeat(picked, IMG_DEV)


def draw_heights(key, part):
    chosen = chosen_images(key)
    key = jax.random.fold_in(key, 1)
    sampled = jax.random.randint(key, (IMAGES,), GRID_H // 2 + 1, GRID_H + 1)
    return jnp.where(chosen, GRID_H, sampled).astype(jnp.int32)


def draw_widths(key, part):
    chosen = chosen_images(key)
    key = jax.random.fold_in(key, 2)
    sampled = jax.random.randint(key, (IMAGES,), GRID_W // 2 + 1, GRID_W + 1)
    return jnp.where(chosen, GRID_W, sampled).astype(jnp.int32)


def draw_keep_flags(key, part):
    chosen = chosen_images(key)
    key = jax.random.fold_in(key, 3)
    levels = 10 + 85 * jnp.arange(IMAGES) // IMAGES
    sampled = jax.random.randint(key, (IMAGES, 2), 0, 100)
    return ((sampled < levels[:, None]) | chosen[:, None]).astype(jnp.int32)


def steps_of(rng, dims, shards, low, largest):
    def one(axis_at, shards_of):
        draws = jax.random.uniform(jax.random.fold_in(jax.random.fold_in(rng, 6), axis_at), (shards_of,), jnp.float32, low / len(shards), largest / len(shards))
        return jnp.repeat(jnp.exp(draws), dims[axis_at] // shards_of).reshape((-1,) + (1,) * (len(dims) - axis_at - 1))

    level = one(*shards[0])
    for cut in shards[1:]:
        level = level * one(*cut)
    return level


def normal_values(key, dims, scale, most, shards=(), dtype=jnp.bfloat16):
    drawn = jax.random.normal(key, dims, jnp.float32) * scale
    if len(shards) > 0:
        drawn = steps_of(key, dims, shards, -0.22, 0.18) * drawn
    return jnp.clip(drawn, min=-most, max=most).astype(dtype)


def setup_inputs(seed: int = 0) -> dict:
    splits = jax.random.split(jax.random.key(seed), 20)
    tokens = normal_values(splits[0], (IMAGES, GRID_H, GRID_W, DIM), 1.0, 6.0, ((0, 4), (1, 4), (2, 2)))
    heights = draw_heights(jax.random.fold_in(splits[19], 71), 0)
    widths = draw_widths(jax.random.fold_in(splits[19], 71), 0)
    keep_flags = draw_keep_flags(jax.random.fold_in(splits[19], 71), 0)
    out_grad = normal_values(splits[4], (IMAGES, GRID_H, GRID_W, DIM), 1.0, 6.0, ((0, 4), (1, 4), (2, 2)))
    first_gain = jnp.clip(1.0 + 0.1 * jax.random.normal(splits[5], (DIM,), jnp.float32), 0.5, 1.5)
    first_shift = normal_values(splits[6], (DIM,), 0.3, 2.0, (), jnp.float32)
    triple_weight = normal_values(splits[7], (DIM, 3 * DIM), DIM ** -0.5, 0.375)
    query_value_bias = normal_values(splits[8], (2, DIM), 0.5, 3.0, (), jnp.float32)
    position_kernel = normal_values(splits[9], (3, 3, DIM), 0.15, 1.0, (), jnp.float32)
    position_bias = normal_values(splits[10], (DIM,), 0.3, 2.0, (), jnp.float32)
    mixing_weight = normal_values(splits[11], (DIM, DIM), (DIM // 16) ** -0.5, 1.5)
    mixing_bias = normal_values(splits[12], (DIM,), 0.3, 2.0, (), jnp.float32)
    second_gain = jnp.clip(1.0 + 0.1 * jax.random.normal(splits[13], (DIM,), jnp.float32), 0.5, 1.5)
    second_shift = normal_values(splits[14], (DIM,), 0.3, 2.0, (), jnp.float32)
    expand_weight = normal_values(splits[15], (DIM, HIDDEN_SIZE), DIM ** -0.5, 0.375)
    expand_bias = normal_values(splits[16], (HIDDEN_SIZE,), 0.5, 3.0, (), jnp.float32)
    reduce_weight = normal_values(splits[17], (HIDDEN_SIZE, DIM), HIDDEN_SIZE ** -0.5, 0.1875)
    reduce_bias = normal_values(splits[18], (DIM,), 0.3, 2.0, (), jnp.float32)
    return dict(tokens=tokens, heights=heights, widths=widths, keep_flags=keep_flags, out_grad=out_grad, first_gain=first_gain, first_shift=first_shift, triple_weight=triple_weight, query_value_bias=query_value_bias, position_kernel=position_kernel, position_bias=position_bias, mixing_weight=mixing_weight, mixing_bias=mixing_bias, second_gain=second_gain, second_shift=second_shift, expand_weight=expand_weight, expand_bias=expand_bias, reduce_weight=reduce_weight, reduce_bias=reduce_bias)


highest = lax.Precision.HIGHEST

@jax.custom_vjp
def low(v):
    return lax.optimization_barrier(v.astype(jnp.bfloat16)).astype(jnp.float32)

@jax.custom_vjp
def low_back(v):
    return v

def low_keep(v):
    return (low(v), None)

def low_pass(kept, grad):
    return (grad,)

def back_keep(v):
    return (v, None)

def back_low(kept, grad):
    return (low(grad),)
low.defvjp(low_keep, low_pass)
low_back.defvjp(back_keep, back_low)

def layer_norm(source, gain_row, shift_row):
    average = lax.optimization_barrier(jnp.mean(source, axis=-1, keepdims=True))
    centered = source - average
    spread = lax.optimization_barrier(jnp.mean(centered * centered, axis=-1, keepdims=True))
    return centered * lax.rsqrt(spread + 1e-05) * gain_row + shift_row

def rows_layout(source, head_count):
    row_count, col_count, features = source.shape
    head_size = features // head_count
    shaped = source.reshape(row_count // STRIPE, STRIPE, col_count, head_count, head_size)
    return shaped.transpose(0, 3, 1, 2, 4).reshape(row_count // STRIPE, head_count, STRIPE * col_count, head_size)

def rows_back(source, col_count):
    groups, head_count, length, head_size = source.shape
    shaped = source.reshape(groups, head_count, STRIPE, col_count, head_size)
    return shaped.transpose(0, 2, 3, 1, 4).reshape(groups * STRIPE, col_count, head_count * head_size)

def cols_layout(source, head_count):
    row_count, col_count, features = source.shape
    head_size = features // head_count
    shaped = source.reshape(row_count, col_count // STRIPE, STRIPE, head_count, head_size)
    return shaped.transpose(1, 3, 0, 2, 4).reshape(col_count // STRIPE, head_count, row_count * STRIPE, head_size)

def cols_back(source, row_count):
    groups, head_count, length, head_size = source.shape
    shaped = source.reshape(groups, head_count, row_count, STRIPE, head_size)
    return shaped.transpose(2, 0, 3, 1, 4).reshape(row_count, groups * STRIPE, head_count * head_size)

def rows_mask(valid):
    row_count, col_count = valid.shape
    return valid.reshape(row_count // STRIPE, STRIPE * col_count)

def cols_mask(valid):
    row_count, col_count = valid.shape
    return valid.reshape(row_count, col_count // STRIPE, STRIPE).transpose(1, 0, 2).reshape(col_count // STRIPE, row_count * STRIPE)

def conv_rows(source, kernel, bias_row):
    row_count, col_count, channels = source.shape
    blocks = source.reshape(row_count // STRIPE, STRIPE, col_count, channels)
    padded = jnp.pad(blocks, ((0, 0), (1, 1), (1, 1), (0, 0)))
    summed = bias_row
    for offset_row in range(3):
        for offset_col in range(3):
            summed = summed + padded[:, offset_row:offset_row + STRIPE, offset_col:offset_col + col_count] * kernel[offset_row, offset_col]
    return summed.reshape(row_count, col_count, channels)

def conv_cols(source, kernel, bias_row):
    row_count, col_count, channels = source.shape
    blocks = source.reshape(row_count, col_count // STRIPE, STRIPE, channels)
    padded = jnp.pad(blocks, ((1, 1), (0, 0), (1, 1), (0, 0)))
    summed = bias_row
    for offset_row in range(3):
        for offset_col in range(3):
            summed = summed + padded[offset_row:offset_row + row_count, :, offset_col:offset_col + STRIPE] * kernel[offset_row, offset_col]
    return summed.reshape(row_count, col_count, channels)

def attend(queries, keys, values, valid):
    scaling = queries.shape[-1] ** (-0.5)
    scores = jnp.einsum('ghqd,ghkd->ghqk', queries, keys, precision=highest) * scaling
    scores = low_back(jnp.where(valid[:, None, None, :], scores, -1e+30))
    highest_score = lax.optimization_barrier(jnp.max(scores, axis=-1, keepdims=True))
    weights = jnp.exp(scores - highest_score)
    soft = low(weights / lax.optimization_barrier(jnp.sum(weights, axis=-1, keepdims=True)))
    return jnp.einsum('ghqk,ghkd->ghqd', soft, values, precision=highest)

def stripe_branch(queries, keys, values, valid, kernel, bias_row, across):
    head_count = HEADS // 2
    masked = values * valid[..., None].astype(jnp.float32)
    if across:
        attended = attend(rows_layout(queries, head_count), rows_layout(keys, head_count), rows_layout(values, head_count), rows_mask(valid))
        return rows_back(attended, queries.shape[1]) + conv_rows(masked, kernel, bias_row)
    attended = attend(cols_layout(queries, head_count), cols_layout(keys, head_count), cols_layout(values, head_count), cols_mask(valid))
    return cols_back(attended, queries.shape[0]) + conv_cols(masked, kernel, bias_row)

def block(source, valid, factor, params):
    first_gain, first_shift, triple_weight, query_value_bias, position_kernel, position_bias, mixing_weight, mixing_bias, second_gain, second_shift, expand_weight, expand_bias, reduce_weight, reduce_bias = params
    allowed = valid.astype(jnp.float32)
    half = DIM // 2
    flat = source.reshape(-1, DIM)
    normed = low(layer_norm(flat, first_gain, first_shift))
    bias_full = jnp.concatenate([query_value_bias[0], jnp.zeros((DIM,), jnp.float32), query_value_bias[1]])
    triple = low(low_back(jnp.dot(normed, triple_weight, precision=highest) + bias_full))
    triple = triple.reshape(GRID_H, GRID_W, 3 * DIM)
    queries = triple[..., :DIM]
    keys_all = triple[..., DIM:2 * DIM]
    values_all = triple[..., 2 * DIM:]
    across_out = stripe_branch(queries[..., :half], keys_all[..., :half], values_all[..., :half], valid, position_kernel[..., :half], position_bias[:half], True)
    down_out = stripe_branch(queries[..., half:], keys_all[..., half:], values_all[..., half:], valid, position_kernel[..., half:], position_bias[half:], False)
    joined = low(low_back(jnp.concatenate([across_out, down_out], axis=-1).reshape(-1, DIM)))
    mixed = low_back(jnp.dot(joined, mixing_weight, precision=highest) + mixing_bias)
    middle = flat + (factor[0] * allowed).reshape(-1, 1) * mixed
    normed_two = low(layer_norm(middle, second_gain, second_shift))
    hidden_pre = low_back(jnp.dot(normed_two, expand_weight, precision=highest) + expand_bias)
    hidden_act = low(jax.nn.gelu(hidden_pre))
    reduced = low_back(jnp.dot(hidden_act, reduce_weight, precision=highest) + reduce_bias)
    return (middle + (factor[1] * allowed).reshape(-1, 1) * reduced).reshape(source.shape)

def reference(tokens, heights, widths, keep_flags, out_grad, first_gain, first_shift, triple_weight, query_value_bias, position_kernel, position_bias, mixing_weight, mixing_bias, second_gain, second_shift, expand_weight, expand_bias, reduce_weight, reduce_bias):
    params = tuple((item.astype(jnp.float32) for item in (first_gain, first_shift, triple_weight, query_value_bias, position_kernel, position_bias, mixing_weight, mixing_bias, second_gain, second_shift, expand_weight, expand_bias, reduce_weight, reduce_bias)))
    kept = lax.optimization_barrier(jnp.sum(keep_flags.astype(jnp.float32), axis=0)) / IMAGES
    factors = keep_flags.astype(jnp.float32) / kept
    row_ids = jnp.arange(GRID_H).astype(jnp.int32)
    col_ids = jnp.arange(GRID_W).astype(jnp.int32)

    def per_image(carry, item):
        image, height, width, factor, cotangent = item
        valid = (row_ids[:, None] < height) & (col_ids[None, :] < width)

        def forward(source, weights):
            return block(source, valid, factor, weights)
        result, pull = jax.vjp(forward, image.astype(jnp.float32), params)
        source_grad, weight_grads = pull(cotangent.astype(jnp.float32))
        carry = tuple((summed + piece for summed, piece in zip(carry, weight_grads)))
        return (carry, (result.astype(jnp.bfloat16), source_grad.astype(jnp.bfloat16)))
    start = tuple((jnp.zeros(item.shape, jnp.float32) for item in params))
    sums, outputs = lax.scan(per_image, start, (tokens, heights, widths, factors, out_grad))
    return (outputs[0], outputs[1], sums[0], sums[1], sums[2], sums[3], sums[4], sums[5], sums[6], sums[7], sums[8], sums[9], sums[10], sums[11], sums[12], sums[13])
```

```python
import functools

import jax
import jax.numpy as jnp
from jax import lax
from jax.experimental import pallas as pl
from jax.experimental.pallas import tpu as pltpu
from jax.sharding import PartitionSpec as P

DIM = 256
HALF = 128
HEADS = 4
SIZE = 32
STRIPE = 7
ROWS = 28
SLOT = 8
PIX = ROWS * SLOT
HIDDEN = 1024
F32 = jnp.float32
BF16 = jnp.bfloat16
LOG2E = 1.4426950408889634
SCALE = SIZE**-0.5
EPS = 1e-05
GELU_C = 0.7978845608028654
GELU_A = 0.044715
VMEM_LIMIT = 56 * 1024 * 1024


def nn(a, b):
    return lax.dot_general(a, b, (((1,), (0,)), ((), ())), preferred_element_type=F32)


def nt(a, b):
    return lax.dot_general(a, b, (((1,), (1,)), ((), ())), preferred_element_type=F32)


def tn(a, b):
    return lax.dot_general(a, b, (((0,), (0,)), ((), ())), preferred_element_type=F32)


def col_sum(v):
    return jnp.sum(v, axis=0, keepdims=True)


def normalize(source):
    average = jnp.mean(source, axis=-1, keepdims=True)
    centered = source - average
    spread = jnp.mean(centered * centered, axis=-1, keepdims=True)
    rstd = lax.rsqrt(spread + EPS)
    return centered * rstd, rstd


def norm_back(grad_hat, hat, rstd):
    return rstd * (
        grad_hat
        - jnp.mean(grad_hat, axis=-1, keepdims=True)
        - hat * jnp.mean(grad_hat * hat, axis=-1, keepdims=True)
    )


def head_lanes(shape):
    return lax.broadcasted_iota(jnp.int32, shape, len(shape) - 1) // SIZE


def split_cols(source, wide, parts):
    wide[:, 0:ROWS, :] = source.astype(F32)
    slot = lax.broadcasted_iota(jnp.int32, (ROWS, SLOT, DIM), 1)
    for s in range(4):
        parts[s] = jnp.where(slot < STRIPE, wide[:, STRIPE * s : STRIPE * s + SLOT, :], 0.0)


def merge_cols(parts, wide):
    for s in range(4):
        wide[:, STRIPE * s : STRIPE * s + SLOT, :] = parts[s]
    return wide[:, 0:ROWS, :]


class Meta:
    def __init__(self, ref, count):
        self.ref = ref
        self.count = count

    def height(self, i):
        return self.ref[i]

    def width(self, i):
        return self.ref[self.count + i]

    def keep(self, i):
        return self.ref[2 * self.count + i]

    def feed(self, i):
        return self.ref[3 * self.count + i]

    def row(self):
        return self.ref[4 * self.count]

    def col(self):
        return self.ref[4 * self.count + 1]


def prep_kernel(count, first, meta_ref, tok_ref, d0, d1, d2, d3, keep_ref, send_ref, wide, parts):
    meta = Meta(meta_ref, count)
    split_cols(tok_ref[0], wide, parts)
    r, c = meta.row(), meta.col()
    for k, out in enumerate((d0, d1, d2, d3)):
        out[0] = parts[lax.rem(r + k, 4)].reshape(PIX, DIM).astype(BF16)
    for u in range(2):
        for out, pair in ((keep_ref, 1 - c), (send_ref, c)):
            t = 2 * pair + u
            piece = parts[:, pl.ds(STRIPE * t, STRIPE)]
            out[0, u] = piece.reshape(PIX, DIM).astype(BF16)


def down_mask(height, width, stripe):
    shape = (4 * ROWS, SLOT, HALF)
    row = lax.broadcasted_iota(jnp.int32, shape, 0)
    j = lax.broadcasted_iota(jnp.int32, shape, 1)
    limit = jnp.minimum(STRIPE, width - STRIPE * stripe)
    return jnp.where((row < height) & (j < limit), 1.0, 0.0)


def across_mask(height, width, stripe):
    shape = (8, STRIPE, SLOT, HALF)
    b = lax.broadcasted_iota(jnp.int32, shape, 0)
    row = lax.broadcasted_iota(jnp.int32, shape, 1)
    j = lax.broadcasted_iota(jnp.int32, shape, 2)
    good = (row < height - STRIPE * stripe) & (j < STRIPE) & (b * STRIPE + j < width)
    return jnp.where(good, 1.0, 0.0)


def moved_rows(v, axis, step):
    if step == 0:
        return v
    size = v.shape[axis]
    zero_shape = v.shape[:axis] + (1,) + v.shape[axis + 1 :]
    zero = jnp.zeros(zero_shape, v.dtype)
    if step > 0:
        return jnp.concatenate([lax.slice_in_dim(v, 1, size, axis=axis), zero], axis=axis)
    return jnp.concatenate([zero, lax.slice_in_dim(v, 0, size - 1, axis=axis)], axis=axis)


def roll8(v, shift):
    shape = v.shape
    flat = v.reshape(-1, SLOT, HALF)
    return pltpu.roll(flat, shift, 1).reshape(shape)


def moved_cols_down(v, step):
    if step == 0:
        return v
    return roll8(v, 1 if step < 0 else SLOT - 1)


def moved_cols_across(v, step):
    if step == 0:
        return v
    slot = lax.broadcasted_iota(jnp.int32, v.shape, 2)
    if step < 0:
        return jnp.where(slot == 0, moved_rows(roll8(v, 2), 0, -1), roll8(v, 1))
    return jnp.where(slot == STRIPE - 1, moved_rows(roll8(v, SLOT - 2), 0, 1), roll8(v, SLOT - 1))


def taps(v, across):
    moved_cols = moved_cols_across if across else moved_cols_down
    row_axis = 1 if across else 0
    for b in range(3):
        side = moved_cols(v, b - 1)
        for a in range(3):
            yield a, b, moved_rows(side, row_axis, a - 1)


def position_term(v, kern_ref, bias_ref, lanes, across):
    total = bias_ref[0:1, lanes]
    for a, b, moved in taps(v, across):
        total = total + moved * kern_ref[3 * a + b : 3 * a + b + 1, lanes]
    return total


def position_back(grad, v, kern_ref, lanes, across):
    total = 0.0
    for a, b, moved in taps(grad, across):
        k = 3 * (2 - a) + (2 - b)
        total = total + moved * kern_ref[k : k + 1, lanes]
    kernel_grads = []
    flat = grad.reshape(-1, HALF)
    found = {}
    for a, b, moved in taps(v, across):
        found[3 * a + b] = col_sum(flat * moved.reshape(-1, HALF))
    for k in range(9):
        kernel_grads.append(found[k])
    return total, kernel_grads, col_sum(flat)


def attend_forward(blocks, active, x_ref, mask, weight_ref, bias_ref, gain_ref, shift_ref,
                   q_out, k_out, v_out, at_out, lse_out, key_ref, query_ref, value_ref, a_ref):
    n = blocks * PIX

    def project(b, carry):
        hat, unused = normalize(x_ref[b].astype(F32))
        normed = (hat * gain_ref[...] + shift_ref[...]).astype(BF16)
        triple = (nn(normed, weight_ref[...]) + bias_ref[...]).astype(BF16)
        q_out[b] = triple[:, 0:HALF]
        k_out[b] = triple[:, HALF : 2 * HALF]
        v_out[b] = triple[:, 2 * HALF :]
        return carry

    lax.fori_loop(0, blocks, project, 0)
    prepare_keys(blocks, mask, k_out, key_ref)
    prepare_queries(blocks, q_out, query_ref)
    masked = v_out[...].reshape(n, HALF).astype(F32) * mask
    turned = masked.T
    flags = mask.T[0:16]
    for h in range(HEADS):
        value_ref[h] = jnp.concatenate([turned[SIZE * h : SIZE * h + SIZE], flags], 0).astype(BF16)

    def attend(q, carry):
        keys = key_ref[...]
        keys = jnp.concatenate([keys, keys], axis=1)
        pieces, sums = [], []
        for h in range(HEADS):
            scores = nt(keys, query_ref[h, q])
            top = jnp.max(scores, axis=0, keepdims=True)
            weights = jnp.exp2(scores - top).astype(BF16)
            out = nn(value_ref[h], weights)
            total = out[SIZE : SIZE + 1]
            pieces.append(out[0:SIZE] / total)
            sums.append(top + jnp.log2(total))
        joined = jnp.concatenate(pieces, axis=0)
        at_out[q] = joined
        lse_out[q] = jnp.concatenate(sums + sums, axis=0)
        a_ref[q] = joined.T
        return carry

    lax.fori_loop(0, active, attend, 0)

    def clear(q, carry):
        a_ref[q] = jnp.zeros((PIX, HALF), F32)
        return carry

    lax.fori_loop(active, blocks, clear, 0)
    return masked


def prepare_keys(blocks, mask, k_ref, key_ref):
    keys = k_ref[...].reshape(blocks * PIX, HALF).astype(F32)
    key_ref[...] = jnp.where(mask > 0.0, keys, keys[0:1]).astype(BF16)


def prepare_queries(blocks, q_ref, query_ref):
    def one(b, carry):
        query = q_ref[b].astype(F32) * (SCALE * LOG2E)
        high = query.astype(BF16)
        low = (query - high.astype(F32)).astype(BF16)
        both = jnp.concatenate([high, low], axis=1)
        lane = lax.broadcasted_iota(jnp.int32, (PIX, 2 * HALF), 1)
        head = lax.rem(lane, HALF) // SIZE
        for h in range(HEADS):
            query_ref[h, b] = jnp.where(head == h, both, jnp.zeros_like(both))
        return carry

    lax.fori_loop(0, blocks, one, 0)


def active_down(height):
    return (height + ROWS - 1) // ROWS


def forward_kernel(count, first, meta_ref, xd0, xd1, xd2, xd3, xa_keep, xa_recv,
                   wd_ref, wa_ref, bd_ref, ba_ref, gain_ref, shift_ref, kern_ref, pos_ref,
                   jd0, jd1, jd2, jd3, ja_keep, ja_send,
                   qd, kd, vd, atd, lsed, qa, ka, va, ata, lsea,
                   xd, key_d, query_d, value_d, a_d, xa, key_a, query_a, value_a, a_a):
    meta = Meta(meta_ref, count)
    i = first + pl.program_id(0)
    r, c = meta.row(), meta.col()
    height, width = meta.height(i), meta.width(i)
    down_stripe = 4 * c + r
    down_live = (meta.keep(i) > 0) & (STRIPE * down_stripe < width)

    @pl.when(down_live)
    def _():
        for k, ref in enumerate((xd0, xd1, xd2, xd3)):
            xd[lax.rem(r + 4 - k, 4)] = ref[0]
        mask3 = down_mask(height, width, down_stripe)
        masked = attend_forward(
            4, active_down(height), xd, mask3.reshape(4 * PIX, HALF), wd_ref, bd_ref, gain_ref, shift_ref,
            qd.at[0], kd.at[0], vd.at[0], atd.at[0], lsed.at[0], key_d, query_d, value_d, a_d)
        term = position_term(masked.reshape(4 * ROWS, SLOT, HALF), kern_ref, pos_ref, slice(HALF, DIM), False)
        a_d[...] = a_d[...] + term.reshape(4, PIX, HALF)

    @pl.when(jnp.logical_not(down_live))
    def _():
        a_d[...] = jnp.zeros_like(a_d)

    for k, ref in enumerate((jd0, jd1, jd2, jd3)):
        ref[0] = a_d[lax.rem(r + k, 4)].astype(BF16)

    for u in range(2):
        stripe = 4 * r + 2 * (1 - c) + u
        live = (meta.keep(i) > 0) & (STRIPE * stripe < height)

        @pl.when(live)
        def _():
            xa[c] = xa_keep[0, u]
            xa[1 - c] = xa_recv[0, u]
            mask4 = across_mask(height, width, stripe)
            masked = attend_forward(
                2, 2, xa, mask4.reshape(2 * PIX, HALF), wa_ref, ba_ref, gain_ref, shift_ref,
                qa.at[0, u], ka.at[0, u], va.at[0, u], ata.at[0, u], lsea.at[0, u],
                key_a, query_a, value_a, a_a)
            term = position_term(masked.reshape(8, STRIPE, SLOT, HALF), kern_ref, pos_ref, slice(0, HALF), True)
            a_a[...] = a_a[...] + term.reshape(2, PIX, HALF)

        @pl.when(jnp.logical_not(live))
        def _():
            a_a[...] = jnp.zeros_like(a_a)

        ja_keep[0, u] = a_a[c].astype(BF16)
        ja_send[0, u] = a_a[1 - c].astype(BF16)


def pixel_mask(height, width, first_block, blocks, r, c):
    shape = (blocks, ROWS, SLOT, HALF)
    s = lax.broadcasted_iota(jnp.int32, shape, 0) + first_block
    row = lax.broadcasted_iota(jnp.int32, shape, 1)
    j = lax.broadcasted_iota(jnp.int32, shape, 2)
    good = (row < height - ROWS * r) & (j < STRIPE) & (s * STRIPE + j < width - ROWS * c)
    mask = jnp.where(good, 1.0, 0.0).reshape(blocks * PIX, HALF)
    return jnp.concatenate([mask, mask], axis=1)


def middle_kernel(count, first, meta_ref, fact_ref, xd0, xd1, xd2, xd3, jd0, jd1, jd2, jd3, ja_keep, ja_recv, grad_ref,
                  wm_ref, bm_ref, gain_ref, shift_ref, we_ref, be_ref, wr_ref, br_ref, in_r, in_e, in_m, in_v,
                  out_ref, dm_ref, dd0, dd1, dd2, dd3, da_keep, da_send, acc_r, acc_e, acc_m, acc_v,
                  x_ref, g_ref, ja_ref, j_ref, o_ref, dj_ref, wide):
    meta = Meta(meta_ref, count)
    step = pl.program_id(0)
    i = first + step
    r, c = meta.row(), meta.col()
    height, width = meta.height(i), meta.width(i)
    attend_factor = fact_ref[2 * i]
    feed_factor = fact_ref[2 * i + 1]

    @pl.when(step == 0)
    def _():
        acc_r[...] = in_r[...]
        acc_e[...] = in_e[...]
        acc_m[...] = in_m[...]
        acc_v[...] = in_v[...]

    split_cols(grad_ref[0], wide, g_ref)
    for k, (xs, js) in enumerate(((xd0, jd0), (xd1, jd1), (xd2, jd2), (xd3, jd3))):
        x_ref[lax.rem(r + k, 4)] = xs[0]
        j_ref[lax.rem(r + 4 - k, 4), :, HALF:] = js[0]
    for u in range(2):
        for source, pair in ((ja_keep, 1 - c), (ja_recv, c)):
            t = 2 * pair + u
            ja_ref[:, pl.ds(STRIPE * t, STRIPE)] = source[0, u].astype(F32).reshape(4, STRIPE, SLOT, HALF)
    j_ref[:, :, 0:HALF] = ja_ref[...].reshape(4, PIX, HALF).astype(BF16)

    group = 2
    size = group * PIX

    def one(b, carry):
        where = pl.ds(group * b, group)
        mask = pixel_mask(height, width, group * b, group, r, c)
        scale_attend = mask * attend_factor
        scale_feed = mask * feed_factor
        x = x_ref[where].reshape(size, DIM).astype(F32)
        joined = j_ref[where].reshape(size, DIM)
        g = g_ref[where].reshape(size, DIM)
        mixed = nn(joined, wm_ref[...]) + bm_ref[...]
        middle = x + scale_attend * mixed
        hat, rstd = normalize(middle)
        normed = (hat * gain_ref[...] + shift_ref[...]).astype(BF16)
        d_reduced = (scale_feed * g).astype(BF16)
        pre = nn(normed, we_ref[...]) + be_ref[...]
        square = pre * pre
        bend = jnp.tanh(pre * (GELU_C + (GELU_C * GELU_A) * square))
        half_one = 0.5 + 0.5 * bend
        act = (pre * half_one).astype(BF16)
        slope = half_one + (0.5 * pre) * (1.0 - bend * bend) * (GELU_C + (3.0 * GELU_C * GELU_A) * square)
        reduced = nn(act, wr_ref[...]) + br_ref[...]
        o_ref[where] = (middle + scale_feed * reduced).reshape(group, ROWS, SLOT, DIM)
        acc_r[...] += tn(d_reduced, act)
        d_act = nt(d_reduced, wr_ref[...])
        d_hidden = d_act * slope
        d_hidden_low = d_hidden.astype(BF16)
        acc_e[...] += tn(normed, d_hidden_low)
        d_hidden_sum = col_sum(d_hidden_low.astype(F32))
        d_normed = nt(d_hidden_low, we_ref[...])
        d_middle = g + norm_back(d_normed * gain_ref[...], hat, rstd)
        dm_ref[0, where] = d_middle.reshape(group, PIX, DIM)
        d_mixed = (scale_attend * d_middle).astype(BF16)
        acc_m[...] += tn(joined, d_mixed)
        dj_ref[where] = nt(d_mixed, wm_ref[...]).reshape(group, ROWS, SLOT, DIM)
        rows = [d_hidden_sum[:, DIM * k : DIM * k + DIM] for k in range(4)]
        rows.append(col_sum(d_reduced.astype(F32)))
        rows.append(col_sum(d_normed * hat))
        rows.append(col_sum(d_normed))
        rows.append(col_sum(d_mixed.astype(F32)))
        acc_v[...] += jnp.concatenate(rows, axis=0)
        return carry

    lax.fori_loop(0, 4 // group, one, 0)
    out_ref[0] = merge_cols(o_ref, wide).astype(BF16)
    for k, ref in enumerate((dd0, dd1, dd2, dd3)):
        ref[0] = dj_ref[lax.rem(r + k, 4), :, :, HALF:].reshape(PIX, HALF).astype(BF16)
    for u in range(2):
        for ref, pair in ((da_keep, 1 - c), (da_send, c)):
            t = 2 * pair + u
            ref[0, u] = dj_ref[:, pl.ds(STRIPE * t, STRIPE), :, 0:HALF].reshape(PIX, HALF).astype(BF16)


def attend_backward(blocks, active, across, lanes, x_ref, mask, weight_ref, gain_ref, shift_ref, kern_ref,
                    q_ref, k_ref, v_ref, at_ref, lse_ref, da_ref, out_ref, acc_w, acc_v,
                    key_ref, query_ref, turned_ref, dq_ref, dk_ref, dv_ref):
    n = blocks * PIX
    prepare_keys(blocks, mask, k_ref, key_ref)
    prepare_queries(blocks, q_ref, query_ref)
    turned_ref[...] = (k_ref[...].reshape(n, HALF).astype(F32) * mask).T.astype(BF16)
    grid = (8, STRIPE, SLOT, HALF) if across else (4 * ROWS, SLOT, HALF)
    masked = v_ref[...].reshape(n, HALF).astype(F32) * mask
    grad = da_ref[...].reshape(n, HALF).astype(F32)
    back, kernel_rows, bias_row = position_back(grad.reshape(grid), masked.reshape(grid), kern_ref, lanes, across)
    dv_ref[...] = back.reshape(n, HALF)
    dk_ref[...] = jnp.zeros((n, HALF), F32)
    acc_v[4:14, lanes] += jnp.concatenate([bias_row] + kernel_rows, axis=0)

    def attend(q, carry):
        keys = key_ref[...]
        keys = jnp.concatenate([keys, keys], axis=1)
        values = v_ref[...].reshape(n, HALF)
        up = da_ref[q]
        query = q_ref[q]
        product = up.astype(F32).T * at_ref[q]
        head = head_lanes((PIX, HALF))
        dk, dv, dq = 0.0, 0.0, []
        for h in range(HEADS):
            up_h = jnp.where(head == h, up, jnp.zeros_like(up))
            query_h = jnp.where(head == h, query, jnp.zeros_like(query))
            soft = jnp.exp2(nt(keys, query_ref[h, q]) - lse_ref[q, h : h + 1])
            delta = col_sum(product[SIZE * h : SIZE * h + SIZE])
            score = (soft * (nt(values, up_h) - delta)).astype(BF16)
            dv = dv + nn(soft.astype(BF16), up_h)
            dk = dk + nn(score, query_h)
            dq.append(nn(turned_ref[SIZE * h : SIZE * h + SIZE], score))
        dv_ref[...] += dv
        dk_ref[...] += dk
        dq_ref[q] = jnp.concatenate(dq, axis=0).T * SCALE
        return carry

    lax.fori_loop(0, active, attend, 0)

    def clear(q, carry):
        dq_ref[q] = jnp.zeros((PIX, HALF), F32)
        return carry

    lax.fori_loop(active, blocks, clear, 0)
    dv_ref[...] = dv_ref[...] * mask
    dk_ref[...] = dk_ref[...] * (mask * SCALE)

    def finish(b, carry):
        part = pl.ds(pl.multiple_of(b * PIX, PIX), PIX)
        triple = jnp.concatenate([dq_ref[b], dk_ref[part], dv_ref[part]], axis=1).astype(BF16)
        hat, rstd = normalize(x_ref[b].astype(F32))
        normed = (hat * gain_ref[...] + shift_ref[...]).astype(BF16)
        acc_w[...] += tn(normed, triple)
        d_normed = nt(triple, weight_ref[...])
        sums = col_sum(triple.astype(F32))
        acc_v[0:1] += col_sum(d_normed * hat)
        acc_v[1:2] += col_sum(d_normed)
        acc_v[2:3, lanes] += sums[:, 0:HALF]
        acc_v[3:4, lanes] += sums[:, 2 * HALF :]
        out_ref[b] = norm_back(d_normed * gain_ref[...], hat, rstd).astype(BF16)
        return carry

    lax.fori_loop(0, blocks, finish, 0)


def backward_kernel(count, first, meta_ref, xd0, xd1, xd2, xd3, xa_keep, xa_recv, dd0, dd1, dd2, dd3, da_keep, da_recv,
                    qd, kd, vd, atd, lsed, qa, ka, va, ata, lsea, wd_ref, wa_ref, gain_ref, shift_ref, kern_ref,
                    in_wd, in_wa, in_v,
                    pd0, pd1, pd2, pd3, pa_keep, pa_send, acc_wd, acc_wa, acc_v,
                    xd, key_d, query_d, turned_d, dq_d, dk_d, dv_d, up_d, part_d,
                    xa, key_a, query_a, turned_a, dq_a, dk_a, dv_a, up_a, part_a):
    meta = Meta(meta_ref, count)
    step = pl.program_id(0)
    i = first + step
    r, c = meta.row(), meta.col()
    height, width = meta.height(i), meta.width(i)

    @pl.when(step == 0)
    def _():
        acc_wd[...] = in_wd[...]
        acc_wa[...] = in_wa[...]
        acc_v[...] = in_v[...]

    down_stripe = 4 * c + r
    down_live = (meta.keep(i) > 0) & (STRIPE * down_stripe < width)

    @pl.when(down_live)
    def _():
        for k, (xs, ds) in enumerate(((xd0, dd0), (xd1, dd1), (xd2, dd2), (xd3, dd3))):
            q = lax.rem(r + 4 - k, 4)
            xd[q] = xs[0]
            up_d[q] = ds[0]
        mask = down_mask(height, width, down_stripe).reshape(4 * PIX, HALF)
        attend_backward(4, active_down(height), False, slice(HALF, DIM), xd, mask, wd_ref, gain_ref, shift_ref, kern_ref,
                        qd.at[0], kd.at[0], vd.at[0], atd.at[0], lsed.at[0], up_d, part_d, acc_wd, acc_v,
                        key_d, query_d, turned_d, dq_d, dk_d, dv_d)

    @pl.when(jnp.logical_not(down_live))
    def _():
        part_d[...] = jnp.zeros_like(part_d)

    for k, ref in enumerate((pd0, pd1, pd2, pd3)):
        ref[0] = part_d[lax.rem(r + k, 4)]

    for u in range(2):
        stripe = 4 * r + 2 * (1 - c) + u
        live = (meta.keep(i) > 0) & (STRIPE * stripe < height)

        @pl.when(live)
        def _():
            xa[c] = xa_keep[0, u]
            xa[1 - c] = xa_recv[0, u]
            up_a[c] = da_keep[0, u]
            up_a[1 - c] = da_recv[0, u]
            mask = across_mask(height, width, stripe).reshape(2 * PIX, HALF)
            attend_backward(2, 2, True, slice(0, HALF), xa, mask, wa_ref, gain_ref, shift_ref, kern_ref,
                            qa.at[0, u], ka.at[0, u], va.at[0, u], ata.at[0, u], lsea.at[0, u],
                            up_a, part_a, acc_wa, acc_v,
                            key_a, query_a, turned_a, dq_a, dk_a, dv_a)

        @pl.when(jnp.logical_not(live))
        def _():
            part_a[...] = jnp.zeros_like(part_a)

        pa_keep[0, u] = part_a[c]
        pa_send[0, u] = part_a[1 - c]


def finish_kernel(count, first, meta_ref, dm_ref, pd0, pd1, pd2, pd3, pa_keep, pa_recv, out_ref, total, wide):
    meta = Meta(meta_ref, count)
    r, c = meta.row(), meta.col()
    total[...] = dm_ref[0].reshape(4, ROWS, SLOT, DIM)
    for k, ref in enumerate((pd0, pd1, pd2, pd3)):
        s = lax.rem(r + 4 - k, 4)
        total[s] += ref[0].astype(F32).reshape(ROWS, SLOT, DIM)
    for u in range(2):
        for ref, pair in ((pa_keep, 1 - c), (pa_recv, c)):
            where = pl.ds(STRIPE * (2 * pair + u), STRIPE)
            total[:, where] += ref[0, u].astype(F32).reshape(4, STRIPE, SLOT, DIM)
    out_ref[0] = merge_cols(total, wide).astype(BF16)


def whole(shape):
    zeros = (0,) * len(shape)
    return pl.BlockSpec(shape, lambda i, *unused: zeros)


def per_image(shape, first=0):
    zeros = (0,) * len(shape)
    return pl.BlockSpec((1,) + shape, lambda i, *unused: (first + i,) + zeros)


def call(body, name, batch, scalars, inputs, outputs, scratch, flops):
    in_specs = [spec for spec, unused in inputs]
    out_specs = [spec for spec, unused in outputs]
    moved = sum(value.size * value.dtype.itemsize for unused, value in inputs)
    return pl.pallas_call(
        body,
        out_shape=[shape for unused, shape in outputs],
        grid_spec=pltpu.PrefetchScalarGridSpec(
            num_scalar_prefetch=len(scalars),
            grid=(batch,),
            in_specs=in_specs,
            out_specs=out_specs,
            scratch_shapes=scratch,
        ),
        compiler_params=pltpu.CompilerParams(
            dimension_semantics=("arbitrary",), vmem_limit_bytes=VMEM_LIMIT
        ),
        cost_estimate=pl.CostEstimate(flops=flops, bytes_accessed=moved, transcendentals=0),
        name=name,
    )(*scalars, *[value for unused, value in inputs])


def struct(shape, dtype):
    return jax.ShapeDtypeStruct(shape, dtype)


def images_out(batch, shape, dtype):
    return per_image(shape), struct((batch,) + shape, dtype)


def whole_out(shape, dtype=F32):
    return whole(shape), struct(shape, dtype)


def row_exchange(parts):
    out = [parts[0]]
    size = lax.axis_size("row")
    for k in range(1, size):
        out.append(lax.ppermute(parts[k], "row", [(q, (q + k) % size) for q in range(size)]))
    return out


def col_exchange(part):
    return lax.ppermute(part, "col", [(0, 1), (1, 0)])


def bits_of(size):
    found = []
    bit = 1
    while bit < size:
        found.append(bit)
        bit *= 2
    return found


def kept_total(flags):
    total = flags
    size = lax.axis_size("batch")
    for bit in bits_of(size):
        total = total + lax.ppermute(total, "batch", [(q, q ^ bit) for q in range(size)])
    return total


def grad_total(packed):
    steps = []
    for axis in ("batch", "col", "row"):
        size = lax.axis_size(axis)
        for bit in bits_of(size):
            steps.append((axis, size, bit, (lax.axis_index(axis) // bit) % 2))
    for axis, size, bit, me in steps:
        half = packed.shape[0] // 2
        sent = lax.dynamic_slice_in_dim(packed, (1 - me) * half, half).astype(BF16)
        mine = lax.dynamic_slice_in_dim(packed, me * half, half)
        packed = mine + lax.ppermute(sent, axis, [(q, q ^ bit) for q in range(size)]).astype(F32)
    packed = packed.astype(BF16)
    for axis, size, bit, me in steps[::-1]:
        other = lax.ppermute(packed, axis, [(q, q ^ bit) for q in range(size)])
        packed = jnp.where(
            me == 0, jnp.concatenate([packed, other]), jnp.concatenate([other, packed])
        )
    return packed.astype(F32)


def pack(items, devices):
    rows = jnp.concatenate([item.reshape(-1, DIM) for item in items])
    unit = 16 * devices
    missing = (-rows.shape[0]) % unit
    return jnp.pad(rows, ((0, missing), (0, 0)))


def per_device(batch, devices, tokens, heights, widths, keep_flags, out_grad, first_gain, first_shift, triple_weight,
               query_value_bias, position_kernel, position_bias, mixing_weight, mixing_bias, second_gain, second_shift,
               expand_weight, expand_bias, reduce_weight, reduce_bias):
    count = tokens.shape[0]
    chunks = count // batch
    r, c = lax.axis_index("row"), lax.axis_index("col")
    meta = jnp.concatenate(
        [heights, widths, keep_flags[:, 0], keep_flags[:, 1], jnp.stack([r, c]).astype(jnp.int32)]
    )
    kept = kept_total(jnp.sum(keep_flags.astype(F32), axis=0))
    share = kept / (count * lax.axis_size("batch"))
    factors = (keep_flags.astype(F32) / share).reshape(-1)

    def branch_weight(lo):
        return jnp.concatenate([triple_weight[:, DIM * k + lo : DIM * k + lo + HALF] for k in range(3)], axis=1)

    wa, wd = branch_weight(0), branch_weight(HALF)
    zeros = jnp.zeros((HALF,), F32)
    ba = jnp.concatenate([query_value_bias[0, :HALF], zeros, query_value_bias[1, :HALF]])[None]
    bd = jnp.concatenate([query_value_bias[0, HALF:], zeros, query_value_bias[1, HALF:]])[None]
    gain1, shift1 = first_gain[None], first_shift[None]
    gain2, shift2 = second_gain[None], second_shift[None]
    kern = jnp.pad(position_kernel.reshape(9, DIM), ((0, 7), (0, 0)))
    pos = position_bias[None]

    def full(value):
        return whole(value.shape), value

    def chunk_in(value):
        return per_image(value.shape[1:]), value

    pix = (PIX, DIM)
    half = (PIX, HALF)
    pair = (2, PIX, DIM)
    pair_half = (2, PIX, HALF)

    prepared = []
    for k in range(chunks):
        first = k * batch
        outs = call(
            functools.partial(prep_kernel, count, first), "prep", batch, [meta],
            [(per_image((ROWS, ROWS, DIM), first), tokens)],
            [images_out(batch, pix, BF16)] * 4 + [images_out(batch, pair, BF16)] * 2,
            [pltpu.VMEM((ROWS, 32, DIM), F32), pltpu.VMEM((4, ROWS, SLOT, DIM), F32)], 1000)
        own = outs[0:4]
        prepared.append((own, row_exchange(own), outs[4], col_exchange(outs[5])))

    down = (4, PIX, HALF)
    ahead = []
    for k in range(chunks):
        first = k * batch
        own, xd, xa_keep, xa_recv = prepared[k]
        side = [
            images_out(batch, down, BF16), images_out(batch, down, BF16), images_out(batch, down, BF16),
            images_out(batch, (4, HALF, PIX), F32), images_out(batch, (4, 8, PIX), F32),
            images_out(batch, (2,) + pair_half, BF16), images_out(batch, (2,) + pair_half, BF16),
            images_out(batch, (2,) + pair_half, BF16),
            images_out(batch, (2, 2, HALF, PIX), F32), images_out(batch, (2, 2, 8, PIX), F32),
        ]

        def scratch(blocks):
            n = blocks * PIX
            return [
                pltpu.VMEM((blocks, PIX, DIM), BF16), pltpu.VMEM((n, HALF), BF16),
                pltpu.VMEM((HEADS, blocks, PIX, DIM), BF16), pltpu.VMEM((HEADS, SIZE + 16, n), BF16),
                pltpu.VMEM((blocks, PIX, HALF), F32),
            ]

        outs = call(
            functools.partial(forward_kernel, count, first), "attend_forward", batch, [meta],
            [chunk_in(v) for v in xd] + [chunk_in(xa_keep), chunk_in(xa_recv)]
            + [full(v) for v in (wd, wa, bd, ba, gain1, shift1, kern, pos)],
            [images_out(batch, half, BF16)] * 4 + [images_out(batch, pair_half, BF16)] * 2 + side,
            scratch(4) + scratch(2), 10**9 * batch)
        ahead.append((row_exchange(outs[0:4]), outs[4], col_exchange(outs[5]), outs[6:]))

    sums = [
        jnp.zeros((DIM, HIDDEN), F32),
        jnp.zeros((DIM, HIDDEN), F32),
        jnp.zeros((DIM, DIM), F32),
        jnp.zeros((8, DIM), F32),
    ]
    outputs, middles, upward = [], [], []
    for k in range(chunks):
        first = k * batch
        own = prepared[k][0]
        jd, ja_keep, ja_recv, unused = ahead[k]
        outs = call(
            functools.partial(middle_kernel, count, first), "middle", batch, [meta, factors],
            [chunk_in(v) for v in own] + [chunk_in(v) for v in jd] + [chunk_in(ja_keep), chunk_in(ja_recv)]
            + [(per_image((ROWS, ROWS, DIM), first), out_grad)]
            + [full(v) for v in (mixing_weight, mixing_bias[None], gain2, shift2, expand_weight, expand_bias[None],
                                 reduce_weight, reduce_bias[None])]
            + [full(v) for v in sums],
            [images_out(batch, (ROWS, ROWS, DIM), BF16), images_out(batch, (4,) + pix, F32)]
            + [images_out(batch, half, BF16)] * 4 + [images_out(batch, pair_half, BF16)] * 2
            + [whole_out(v.shape) for v in sums],
            [pltpu.VMEM((4,) + pix, BF16), pltpu.VMEM((4, ROWS, SLOT, DIM), F32),
             pltpu.VMEM((4, ROWS, SLOT, HALF), F32), pltpu.VMEM((4,) + pix, BF16),
             pltpu.VMEM((4, ROWS, SLOT, DIM), F32), pltpu.VMEM((4, ROWS, SLOT, DIM), F32),
             pltpu.VMEM((ROWS, 32, DIM), F32)], 5 * 10**9 * batch)
        outputs.append(outs[0])
        middles.append(outs[1])
        upward.append((row_exchange(outs[2:6]), outs[6], col_exchange(outs[7])))
        sums = outs[8:]
    reduced_pack = grad_total(pack([sums[0], sums[1], sums[2], sums[3]], devices))

    back_sums = [jnp.zeros((DIM, 3 * HALF), F32), jnp.zeros((DIM, 3 * HALF), F32), jnp.zeros((16, DIM), F32)]
    parts = []
    for k in range(chunks):
        first = k * batch
        own, xd, xa_keep, xa_recv = prepared[k]
        dd, da_keep, da_recv = upward[k]
        saved = ahead[k][3]

        def scratch(blocks):
            n = blocks * PIX
            return [
                pltpu.VMEM((blocks, PIX, DIM), BF16), pltpu.VMEM((n, HALF), BF16),
                pltpu.VMEM((HEADS, blocks, PIX, DIM), BF16), pltpu.VMEM((HALF, n), BF16),
                pltpu.VMEM((blocks, PIX, HALF), F32), pltpu.VMEM((n, HALF), F32), pltpu.VMEM((n, HALF), F32),
                pltpu.VMEM((blocks, PIX, HALF), BF16), pltpu.VMEM((blocks, PIX, DIM), BF16),
            ]

        outs = call(
            functools.partial(backward_kernel, count, first), "attend_backward", batch, [meta],
            [chunk_in(v) for v in xd] + [chunk_in(xa_keep), chunk_in(xa_recv)]
            + [chunk_in(v) for v in dd] + [chunk_in(da_keep), chunk_in(da_recv)]
            + [chunk_in(v) for v in saved]
            + [full(v) for v in (wd, wa, gain1, shift1, kern)] + [full(v) for v in back_sums],
            [images_out(batch, pix, BF16)] * 4 + [images_out(batch, pair, BF16)] * 2
            + [whole_out(v.shape) for v in back_sums],
            scratch(4) + scratch(2), 3 * 10**9 * batch)
        parts.append((row_exchange(outs[0:4]), outs[4], col_exchange(outs[5])))
        back_sums = outs[6:]
    back_pack = grad_total(pack(back_sums, devices))

    finals = []
    for k in range(chunks):
        first = k * batch
        pd, pa_keep, pa_recv = parts[k]
        finals.append(call(
            functools.partial(finish_kernel, count, first), "finish", batch, [meta],
            [chunk_in(middles[k])] + [chunk_in(v) for v in pd] + [chunk_in(pa_keep), chunk_in(pa_recv)],
            [images_out(batch, (ROWS, ROWS, DIM), BF16)],
            [pltpu.VMEM((4, ROWS, SLOT, DIM), F32), pltpu.VMEM((ROWS, 32, DIM), F32)], 1000)[0])

    reduce_weight_grad = reduced_pack[0:1024].reshape(DIM, HIDDEN).T
    expand_weight_grad = reduced_pack[1024:2048].reshape(DIM, HIDDEN)
    mixing_weight_grad = reduced_pack[2048:2304]
    rows = reduced_pack[2304:2312]
    down_grad = back_pack[0:384].reshape(DIM, 3 * HALF)
    across_grad = back_pack[384:768].reshape(DIM, 3 * HALF)
    triple_weight_grad = jnp.concatenate(
        [
            side[:, HALF * k : HALF * k + HALF]
            for k in range(3)
            for side in (across_grad, down_grad)
        ],
        axis=1,
    )
    back_rows = back_pack[768:784]
    return (
        jnp.concatenate(outputs),
        jnp.concatenate(finals),
        back_rows[0],
        back_rows[1],
        triple_weight_grad,
        back_rows[2:4],
        back_rows[5:14].reshape(3, 3, DIM),
        back_rows[4],
        mixing_weight_grad,
        rows[7],
        rows[5],
        rows[6],
        expand_weight_grad,
        rows[0:4].reshape(HIDDEN),
        reduce_weight_grad,
        rows[4],
    )


def solution(mesh):
    spread = P("batch", "row", "col", None)
    in_specs = (spread, P("batch"), P("batch"), P("batch", None), spread) + (P(),) * 14
    out_specs = (spread, spread) + (P(),) * 14
    devices = mesh.shape["batch"] * mesh.shape["row"] * mesh.shape["col"]
    return jax.shard_map(
        functools.partial(per_device, 2, devices),
        mesh=mesh, in_specs=in_specs, out_specs=out_specs, check_vma=False)
```

```python
import functools

import jax
import jax.numpy as jnp
from jax import lax
from jax.experimental import pallas as pl
from jax.experimental.pallas import tpu as pltpu
from jax.sharding import PartitionSpec as P

DIM = 256
HALF = 128
HEADS = 4
SIZE = 32
STRIPE = 7
ROWS = 28
SLOT = 8
PIX = ROWS * SLOT
HIDDEN = 1024
VEC = 3 * DIM
F32 = jnp.float32
BF16 = jnp.bfloat16
LOG2E = 1.4426950408889634
SCALE = SIZE**-0.5
EPS = 1e-05
GELU_C = 0.7978845608028654
GELU_A = 0.044715
VMEM_LIMIT = 56 * 1024 * 1024


def nn(a, b):
    return lax.dot_general(a, b, (((1,), (0,)), ((), ())), preferred_element_type=F32)


def nt(a, b):
    return lax.dot_general(a, b, (((1,), (1,)), ((), ())), preferred_element_type=F32)


def tn(a, b):
    return lax.dot_general(a, b, (((0,), (0,)), ((), ())), preferred_element_type=F32)


def col_sum(v):
    return jnp.sum(v, axis=0, keepdims=True)


def normalize(source):
    average = jnp.mean(source, axis=-1, keepdims=True)
    centered = source - average
    spread = jnp.mean(centered * centered, axis=-1, keepdims=True)
    rstd = lax.rsqrt(spread + EPS)
    return centered * rstd, rstd


def norm_back(grad_hat, hat, rstd):
    return rstd * (
        grad_hat
        - jnp.mean(grad_hat, axis=-1, keepdims=True)
        - hat * jnp.mean(grad_hat * hat, axis=-1, keepdims=True)
    )


def head_lanes(shape):
    return lax.broadcasted_iota(jnp.int32, shape, len(shape) - 1) // SIZE


def split_cols(source, wide, parts):
    wide[:, 0:ROWS, :] = source.astype(F32)
    slot = lax.broadcasted_iota(jnp.int32, (ROWS, SLOT, DIM), 1)
    for s in range(4):
        parts[s] = jnp.where(slot < STRIPE, wide[:, STRIPE * s : STRIPE * s + SLOT, :], 0.0)


def merge_cols(parts, wide):
    for s in range(4):
        wide[:, STRIPE * s : STRIPE * s + SLOT, :] = parts[s]
    return wide[:, 0:ROWS, :]


class Meta:
    def __init__(self, ref, count):
        self.ref = ref
        self.count = count

    def height(self, i):
        return self.ref[i]

    def width(self, i):
        return self.ref[self.count + i]

    def keep(self, i):
        return self.ref[2 * self.count + i]

    def feed(self, i):
        return self.ref[3 * self.count + i]

    def row(self):
        return self.ref[4 * self.count]

    def col(self):
        return self.ref[4 * self.count + 1]


def pair_start(owner):
    return 2 * (1 - owner)


def from_rows(refs, r, out):
    for k, ref in enumerate(refs):
        out[lax.rem(r + 4 - k, 4)] = ref[0]


def to_rows(refs, r, source):
    for k, ref in enumerate(refs):
        ref[0] = source[lax.rem(r + k, 4)]


def own_stripes(keep_ref, other_ref, c):
    for ref, owner in ((keep_ref, c), (other_ref, 1 - c)):
        for u in range(2):
            yield pl.ds(STRIPE * (pair_start(owner) + u), STRIPE), ref.at[0, u]


def prep_kernel(count, first, meta_ref, tok_ref, d0, d1, d2, d3, keep_ref, send_ref, wide, parts):
    meta = Meta(meta_ref, count)
    split_cols(tok_ref[0], wide, parts)
    r, c = meta.row(), meta.col()
    for k, ref in enumerate((d0, d1, d2, d3)):
        ref[0] = parts[lax.rem(r + k, 4)].reshape(PIX, DIM).astype(BF16)
    for where, ref in own_stripes(keep_ref, send_ref, c):
        ref[...] = parts[:, where].reshape(PIX, DIM).astype(BF16)


def down_mask(height, width, stripe):
    shape = (4 * ROWS, SLOT, HALF)
    row = lax.broadcasted_iota(jnp.int32, shape, 0)
    j = lax.broadcasted_iota(jnp.int32, shape, 1)
    limit = jnp.minimum(STRIPE, width - STRIPE * stripe)
    return jnp.where((row < height) & (j < limit), 1.0, 0.0)


def across_mask(height, width, stripe):
    shape = (2, 8, STRIPE, SLOT, HALF)
    u = lax.broadcasted_iota(jnp.int32, shape, 0)
    b = lax.broadcasted_iota(jnp.int32, shape, 1)
    row = lax.broadcasted_iota(jnp.int32, shape, 2)
    j = lax.broadcasted_iota(jnp.int32, shape, 3)
    good = (STRIPE * u + row < height - STRIPE * stripe) & (j < STRIPE) & (b * STRIPE + j < width)
    return jnp.where(good, 1.0, 0.0)


def moved_rows(v, axis, step):
    if step == 0:
        return v
    size = v.shape[axis]
    zero_shape = v.shape[:axis] + (1,) + v.shape[axis + 1 :]
    zero = jnp.zeros(zero_shape, v.dtype)
    if step > 0:
        return jnp.concatenate([lax.slice_in_dim(v, 1, size, axis=axis), zero], axis=axis)
    return jnp.concatenate([zero, lax.slice_in_dim(v, 0, size - 1, axis=axis)], axis=axis)


def roll8(v, shift):
    shape = v.shape
    flat = v.reshape(-1, SLOT, HALF)
    return pltpu.roll(flat, shift, 1).reshape(shape)


def moved_cols_down(v, step):
    if step == 0:
        return v
    return roll8(v, 1 if step < 0 else SLOT - 1)


def moved_cols_across(v, step):
    if step == 0:
        return v
    slot = lax.broadcasted_iota(jnp.int32, v.shape, 3)
    if step < 0:
        return jnp.where(slot == 0, moved_rows(roll8(v, 2), 1, -1), roll8(v, 1))
    return jnp.where(slot == STRIPE - 1, moved_rows(roll8(v, SLOT - 2), 1, 1), roll8(v, SLOT - 1))


def taps(v, across):
    moved_cols = moved_cols_across if across else moved_cols_down
    row_axis = 2 if across else 0
    for b in range(3):
        side = moved_cols(v, b - 1)
        for a in range(3):
            yield a, b, moved_rows(side, row_axis, a - 1)


def position_term(v, kern_ref, bias_ref, lanes, across):
    total = bias_ref[0:1, lanes]
    for a, b, moved in taps(v, across):
        total = total + moved * kern_ref[3 * a + b : 3 * a + b + 1, lanes]
    return total


def position_back(grad, v, kern_ref, lanes, across):
    total = 0.0
    for a, b, moved in taps(grad, across):
        k = 3 * (2 - a) + (2 - b)
        total = total + moved * kern_ref[k : k + 1, lanes]
    kernel_grads = []
    flat = grad.reshape(-1, HALF)
    found = {}
    for a, b, moved in taps(v, across):
        found[3 * a + b] = col_sum(flat * moved.reshape(-1, HALF))
    for k in range(9):
        kernel_grads.append(found[k])
    return total, kernel_grads, col_sum(flat)


DOWN_GRID = (4 * ROWS, SLOT, HALF)
ACROSS_GRID = (2, 8, STRIPE, SLOT, HALF)
DOWN_SIZES = (640, 768, 896)
ACROSS_SIZES = (336, 448)
DOWN_GROUP = 2
DOWN_BACK_GROUP = 1
PIXELS = 4 * PIX


def by_size(used, sizes, body):
    below = None
    for n in sizes:
        fits = used <= n
        if n == sizes[-1]:
            fits = True if below is None else used > below
        elif below is not None:
            fits = fits & (used > below)
        pl.when(fits)(functools.partial(body, n))
        below = n


def project(x_ref, weight_ref, bias_ref, gain_ref, shift_ref):
    hat, unused = normalize(x_ref[...].reshape(PIXELS, DIM).astype(F32))
    normed = (hat * gain_ref[...] + shift_ref[...]).astype(BF16)
    return (nn(normed, weight_ref[...]) + bias_ref[...]).astype(BF16)


def split_queries(query):
    scaled = query.astype(F32) * (SCALE * LOG2E)
    high = scaled.astype(BF16)
    low = (scaled - high.astype(F32)).astype(BF16)
    return jnp.concatenate([high, low], axis=1)


def valid_keys(keys, mask, stripes):
    size = PIXELS // stripes
    keys = keys.astype(F32)
    fixed = [
        jnp.where(
            mask[size * u : size * u + size] > 0.0, keys[size * u : size * u + size], keys[size * u : size * u + 1]
        )
        for u in range(stripes)
    ]
    return jnp.concatenate(fixed, axis=0).astype(BF16)


def only_head(value, h):
    lane = lax.broadcasted_iota(jnp.int32, value.shape, 1)
    return jnp.where(lax.rem(lane, HALF) // SIZE == h, value, jnp.zeros_like(value))


def attend(key_ref, query_ref, turned_ref, base, at_out, lse_out, a_ref, full, group, n):
    part = pl.ds(base, n)
    whole_part = pl.ds(base, full)

    def heads_of(t, carry):
        heads = [t * group + j for j in range(group)]
        keys = key_ref[part]
        keys = jnp.concatenate([keys, keys], axis=1)
        queries = query_ref[part]
        scores = [nt(keys, only_head(queries, h)) for h in heads]
        tops = [jnp.max(s, axis=0, keepdims=True) for s in scores]
        weights = [jnp.exp2(s - top).astype(BF16) for s, top in zip(scores, tops)]
        outs = [nn(turned_ref[h, :, 0:n], w) for h, w in zip(heads, weights)]
        for h, out, top in zip(heads, outs, tops):
            total = out[SIZE : SIZE + 1]
            at_out[pl.ds(pl.multiple_of(h * SIZE, SIZE), SIZE), 0:n] = out[0:SIZE] / total
            lse_out[pl.ds(h, 1), 0:n] = top + jnp.log2(total)
        return carry

    if group == HEADS:
        heads_of(0, 0)
    else:
        lax.fori_loop(0, HEADS // group, heads_of, 0)
    if n < full:
        a_ref[whole_part] = jnp.zeros((full, HALF), F32)
    a_ref[part] = at_out[:, 0:n].T


def prepare_forward(x_ref, mask, stripes, weight_ref, bias_ref, gain_ref, shift_ref, saved, key_ref, query_ref, turned_ref):
    q_out, k_out, v_out = saved
    triple = project(x_ref, weight_ref, bias_ref, gain_ref, shift_ref)
    q_out[...] = triple[:, 0:HALF]
    k_out[...] = triple[:, HALF : 2 * HALF]
    v_out[...] = triple[:, 2 * HALF :]
    query_ref[...] = split_queries(triple[:, 0:HALF])
    key_ref[...] = valid_keys(triple[:, HALF : 2 * HALF], mask, stripes)
    masked = triple[:, 2 * HALF :].astype(F32) * mask
    turned = masked.T
    flags = mask.T[0:16]
    size = PIXELS // stripes
    for u in range(stripes):
        part = slice(size * u, size * u + size)
        for h in range(HEADS):
            rows = jnp.concatenate([turned[SIZE * h : SIZE * h + SIZE, part], flags[:, part]], axis=0)
            turned_ref[u, h] = rows.astype(BF16)
    return masked


def down_used(height):
    return SLOT * height


def live_stripes(height, stripe):
    return jnp.where(STRIPE * (stripe + 1) < height, 2, 1)


def across_used(width):
    return STRIPE * SLOT * ((width + STRIPE - 1) // STRIPE)


def forward_down_kernel(count, first, meta_ref, xd0, xd1, xd2, xd3, weight_ref, bias_ref, gain_ref, shift_ref,
                        kern_ref, pos_ref, jd0, jd1, jd2, jd3, q_out, k_out, v_out, at_out, lse_out,
                        x_ref, key_ref, query_ref, turned_ref, a_ref, j_ref):
    meta = Meta(meta_ref, count)
    i = first + pl.program_id(0)
    r, c = meta.row(), meta.col()
    height, width = meta.height(i), meta.width(i)
    stripe = 4 * c + r
    live = (meta.keep(i) > 0) & (STRIPE * stripe < width)

    @pl.when(live)
    def _():
        from_rows((xd0, xd1, xd2, xd3), r, x_ref)
        mask = down_mask(height, width, stripe)
        masked = prepare_forward(
            x_ref, mask.reshape(PIXELS, HALF), 1, weight_ref, bias_ref, gain_ref, shift_ref,
            (q_out.at[0], k_out.at[0], v_out.at[0]), key_ref, query_ref, turned_ref)

        def size(n):
            attend(key_ref, query_ref, turned_ref.at[0], 0, at_out.at[0], lse_out.at[0], a_ref, PIXELS, DOWN_GROUP, n)

        by_size(down_used(height), DOWN_SIZES, size)
        term = position_term(masked.reshape(DOWN_GRID), kern_ref, pos_ref, slice(HALF, DIM), False)
        total = a_ref[...] + term.reshape(PIXELS, HALF)
        j_ref[...] = total.astype(BF16).reshape(4, PIX, HALF)
        to_rows((jd0, jd1, jd2, jd3), r, j_ref)

    @pl.when(jnp.logical_not(live))
    def _():
        for ref in (jd0, jd1, jd2, jd3):
            ref[...] = jnp.zeros_like(ref)


def forward_across_kernel(count, first, meta_ref, xa_keep, xa_recv, weight_ref, bias_ref, gain_ref, shift_ref,
                          kern_ref, pos_ref, ja_keep, ja_send, q_out, k_out, v_out, at_out, lse_out,
                          x_ref, key_ref, query_ref, turned_ref, a_ref, j_ref):
    meta = Meta(meta_ref, count)
    i = first + pl.program_id(0)
    r, c = meta.row(), meta.col()
    height, width = meta.height(i), meta.width(i)
    stripe = 4 * r + pair_start(c)
    live = (meta.keep(i) > 0) & (STRIPE * stripe < height)

    @pl.when(live)
    def _():
        mask = across_mask(height, width, stripe)
        for u in range(2):
            x_ref[2 * u + c] = xa_keep[0, u]
            x_ref[2 * u + 1 - c] = xa_recv[0, u]
        masked = prepare_forward(
            x_ref, mask.reshape(PIXELS, HALF), 2, weight_ref, bias_ref, gain_ref, shift_ref,
            (q_out.at[0], k_out.at[0], v_out.at[0]), key_ref, query_ref, turned_ref)
        half = PIXELS // 2
        a_ref[half:] = jnp.zeros((half, HALF), F32)

        def stripe_of(u, carry):
            def size(n):
                base = pl.multiple_of(u * half, half)
                attend(key_ref, query_ref, turned_ref.at[u], base, at_out.at[0, u], lse_out.at[0, u], a_ref, half, HEADS, n)

            by_size(across_used(width), ACROSS_SIZES, size)
            return carry

        lax.fori_loop(0, live_stripes(height, stripe), stripe_of, 0)
        term = position_term(masked.reshape(ACROSS_GRID), kern_ref, pos_ref, slice(0, HALF), True)
        j_ref[...] = (a_ref[...] + term.reshape(PIXELS, HALF)).astype(BF16).reshape(4, PIX, HALF)
        for u in range(2):
            ja_keep[0, u] = j_ref[2 * u + c]
            ja_send[0, u] = j_ref[2 * u + 1 - c]

    @pl.when(jnp.logical_not(live))
    def _():
        ja_keep[...] = jnp.zeros_like(ja_keep)
        ja_send[...] = jnp.zeros_like(ja_send)


def pixel_mask(height, width, first_block, blocks, r, c):
    shape = (blocks, ROWS, SLOT, HALF)
    s = lax.broadcasted_iota(jnp.int32, shape, 0) + first_block
    row = lax.broadcasted_iota(jnp.int32, shape, 1)
    j = lax.broadcasted_iota(jnp.int32, shape, 2)
    good = (row < height - ROWS * r) & (j < STRIPE) & (s * STRIPE + j < width - ROWS * c)
    mask = jnp.where(good, 1.0, 0.0).reshape(blocks * PIX, HALF)
    return jnp.concatenate([mask, mask], axis=1)


def middle_kernel(count, first, meta_ref, fact_ref, xd0, xd1, xd2, xd3, jd0, jd1, jd2, jd3, ja_keep, ja_recv, grad_ref,
                  wm_ref, bm_ref, gain_ref, shift_ref, we_ref, be_ref, wr_ref, br_ref, start, start_v,
                  out_ref, dm_ref, dd0, dd1, dd2, dd3, da_keep, da_send, acc, acc_v,
                  x_ref, g_ref, ja_ref, j_ref, o_ref, dj_ref, wide):
    meta = Meta(meta_ref, count)
    step = pl.program_id(0)
    i = first + step
    r, c = meta.row(), meta.col()
    height, width = meta.height(i), meta.width(i)
    attend_factor = fact_ref[2 * i]
    feed_factor = fact_ref[2 * i + 1]

    @pl.when(step == 0)
    def _():
        acc[...] = start[...]
        acc_v[...] = start_v[...]

    split_cols(grad_ref[0], wide, g_ref)
    for k, (xs, js) in enumerate(((xd0, jd0), (xd1, jd1), (xd2, jd2), (xd3, jd3))):
        x_ref[lax.rem(r + k, 4)] = xs[0]
        j_ref[lax.rem(r + 4 - k, 4), :, HALF:] = js[0]
    for where, ref in own_stripes(ja_keep, ja_recv, c):
        ja_ref[:, where] = ref[...].astype(F32).reshape(4, STRIPE, SLOT, HALF)
    j_ref[:, :, 0:HALF] = ja_ref[...].reshape(4, PIX, HALF).astype(BF16)

    group = 2
    size = group * PIX

    def one(b, carry):
        where = pl.ds(group * b, group)
        mask = pixel_mask(height, width, group * b, group, r, c)
        scale_attend = mask * attend_factor
        scale_feed = mask * feed_factor
        x = x_ref[where].reshape(size, DIM).astype(F32)
        joined = j_ref[where].reshape(size, DIM)
        g = g_ref[where].reshape(size, DIM)
        mixed = nn(joined, wm_ref[...]) + bm_ref[...]
        middle = x + scale_attend * mixed
        hat, rstd = normalize(middle)
        normed = (hat * gain_ref[...] + shift_ref[...]).astype(BF16)
        d_reduced = (scale_feed * g).astype(BF16)
        pre = nn(normed, we_ref[...]) + be_ref[...]
        square = pre * pre
        bend = jnp.tanh(pre * (GELU_C + (GELU_C * GELU_A) * square))
        half_one = 0.5 + 0.5 * bend
        act = (pre * half_one).astype(BF16)
        slope = half_one + (0.5 * pre) * (1.0 - bend * bend) * (GELU_C + (3.0 * GELU_C * GELU_A) * square)
        reduced = nn(act, wr_ref[...]) + br_ref[...]
        o_ref[where] = (middle + scale_feed * reduced).reshape(group, ROWS, SLOT, DIM)
        acc[:, 0:HIDDEN] += tn(d_reduced, act)
        d_act = nt(d_reduced, wr_ref[...])
        d_hidden = d_act * slope
        d_hidden_low = d_hidden.astype(BF16)
        acc[:, HIDDEN : 2 * HIDDEN] += tn(normed, d_hidden_low)
        d_hidden_sum = col_sum(d_hidden_low.astype(F32))
        d_normed = nt(d_hidden_low, we_ref[...])
        d_middle = g + norm_back(d_normed * gain_ref[...], hat, rstd)
        dm_ref[0, where] = d_middle.reshape(group, PIX, DIM)
        d_mixed = (scale_attend * d_middle).astype(BF16)
        acc[:, 2 * HIDDEN :] += tn(joined, d_mixed)
        dj_ref[where] = nt(d_mixed, wm_ref[...]).reshape(group, ROWS, SLOT, DIM)
        rows = [d_hidden_sum[:, DIM * k : DIM * k + DIM] for k in range(4)]
        rows.append(col_sum(d_reduced.astype(F32)))
        rows.append(col_sum(d_normed * hat))
        rows.append(col_sum(d_normed))
        rows.append(col_sum(d_mixed.astype(F32)))
        acc_v[...] += jnp.concatenate(rows, axis=0)
        return carry

    lax.fori_loop(0, 4 // group, one, 0)
    out_ref[0] = merge_cols(o_ref, wide).astype(BF16)
    for k, ref in enumerate((dd0, dd1, dd2, dd3)):
        ref[0] = dj_ref[lax.rem(r + k, 4), :, :, HALF:].reshape(PIX, HALF).astype(BF16)
    for where, ref in own_stripes(da_keep, da_send, c):
        ref[...] = dj_ref[:, where, :, 0:HALF].reshape(PIX, HALF).astype(BF16)


def attend_back(key_ref, query_ref, q_ref, v_ref, turned_ref, up_ref, at_ref, lse_ref, base,
                delta_ref, dqt_ref, dq_ref, dk_ref, dv_ref, full, group, n):
    part = pl.ds(base, n)
    whole_part = pl.ds(base, full)
    product = up_ref[part].astype(F32).T * at_ref[:, 0:n]
    for h in range(HEADS):
        delta_ref[h : h + 1, 0:n] = col_sum(product[SIZE * h : SIZE * h + SIZE])
    dk_ref[whole_part] = jnp.zeros((full, HALF), F32)

    def heads_of(t, carry):
        heads = [t * group + j for j in range(group)]
        keys = key_ref[part]
        keys = jnp.concatenate([keys, keys], axis=1)
        scaled, queries, values, up = query_ref[part], q_ref[part], v_ref[part], up_ref[part]
        ups = [only_head(up, h) for h in heads]
        scores = [nt(keys, only_head(scaled, h)) for h in heads]
        grads = [nt(values, u) for u in ups]
        softs = [jnp.exp2(s - lse_ref[pl.ds(h, 1), 0:n]) for h, s in zip(heads, scores)]
        backs = [(p * (g - delta_ref[pl.ds(h, 1), 0:n])).astype(BF16) for h, p, g in zip(heads, softs, grads)]
        lows = [p.astype(BF16) for p in softs]
        dv, dk = dv_ref[part], dk_ref[part]
        for p, u in zip(lows, ups):
            dv = dv + nn(p, u)
        for h, z in zip(heads, backs):
            dk = dk + nn(z, only_head(queries, h))
        dv_ref[part] = dv
        dk_ref[part] = dk
        for h, z in zip(heads, backs):
            rows = pl.ds(pl.multiple_of(h * SIZE, SIZE), SIZE)
            dqt_ref[rows, 0:n] = nn(turned_ref[rows, 0:n], z)
        return carry

    if group == HEADS:
        heads_of(0, 0)
    else:
        lax.fori_loop(0, HEADS // group, heads_of, 0)
    if n < full:
        dq_ref[whole_part] = jnp.zeros((full, HALF), F32)
    dq_ref[part] = dqt_ref[:, 0:n].T * SCALE


def prepare_back(mask, stripes, across, lanes, kern_ref, saved, up_ref, acc, key_ref, query_ref, turned_ref, dv_ref):
    q_ref, k_ref, v_ref = saved
    grid = ACROSS_GRID if across else DOWN_GRID
    key_ref[...] = valid_keys(k_ref[...], mask, stripes)
    query_ref[...] = split_queries(q_ref[...])
    turned = (k_ref[...].astype(F32) * mask).T.astype(BF16)
    size = PIXELS // stripes
    for u in range(stripes):
        turned_ref[u] = turned[:, size * u : size * u + size]
    masked = v_ref[...].astype(F32) * mask
    grad = up_ref[...].astype(F32)
    back, kernel_rows, bias_row = position_back(grad.reshape(grid), masked.reshape(grid), kern_ref, lanes, across)
    dv_ref[...] = back.reshape(PIXELS, HALF)
    acc[VEC + 4 : VEC + 14, lanes] += jnp.concatenate([bias_row] + kernel_rows, axis=0)


def finish_back(x_ref, mask, lanes, weight_ref, gain_ref, shift_ref, acc, dq_ref, dk_ref, dv_ref):
    triple = jnp.concatenate([dq_ref[...], dk_ref[...] * (mask * SCALE), dv_ref[...] * mask], axis=1).astype(BF16)
    hat, rstd = normalize(x_ref[...].reshape(PIXELS, DIM).astype(F32))
    normed = (hat * gain_ref[...] + shift_ref[...]).astype(BF16)
    grads = tn(normed, triple)
    for k in range(3):
        acc[DIM * k : DIM * k + DIM, lanes] += grads[:, HALF * k : HALF * k + HALF]
    d_normed = nt(triple, weight_ref[...])
    sums = col_sum(triple.astype(F32))
    acc[VEC : VEC + 1] += col_sum(d_normed * hat)
    acc[VEC + 1 : VEC + 2] += col_sum(d_normed)
    acc[VEC + 2 : VEC + 3, lanes] += sums[:, 0:HALF]
    acc[VEC + 3 : VEC + 4, lanes] += sums[:, 2 * HALF :]
    return norm_back(d_normed * gain_ref[...], hat, rstd).astype(BF16).reshape(4, PIX, DIM)


def backward_down_kernel(count, first, meta_ref, xd0, xd1, xd2, xd3, dd0, dd1, dd2, dd3,
                         q_in, k_in, v_in, at_in, lse_in, weight_ref, gain_ref, shift_ref, kern_ref,
                         start, pd0, pd1, pd2, pd3, acc,
                         x_ref, up_ref, key_ref, query_ref, turned_ref, dq_ref, dk_ref, dv_ref, part_ref,
                         delta_ref, dqt_ref):
    meta = Meta(meta_ref, count)
    step = pl.program_id(0)
    i = first + step
    r, c = meta.row(), meta.col()
    height, width = meta.height(i), meta.width(i)

    @pl.when(step == 0)
    def _():
        acc[...] = start[...]

    stripe = 4 * c + r
    live = (meta.keep(i) > 0) & (STRIPE * stripe < width)

    @pl.when(live)
    def _():
        mask = down_mask(height, width, stripe).reshape(PIXELS, HALF)
        lanes = slice(HALF, DIM)
        from_rows((xd0, xd1, xd2, xd3), r, x_ref)
        for k, ref in enumerate((dd0, dd1, dd2, dd3)):
            up_ref[pl.ds(pl.multiple_of(lax.rem(r + 4 - k, 4) * PIX, PIX), PIX)] = ref[0]
        prepare_back(mask, 1, False, lanes, kern_ref, (q_in.at[0], k_in.at[0], v_in.at[0]), up_ref, acc,
                     key_ref, query_ref, turned_ref, dv_ref)

        def size(n):
            attend_back(key_ref, query_ref, q_in.at[0], v_in.at[0], turned_ref.at[0], up_ref, at_in.at[0], lse_in.at[0],
                        0, delta_ref, dqt_ref, dq_ref, dk_ref, dv_ref, PIXELS, DOWN_BACK_GROUP, n)

        by_size(down_used(height), DOWN_SIZES, size)
        part_ref[...] = finish_back(x_ref, mask, lanes, weight_ref, gain_ref, shift_ref, acc, dq_ref, dk_ref, dv_ref)
        to_rows((pd0, pd1, pd2, pd3), r, part_ref)

    @pl.when(jnp.logical_not(live))
    def _():
        for ref in (pd0, pd1, pd2, pd3):
            ref[...] = jnp.zeros_like(ref)


def backward_across_kernel(count, first, meta_ref, xa_keep, xa_recv, da_keep, da_recv,
                           q_in, k_in, v_in, at_in, lse_in, weight_ref, gain_ref, shift_ref, kern_ref,
                           start, pa_keep, pa_send, acc,
                           x_ref, up_ref, key_ref, query_ref, turned_ref, dq_ref, dk_ref, dv_ref, part_ref,
                           delta_ref, dqt_ref):
    meta = Meta(meta_ref, count)
    step = pl.program_id(0)
    i = first + step
    r, c = meta.row(), meta.col()
    height, width = meta.height(i), meta.width(i)

    @pl.when(step == 0)
    def _():
        acc[...] = start[...]

    stripe = 4 * r + pair_start(c)
    live = (meta.keep(i) > 0) & (STRIPE * stripe < height)

    @pl.when(live)
    def _():
        mask = across_mask(height, width, stripe).reshape(PIXELS, HALF)
        lanes = slice(0, HALF)
        for u in range(2):
            for xs, ds, side in ((xa_keep, da_keep, c), (xa_recv, da_recv, 1 - c)):
                x_ref[2 * u + side] = xs[0, u]
                up_ref[pl.ds(pl.multiple_of((2 * u + side) * PIX, PIX), PIX)] = ds[0, u]
        prepare_back(mask, 2, True, lanes, kern_ref, (q_in.at[0], k_in.at[0], v_in.at[0]), up_ref, acc,
                     key_ref, query_ref, turned_ref, dv_ref)
        half = PIXELS // 2
        dk_ref[half:] = jnp.zeros((half, HALF), F32)
        dq_ref[half:] = jnp.zeros((half, HALF), F32)

        def stripe_of(u, carry):
            def size(n):
                base = pl.multiple_of(u * half, half)
                attend_back(key_ref, query_ref, q_in.at[0], v_in.at[0], turned_ref.at[u], up_ref,
                            at_in.at[0, u], lse_in.at[0, u], base, delta_ref, dqt_ref, dq_ref, dk_ref, dv_ref,
                            half, HEADS, n)

            by_size(across_used(width), ACROSS_SIZES, size)
            return carry

        lax.fori_loop(0, live_stripes(height, stripe), stripe_of, 0)
        part_ref[...] = finish_back(x_ref, mask, lanes, weight_ref, gain_ref, shift_ref, acc, dq_ref, dk_ref, dv_ref)
        for u in range(2):
            pa_keep[0, u] = part_ref[2 * u + c]
            pa_send[0, u] = part_ref[2 * u + 1 - c]

    @pl.when(jnp.logical_not(live))
    def _():
        pa_keep[...] = jnp.zeros_like(pa_keep)
        pa_send[...] = jnp.zeros_like(pa_send)


def finish_kernel(count, first, meta_ref, dm_ref, pd0, pd1, pd2, pd3, pa_keep, pa_recv, out_ref, total, wide):
    meta = Meta(meta_ref, count)
    r, c = meta.row(), meta.col()
    total[...] = dm_ref[0].reshape(4, ROWS, SLOT, DIM)
    for k, ref in enumerate((pd0, pd1, pd2, pd3)):
        total[lax.rem(r + 4 - k, 4)] += ref[0].astype(F32).reshape(ROWS, SLOT, DIM)
    for where, ref in own_stripes(pa_keep, pa_recv, c):
        total[:, where] += ref[...].astype(F32).reshape(4, STRIPE, SLOT, DIM)
    out_ref[0] = merge_cols(total, wide).astype(BF16)


def whole(shape):
    zeros = (0,) * len(shape)
    return pl.BlockSpec(shape, lambda i, *unused: zeros)


def per_image(shape, first=0):
    zeros = (0,) * len(shape)
    return pl.BlockSpec((1,) + shape, lambda i, *unused: (first + i,) + zeros)


def call(body, name, batch, scalars, inputs, outputs, scratch, micros, held=None):
    in_specs = [spec for spec, unused in inputs]
    out_specs = [spec for spec, unused in outputs]
    moved = sum(value.size * value.dtype.itemsize for unused, value in inputs)
    aliases = {}
    if held is not None:
        inner, skipped = body, len(scalars) + len(inputs)

        def body(*refs):
            inner(*refs[:skipped], *refs[skipped + 1 :])

        in_specs = in_specs + [pl.BlockSpec(memory_space=pl.ANY)]
        inputs = inputs + [(None, held)]
        aliases = {skipped: 0}
    return list(pl.pallas_call(
        body,
        out_shape=[shape for unused, shape in outputs],
        grid_spec=pltpu.PrefetchScalarGridSpec(
            num_scalar_prefetch=len(scalars),
            grid=(batch,),
            in_specs=in_specs,
            out_specs=out_specs,
            scratch_shapes=scratch,
        ),
        compiler_params=pltpu.CompilerParams(
            dimension_semantics=("arbitrary",), vmem_limit_bytes=VMEM_LIMIT
        ),
        input_output_aliases=aliases,
        cost_estimate=pl.CostEstimate(flops=micros * 10**9, bytes_accessed=moved, transcendentals=0),
        name=name,
    )(*scalars, *[value for unused, value in inputs]))


def struct(shape, dtype):
    return jax.ShapeDtypeStruct(shape, dtype)


def images_out(batch, shape, dtype):
    return per_image(shape), struct((batch,) + shape, dtype)


def whole_out(shape, dtype=F32):
    return whole(shape), struct(shape, dtype)


def row_exchange(parts):
    size = lax.axis_size("row")
    return [parts[0]] + [
        lax.ppermute(parts[k], "row", [(q, (q + k) % size) for q in range(size)]) for k in range(1, size)
    ]


def col_exchange(keep, send):
    return [keep, lax.ppermute(send, "col", [(0, 1), (1, 0)])]


def bits_of(size):
    found = []
    bit = 1
    while bit < size:
        found.append(bit)
        bit *= 2
    return found


def kept_total(flags):
    total = flags
    size = lax.axis_size("batch")
    for bit in bits_of(size):
        total = total + lax.ppermute(total, "batch", [(q, q ^ bit) for q in range(size)])
    return total


def send_shares(rows, devices):
    sent = rows.astype(BF16).reshape((devices, -1) + rows.shape[1:])
    return lax.all_to_all(sent, ("batch", "row", "col"), 0, 0)


def sum_shares(received):
    return jnp.sum(received.astype(F32), axis=0).astype(BF16)


def gather_shares(share, devices):
    sent = jnp.broadcast_to(share[None], (devices,) + share.shape)
    return lax.all_to_all(sent, ("batch", "row", "col"), 0, 0).reshape((-1,) + share.shape[1:])


def per_device(batch, devices, tokens, heights, widths, keep_flags, out_grad, first_gain, first_shift, triple_weight,
               query_value_bias, position_kernel, position_bias, mixing_weight, mixing_bias, second_gain, second_shift,
               expand_weight, expand_bias, reduce_weight, reduce_bias):
    count = tokens.shape[0]
    chunks = count // batch
    r, c = lax.axis_index("row"), lax.axis_index("col")
    meta = jnp.concatenate(
        [heights, widths, keep_flags[:, 0], keep_flags[:, 1], jnp.stack([r, c]).astype(jnp.int32)]
    )
    kept = kept_total(jnp.sum(keep_flags.astype(F32), axis=0))
    share = kept / (count * lax.axis_size("batch"))
    factors = (keep_flags.astype(F32) / share).reshape(-1)

    def branch_weight(lo):
        return jnp.concatenate([triple_weight[:, DIM * k + lo : DIM * k + lo + HALF] for k in range(3)], axis=1)

    wa, wd = branch_weight(0), branch_weight(HALF)
    zeros = jnp.zeros((HALF,), F32)
    ba = jnp.concatenate([query_value_bias[0, :HALF], zeros, query_value_bias[1, :HALF]])[None]
    bd = jnp.concatenate([query_value_bias[0, HALF:], zeros, query_value_bias[1, HALF:]])[None]
    gain1, shift1 = first_gain[None], first_shift[None]
    gain2, shift2 = second_gain[None], second_shift[None]
    kern = jnp.pad(position_kernel.reshape(9, DIM), ((0, 7), (0, 0)))
    pos = position_bias[None]

    def full(value):
        return whole(value.shape), value

    def chunk_in(value):
        return per_image(value.shape[1:]), value

    def grid_out(first):
        return per_image((ROWS, ROWS, DIM), first), struct((count, ROWS, ROWS, DIM), BF16)

    pix = (PIX, DIM)
    half = (PIX, HALF)
    pair = (2, PIX, DIM)
    pair_half = (2, PIX, HALF)

    own, across_tokens, down_tokens = [], [], []
    order = meta
    for k in range(chunks):
        first = k * batch
        outs = call(
            functools.partial(prep_kernel, count, first), "prep", batch, [order],
            [(per_image((ROWS, ROWS, DIM), first), tokens)],
            [images_out(batch, pix, BF16)] * 4 + [images_out(batch, pair, BF16)] * 2,
            [pltpu.VMEM((ROWS, 32, DIM), F32), pltpu.VMEM((4, ROWS, SLOT, DIM), F32)], 2 * batch)
        own.append(outs[0:4])
        across_tokens.append(col_exchange(outs[4], outs[5]))
        order, outs[3] = lax.optimization_barrier((order, outs[3]))

    flat = images_out(batch, (PIXELS, HALF), BF16)
    side_down = [flat, flat, flat, images_out(batch, (HALF, PIXELS), F32), images_out(batch, (8, PIXELS), F32)]
    side_across = [flat, flat, flat, images_out(batch, (2, HALF, PIXELS // 2), F32), images_out(batch, (2, 8, PIXELS // 2), F32)]
    blocks = pltpu.VMEM((4, PIX, DIM), BF16)
    low = pltpu.VMEM((PIXELS, HALF), BF16)
    high = pltpu.VMEM((PIXELS, HALF), F32)
    pairs = pltpu.VMEM((PIXELS, DIM), BF16)
    low_blocks = pltpu.VMEM((4, PIX, HALF), BF16)

    ahead_across, ahead_down = [], []
    for k in range(chunks):
        first = k * batch
        if k == 0:
            down_tokens.append(row_exchange(own[0]))
        outs = call(
            functools.partial(forward_across_kernel, count, first), "across_forward", batch, [meta],
            [chunk_in(v) for v in across_tokens[k]] + [full(v) for v in (wa, ba, gain1, shift1, kern, pos)],
            [images_out(batch, pair_half, BF16)] * 2 + side_across,
            [blocks, low, pairs, pltpu.VMEM((2, HEADS, SIZE + 16, PIXELS // 2), BF16), high, low_blocks],
            5 * batch)
        if k + 1 < chunks:
            outs[0], own[k + 1] = lax.optimization_barrier((outs[0], own[k + 1]))
            down_tokens.append(row_exchange(own[k + 1]))
        ahead_across.append((col_exchange(outs[0], outs[1]), outs[2:]))
    for k in range(chunks):
        first = k * batch
        outs = call(
            functools.partial(forward_down_kernel, count, first), "down_forward", batch, [meta],
            [chunk_in(v) for v in down_tokens[k]] + [full(v) for v in (wd, bd, gain1, shift1, kern, pos)],
            [images_out(batch, half, BF16)] * 4 + side_down,
            [blocks, low, pairs, pltpu.VMEM((1, HEADS, SIZE + 16, PIXELS), BF16), high, low_blocks],
            6 * batch)
        ahead_down.append((row_exchange(outs[0:4]), outs[4:]))

    sums = [jnp.zeros((DIM, 2 * HIDDEN + DIM), F32), jnp.zeros((8, DIM), F32)]
    output, middles, upward_down, upward_across = None, [], [], []
    for k in range(chunks):
        first = k * batch
        outs = call(
            functools.partial(middle_kernel, count, first), "middle", batch, [meta, factors],
            [chunk_in(v) for v in own[k] + ahead_down[k][0] + ahead_across[k][0]] + [(per_image((ROWS, ROWS, DIM), first), out_grad)]
            + [full(v) for v in (mixing_weight, mixing_bias[None], gain2, shift2, expand_weight, expand_bias[None],
                                 reduce_weight, reduce_bias[None])]
            + [full(v) for v in sums],
            [grid_out(first), images_out(batch, (4,) + pix, F32)] + [images_out(batch, half, BF16)] * 4
            + [images_out(batch, pair_half, BF16)] * 2 + [whole_out(v.shape) for v in sums],
            [pltpu.VMEM((4,) + pix, BF16), pltpu.VMEM((4, ROWS, SLOT, DIM), F32),
             pltpu.VMEM((4, ROWS, SLOT, HALF), F32), pltpu.VMEM((4,) + pix, BF16),
             pltpu.VMEM((4, ROWS, SLOT, DIM), F32), pltpu.VMEM((4, ROWS, SLOT, DIM), F32),
             pltpu.VMEM((ROWS, 32, DIM), F32)], 9 * batch, output)
        output = outs[0]
        middles.append(outs[1])
        upward_down.append(row_exchange(outs[2:6]))
        upward_across.append(col_exchange(outs[6], outs[7]))
        sums = outs[8:]
    received = send_shares(sums[0], devices)

    back_sums = jnp.zeros((VEC + 16, DIM), F32)
    back_scratch = [high, high, high, blocks, pltpu.VMEM((8, PIXELS), F32), pltpu.VMEM((HALF, PIXELS), F32)]
    parts_down, parts_across = [], []
    for k in range(chunks):
        first = k * batch
        outs = call(
            functools.partial(backward_down_kernel, count, first), "down_backward", batch, [meta],
            [chunk_in(v) for v in down_tokens[k] + upward_down[k] + ahead_down[k][1]]
            + [full(v) for v in (wd, gain1, shift1, kern, back_sums)],
            [images_out(batch, pix, BF16)] * 4 + [whole_out(back_sums.shape)],
            [blocks, low, low, pairs, pltpu.VMEM((1, HALF, PIXELS), BF16)] + back_scratch, 12 * batch)
        parts_down.append(row_exchange(outs[0:4]))
        back_sums = outs[4]
        if k == 0:
            back_sums, received = lax.optimization_barrier((back_sums, received))
            feed = gather_shares(sum_shares(received), devices)
        else:
            back_sums, parts_down[k - 1] = lax.optimization_barrier((back_sums, parts_down[k - 1]))
    for k in range(chunks):
        first = k * batch
        outs = call(
            functools.partial(backward_across_kernel, count, first), "across_backward", batch, [meta],
            [chunk_in(v) for v in across_tokens[k] + upward_across[k] + ahead_across[k][1]]
            + [full(v) for v in (wa, gain1, shift1, kern, back_sums)],
            [images_out(batch, pair, BF16)] * 2 + [whole_out(back_sums.shape)],
            [blocks, low, low, pairs, pltpu.VMEM((2, HALF, PIXELS // 2), BF16)] + back_scratch, 9 * batch)
        parts_across.append(col_exchange(outs[0], outs[1]))
        back_sums = outs[2]
        if k == 0:
            back_sums, feed = lax.optimization_barrier((back_sums, feed))
        else:
            back_sums, parts_across[k - 1], parts_down[-1] = lax.optimization_barrier(
                (back_sums, parts_across[k - 1], parts_down[-1])
            )
    rows = jnp.concatenate([back_sums, sums[1]])
    count_rows = rows.shape[0]
    rows = jnp.pad(rows, ((0, (-count_rows) % (8 * devices)), (0, 0)))
    back_rows = gather_shares(sum_shares(send_shares(rows, devices)), devices).astype(F32)
    feed = feed.astype(F32)

    tokens_grad = None
    for k in range(chunks):
        first = k * batch
        tokens_grad = call(
            functools.partial(finish_kernel, count, first), "finish", batch, [meta],
            [chunk_in(v) for v in [middles[k]] + parts_down[k] + parts_across[k]],
            [grid_out(first)],
            [pltpu.VMEM((4, ROWS, SLOT, DIM), F32), pltpu.VMEM((ROWS, 32, DIM), F32)], 2 * batch, tokens_grad)[0]

    triple_weight_grad = jnp.concatenate([back_rows[DIM * k : DIM * k + DIM] for k in range(3)], axis=1)
    vectors = back_rows[VEC : VEC + 16]
    rows = back_rows[VEC + 16 : VEC + 24]
    return (
        output,
        tokens_grad,
        vectors[0],
        vectors[1],
        triple_weight_grad,
        vectors[2:4],
        vectors[5:14].reshape(3, 3, DIM),
        vectors[4],
        feed[:, 2 * HIDDEN :],
        rows[7],
        rows[5],
        rows[6],
        feed[:, HIDDEN : 2 * HIDDEN],
        rows[0:4].reshape(HIDDEN),
        feed[:, 0:HIDDEN].T,
        rows[4],
    )


def solution(mesh):
    spread = P("batch", "row", "col", None)
    in_specs = (spread, P("batch"), P("batch"), P("batch", None), spread) + (P(),) * 14
    out_specs = (spread, spread) + (P(),) * 14
    devices = mesh.shape["batch"] * mesh.shape["row"] * mesh.shape["col"]
    return jax.shard_map(
        functools.partial(per_device, 2, devices),
        mesh=mesh, in_specs=in_specs, out_specs=out_specs, check_vma=False)
```

```python
import functools

import jax
import jax.numpy as jnp
from jax import lax
from jax.experimental import pallas as pl
from jax.experimental.pallas import tpu as pltpu
from jax.sharding import PartitionSpec as P

DIM = 256
HALF = 128
HEADS = 4
SIZE = 32
STRIPE = 7
ROWS = 28
SLOT = 8
PIX = ROWS * SLOT
HIDDEN = 1024
VEC = 3 * DIM
F32 = jnp.float32
BF16 = jnp.bfloat16
LOG2E = 1.4426950408889634
SCALE = SIZE**-0.5
EPS = 1e-05
GELU_C = 0.7978845608028654
GELU_A = 0.044715
VMEM_LIMIT = 56 * 1024 * 1024


def nn(a, b):
    return lax.dot_general(a, b, (((1,), (0,)), ((), ())), preferred_element_type=F32)


def nt(a, b):
    return lax.dot_general(a, b, (((1,), (1,)), ((), ())), preferred_element_type=F32)


def tn(a, b):
    return lax.dot_general(a, b, (((0,), (0,)), ((), ())), preferred_element_type=F32)


def col_sum(v):
    return jnp.sum(v, axis=0, keepdims=True)


def normalize(source):
    average = jnp.mean(source, axis=-1, keepdims=True)
    centered = source - average
    spread = jnp.mean(centered * centered, axis=-1, keepdims=True)
    rstd = lax.rsqrt(spread + EPS)
    return centered * rstd, rstd


def norm_back(grad_hat, hat, rstd):
    return rstd * (
        grad_hat
        - jnp.mean(grad_hat, axis=-1, keepdims=True)
        - hat * jnp.mean(grad_hat * hat, axis=-1, keepdims=True)
    )


def head_lanes(shape):
    return lax.broadcasted_iota(jnp.int32, shape, len(shape) - 1) // SIZE


def split_cols(source, wide, parts):
    wide[:, 0:ROWS, :] = source.astype(F32)
    slot = lax.broadcasted_iota(jnp.int32, (ROWS, SLOT, DIM), 1)
    for s in range(4):
        parts[s] = jnp.where(slot < STRIPE, wide[:, STRIPE * s : STRIPE * s + SLOT, :], 0.0)


def merge_cols(parts, wide):
    for s in range(4):
        wide[:, STRIPE * s : STRIPE * s + SLOT, :] = parts[s]
    return wide[:, 0:ROWS, :]


class Meta:
    def __init__(self, ref, count):
        self.ref = ref
        self.count = count

    def height(self, i):
        return self.ref[i]

    def width(self, i):
        return self.ref[self.count + i]

    def keep(self, i):
        return self.ref[2 * self.count + i]

    def feed(self, i):
        return self.ref[3 * self.count + i]

    def row(self):
        return self.ref[4 * self.count]

    def col(self):
        return self.ref[4 * self.count + 1]


def pair_start(owner):
    return 2 * (1 - owner)


def from_rows(refs, r, out):
    for k, ref in enumerate(refs):
        out[lax.rem(r + 4 - k, 4)] = ref[0]


def to_rows(refs, r, source):
    for k, ref in enumerate(refs):
        ref[0] = source[lax.rem(r + k, 4)]


def own_stripes(keep_ref, other_ref, c):
    for ref, owner in ((keep_ref, c), (other_ref, 1 - c)):
        for u in range(2):
            yield pl.ds(STRIPE * (pair_start(owner) + u), STRIPE), ref.at[0, u]


def prep_kernel(count, first, meta_ref, tok_ref, d0, d1, d2, d3, keep_ref, send_ref, wide, parts):
    meta = Meta(meta_ref, count)
    split_cols(tok_ref[0], wide, parts)
    r, c = meta.row(), meta.col()
    for k, ref in enumerate((d0, d1, d2, d3)):
        ref[0] = parts[lax.rem(r + k, 4)].reshape(PIX, DIM).astype(BF16)
    for where, ref in own_stripes(keep_ref, send_ref, c):
        ref[...] = parts[:, where].reshape(PIX, DIM).astype(BF16)


def down_mask(height, width, stripe):
    shape = (4 * ROWS, SLOT, HALF)
    row = lax.broadcasted_iota(jnp.int32, shape, 0)
    j = lax.broadcasted_iota(jnp.int32, shape, 1)
    limit = jnp.minimum(STRIPE, width - STRIPE * stripe)
    return jnp.where((row < height) & (j < limit), 1.0, 0.0)


def across_mask(height, width, stripe):
    shape = (2, 8, STRIPE, SLOT, HALF)
    u = lax.broadcasted_iota(jnp.int32, shape, 0)
    b = lax.broadcasted_iota(jnp.int32, shape, 1)
    row = lax.broadcasted_iota(jnp.int32, shape, 2)
    j = lax.broadcasted_iota(jnp.int32, shape, 3)
    good = (STRIPE * u + row < height - STRIPE * stripe) & (j < STRIPE) & (b * STRIPE + j < width)
    return jnp.where(good, 1.0, 0.0)


def down_flags(height, width, stripe):
    at = lax.broadcasted_iota(jnp.int32, (16, PIXELS), 1)
    limit = jnp.minimum(STRIPE, width - STRIPE * stripe)
    good = (at < SLOT * height) & (lax.rem(at, SLOT) < limit)
    return jnp.where(good, 1.0, 0.0).astype(BF16)


def across_flags(height, width, stripe):
    at = lax.broadcasted_iota(jnp.int32, (16, PIXELS), 1)
    size = STRIPE * SLOT
    u = jnp.where(at < PIXELS // 2, 0, 1)
    b = jnp.zeros_like(at)
    for k in range(1, 16):
        b = jnp.where(at >= size * k, k, b)
    rest = at - size * b
    j = lax.rem(rest, SLOT)
    row = (rest - j) // SLOT + STRIPE * u
    col = STRIPE * (b - SLOT * u) + j
    good = (row < height - STRIPE * stripe) & (j < STRIPE) & (col < width)
    return jnp.where(good, 1.0, 0.0).astype(BF16)


def moved_rows(v, axis, step):
    if step == 0:
        return v
    size = v.shape[axis]
    zero_shape = v.shape[:axis] + (1,) + v.shape[axis + 1 :]
    zero = jnp.zeros(zero_shape, v.dtype)
    if step > 0:
        return jnp.concatenate([lax.slice_in_dim(v, 1, size, axis=axis), zero], axis=axis)
    return jnp.concatenate([zero, lax.slice_in_dim(v, 0, size - 1, axis=axis)], axis=axis)


def roll8(v, shift):
    shape = v.shape
    flat = v.reshape(-1, SLOT, HALF)
    return pltpu.roll(flat, shift, 1).reshape(shape)


def moved_cols_down(v, step):
    if step == 0:
        return v
    return roll8(v, 1 if step < 0 else SLOT - 1)


def moved_cols_across(v, step):
    if step == 0:
        return v
    slot = lax.broadcasted_iota(jnp.int32, v.shape, 3)
    if step < 0:
        return jnp.where(slot == 0, moved_rows(roll8(v, 2), 1, -1), roll8(v, 1))
    return jnp.where(slot == STRIPE - 1, moved_rows(roll8(v, SLOT - 2), 1, 1), roll8(v, SLOT - 1))


def taps(v, across):
    moved_cols = moved_cols_across if across else moved_cols_down
    row_axis = 2 if across else 0
    for b in range(3):
        side = moved_cols(v, b - 1)
        for a in range(3):
            yield a, b, moved_rows(side, row_axis, a - 1)


def position_term(v, kern_ref, bias_ref, lanes, across):
    total = bias_ref[0:1, lanes]
    for a, b, moved in taps(v, across):
        total = total + moved * kern_ref[3 * a + b : 3 * a + b + 1, lanes]
    return total


def position_back(grad, v, kern_ref, lanes, across):
    total = 0.0
    for a, b, moved in taps(grad, across):
        k = 3 * (2 - a) + (2 - b)
        total = total + moved * kern_ref[k : k + 1, lanes]
    kernel_grads = []
    flat = grad.reshape(-1, HALF)
    found = {}
    for a, b, moved in taps(v, across):
        found[3 * a + b] = col_sum(flat * moved.reshape(-1, HALF))
    for k in range(9):
        kernel_grads.append(found[k])
    return total, kernel_grads, col_sum(flat)


DOWN_GRID = (4 * ROWS, SLOT, HALF)
ACROSS_GRID = (2, 8, STRIPE, SLOT, HALF)
DOWN_SIZES = (640, 768, 896)
ACROSS_SIZES = (336, 448)
DOWN_GROUP = 4
MIDDLE_GROUP = 2
HIDDEN_TILE = 256
DOWN_BACK_GROUP = 2
PIXELS = 4 * PIX


def by_size(used, sizes, body):
    below = None
    for n in sizes:
        fits = used <= n
        if n == sizes[-1]:
            fits = True if below is None else used > below
        elif below is not None:
            fits = fits & (used > below)
        pl.when(fits)(functools.partial(body, n))
        below = n


def project(x_ref, weight_ref, bias_ref, gain_ref, shift_ref):
    hat, unused = normalize(x_ref[...].reshape(PIXELS, DIM).astype(F32))
    normed = (hat * gain_ref[...] + shift_ref[...]).astype(BF16)
    return (nn(normed, weight_ref[...]) + bias_ref[...]).astype(BF16)


def split_queries(query):
    scaled = query.astype(F32) * (SCALE * LOG2E)
    high = scaled.astype(BF16)
    low = (scaled - high.astype(F32)).astype(BF16)
    return jnp.concatenate([high, low], axis=1)


def valid_keys(keys, mask, stripes):
    size = PIXELS // stripes
    keys = keys.astype(F32)
    fixed = [
        jnp.where(
            mask[size * u : size * u + size] > 0.0, keys[size * u : size * u + size], keys[size * u : size * u + 1]
        )
        for u in range(stripes)
    ]
    return jnp.concatenate(fixed, axis=0).astype(BF16)


def only_head(value, h):
    lane = lax.broadcasted_iota(jnp.int32, value.shape, 1)
    return jnp.where(lax.rem(lane, HALF) // SIZE == h, value, jnp.zeros_like(value))


def attend(key_ref, query_ref, turned_ref, base, at_out, lse_out, a_ref, full, group, n):
    part = pl.ds(base, n)
    whole_part = pl.ds(base, full)

    def heads_of(t, carry):
        heads = [t * group + j for j in range(group)]
        keys = key_ref[part]
        keys = jnp.concatenate([keys, keys], axis=1)
        queries = query_ref[part]
        scores = [nt(keys, only_head(queries, h)) for h in heads]
        tops = [jnp.max(s, axis=0, keepdims=True) for s in scores]
        weights = [jnp.exp2(s - top).astype(BF16) for s, top in zip(scores, tops)]
        outs = [nn(turned_ref[h, :, 0:n], w) for h, w in zip(heads, weights)]
        for h, out, top in zip(heads, outs, tops):
            total = out[SIZE : SIZE + 1]
            at_out[pl.ds(pl.multiple_of(h * SIZE, SIZE), SIZE), 0:n] = out[0:SIZE] / total
            lse_out[pl.ds(h, 1), 0:n] = top + jnp.log2(total)
        return carry

    if group == HEADS:
        heads_of(0, 0)
    else:
        lax.fori_loop(0, HEADS // group, heads_of, 0)
    if n < full:
        a_ref[whole_part] = jnp.zeros((full, HALF), F32)
    a_ref[part] = at_out[:, 0:n].T


def prepare_forward(x_ref, mask, flags, stripes, weight_ref, bias_ref, gain_ref, shift_ref, saved, key_ref, query_ref, turned_ref):
    q_out, k_out, v_out = saved
    triple = project(x_ref, weight_ref, bias_ref, gain_ref, shift_ref)
    q_out[...] = triple[:, 0:HALF]
    k_out[...] = triple[:, HALF : 2 * HALF]
    v_out[...] = triple[:, 2 * HALF :]
    query_ref[...] = split_queries(triple[:, 0:HALF])
    key_ref[...] = valid_keys(triple[:, HALF : 2 * HALF], mask, stripes)
    masked = triple[:, 2 * HALF :].astype(F32) * mask
    turned = masked.astype(BF16).T
    size = PIXELS // stripes
    for u in range(stripes):
        part = slice(size * u, size * u + size)
        for h in range(HEADS):
            turned_ref[u, h, 0:SIZE] = turned[SIZE * h : SIZE * h + SIZE, part]
            turned_ref[u, h, SIZE:] = flags[:, part]
    return masked


def down_used(height):
    return SLOT * height


def live_stripes(height, stripe):
    return jnp.where(STRIPE * (stripe + 1) < height, 2, 1)


def across_used(width):
    return STRIPE * SLOT * ((width + STRIPE - 1) // STRIPE)


def forward_down_kernel(count, first, meta_ref, xd0, xd1, xd2, xd3, weight_ref, bias_ref, gain_ref, shift_ref,
                        kern_ref, pos_ref, jd0, jd1, jd2, jd3, q_out, k_out, v_out, at_out, lse_out,
                        x_ref, key_ref, query_ref, turned_ref, a_ref, j_ref):
    meta = Meta(meta_ref, count)
    i = first + pl.program_id(0)
    r, c = meta.row(), meta.col()
    height, width = meta.height(i), meta.width(i)
    stripe = 4 * c + r
    live = (meta.keep(i) > 0) & (STRIPE * stripe < width)

    @pl.when(live)
    def _():
        from_rows((xd0, xd1, xd2, xd3), r, x_ref)
        mask = down_mask(height, width, stripe)
        masked = prepare_forward(
            x_ref, mask.reshape(PIXELS, HALF), down_flags(height, width, stripe), 1, weight_ref, bias_ref, gain_ref, shift_ref,
            (q_out.at[0], k_out.at[0], v_out.at[0]), key_ref, query_ref, turned_ref)

        def size(n):
            attend(key_ref, query_ref, turned_ref.at[0], 0, at_out.at[0], lse_out.at[0], a_ref, PIXELS, DOWN_GROUP, n)

        by_size(down_used(height), DOWN_SIZES, size)
        term = position_term(masked.reshape(DOWN_GRID), kern_ref, pos_ref, slice(HALF, DIM), False)
        total = a_ref[...] + term.reshape(PIXELS, HALF)
        j_ref[...] = total.astype(BF16).reshape(4, PIX, HALF)
        to_rows((jd0, jd1, jd2, jd3), r, j_ref)

    @pl.when(jnp.logical_not(live))
    def _():
        for ref in (jd0, jd1, jd2, jd3):
            ref[...] = jnp.zeros_like(ref)


def forward_across_kernel(count, first, meta_ref, xa_keep, xa_recv, weight_ref, bias_ref, gain_ref, shift_ref,
                          kern_ref, pos_ref, ja_keep, ja_send, q_out, k_out, v_out, at_out, lse_out,
                          x_ref, key_ref, query_ref, turned_ref, a_ref, j_ref):
    meta = Meta(meta_ref, count)
    i = first + pl.program_id(0)
    r, c = meta.row(), meta.col()
    height, width = meta.height(i), meta.width(i)
    stripe = 4 * r + pair_start(c)
    live = (meta.keep(i) > 0) & (STRIPE * stripe < height)

    @pl.when(live)
    def _():
        mask = across_mask(height, width, stripe)
        for u in range(2):
            x_ref[2 * u + c] = xa_keep[0, u]
            x_ref[2 * u + 1 - c] = xa_recv[0, u]
        masked = prepare_forward(
            x_ref, mask.reshape(PIXELS, HALF), across_flags(height, width, stripe), 2, weight_ref, bias_ref, gain_ref, shift_ref,
            (q_out.at[0], k_out.at[0], v_out.at[0]), key_ref, query_ref, turned_ref)
        half = PIXELS // 2
        a_ref[half:] = jnp.zeros((half, HALF), F32)

        def stripe_of(u, carry):
            def size(n):
                base = pl.multiple_of(u * half, half)
                attend(key_ref, query_ref, turned_ref.at[u], base, at_out.at[0, u], lse_out.at[0, u], a_ref, half, HEADS, n)

            by_size(across_used(width), ACROSS_SIZES, size)
            return carry

        lax.fori_loop(0, live_stripes(height, stripe), stripe_of, 0)
        term = position_term(masked.reshape(ACROSS_GRID), kern_ref, pos_ref, slice(0, HALF), True)
        j_ref[...] = (a_ref[...] + term.reshape(PIXELS, HALF)).astype(BF16).reshape(4, PIX, HALF)
        for u in range(2):
            ja_keep[0, u] = j_ref[2 * u + c]
            ja_send[0, u] = j_ref[2 * u + 1 - c]

    @pl.when(jnp.logical_not(live))
    def _():
        ja_keep[...] = jnp.zeros_like(ja_keep)
        ja_send[...] = jnp.zeros_like(ja_send)


def pixel_mask(height, width, first_block, blocks, r, c):
    shape = (blocks, ROWS, SLOT, HALF)
    s = lax.broadcasted_iota(jnp.int32, shape, 0) + first_block
    row = lax.broadcasted_iota(jnp.int32, shape, 1)
    j = lax.broadcasted_iota(jnp.int32, shape, 2)
    good = (row < height - ROWS * r) & (j < STRIPE) & (s * STRIPE + j < width - ROWS * c)
    mask = jnp.where(good, 1.0, 0.0).reshape(blocks * PIX, HALF)
    return jnp.concatenate([mask, mask], axis=1)


def gelu_pair(pre, d_act):
    square = pre * pre
    bend = jnp.tanh(pre * (GELU_C + (GELU_C * GELU_A) * square))
    half_one = 0.5 + 0.5 * bend
    slope = half_one + (0.5 * pre) * (1.0 - bend * bend) * (GELU_C + (3.0 * GELU_C * GELU_A) * square)
    return (pre * half_one).astype(BF16), (d_act * slope).astype(BF16)


def middle_kernel(count, first, meta_ref, fact_ref, xd0, xd1, xd2, xd3, jd0, jd1, jd2, jd3, ja_keep, ja_recv, grad_ref,
                  wm_ref, bm_ref, gain_ref, shift_ref, we_ref, be_ref, wr_ref, br_ref, *rest):
    if first > 0:
        start, start_v, *rest = rest
    (out_ref, dm_ref, dd0, dd1, dd2, dd3, da_keep, da_send, acc_out, acc_v, acc,
     x_ref, g_ref, ja_ref, j_ref, o_ref, dj_ref, wide) = rest
    meta = Meta(meta_ref, count)
    step = pl.program_id(0)
    i = first + step
    r, c = meta.row(), meta.col()
    height, width = meta.height(i), meta.width(i)
    attend_factor = fact_ref[2 * i]
    feed_factor = fact_ref[2 * i + 1]

    @pl.when(step == 0)
    def _():
        acc[...] = start[...] if first > 0 else jnp.zeros_like(acc)
        acc_v[...] = start_v[...] if first > 0 else jnp.zeros_like(acc_v)

    split_cols(grad_ref[0], wide, g_ref)
    for k, (xs, js) in enumerate(((xd0, jd0), (xd1, jd1), (xd2, jd2), (xd3, jd3))):
        x_ref[lax.rem(r + k, 4)] = xs[0]
        j_ref[lax.rem(r + 4 - k, 4), :, HALF:] = js[0]
    for where, ref in own_stripes(ja_keep, ja_recv, c):
        ja_ref[:, where] = ref[...].astype(F32).reshape(4, STRIPE, SLOT, HALF)
    j_ref[:, :, 0:HALF] = ja_ref[...].reshape(4, PIX, HALF).astype(BF16)

    group = MIDDLE_GROUP
    size = group * PIX

    def one(b, carry):
        where = pl.ds(group * b, group)
        mask = pixel_mask(height, width, group * b, group, r, c)
        scale_attend = mask * attend_factor
        scale_feed = mask * feed_factor
        x = x_ref[where].reshape(size, DIM).astype(F32)
        joined = j_ref[where].reshape(size, DIM)
        g = g_ref[where].reshape(size, DIM)
        mixed = nn(joined, wm_ref[...]) + bm_ref[...]
        middle = x + scale_attend * mixed
        hat, rstd = normalize(middle)
        normed = (hat * gain_ref[...] + shift_ref[...]).astype(BF16)
        d_reduced = (scale_feed * g).astype(BF16)
        turned_grad, turned_normed = d_reduced.T, normed.T
        tiles = HIDDEN // HIDDEN_TILE
        first_dots, hidden = {}, {}
        reduced, d_normed, sums = br_ref[...], 0.0, []
        for t in range(tiles + 2):
            if t < tiles:
                cols = slice(HIDDEN_TILE * t, HIDDEN_TILE * t + HIDDEN_TILE)
                first_dots[t] = nn(normed, we_ref[:, cols]), nt(d_reduced, wr_ref[cols])
            if 1 <= t <= tiles:
                j = t - 1
                cols = slice(HIDDEN_TILE * j, HIDDEN_TILE * j + HIDDEN_TILE)
                pre, d_act = first_dots.pop(j)
                hidden[j] = gelu_pair(pre + be_ref[:, cols], d_act)
            if t >= 2:
                j = t - 2
                cols = slice(HIDDEN_TILE * j, HIDDEN_TILE * j + HIDDEN_TILE)
                wide_cols = slice(HIDDEN + HIDDEN_TILE * j, HIDDEN + HIDDEN_TILE * j + HIDDEN_TILE)
                act, d_hidden = hidden.pop(j)
                reduced = reduced + nn(act, wr_ref[cols])
                d_normed = d_normed + nt(d_hidden, we_ref[:, cols])
                acc[:, cols] += nn(turned_grad, act)
                acc[:, wide_cols] += nn(turned_normed, d_hidden)
                sums.append(col_sum(d_hidden.astype(F32)))
        d_hidden_sum = jnp.concatenate(sums, axis=1)
        o_ref[where] = (middle + scale_feed * reduced).reshape(group, ROWS, SLOT, DIM)
        d_middle = g + norm_back(d_normed * gain_ref[...], hat, rstd)
        dm_ref[0, where] = d_middle.astype(BF16).reshape(group, PIX, DIM)
        d_mixed = (scale_attend * d_middle).astype(BF16)
        acc[:, 2 * HIDDEN :] += tn(joined, d_mixed)
        dj_ref[where] = nt(d_mixed, wm_ref[...]).reshape(group, ROWS, SLOT, DIM)
        rows = [d_hidden_sum[:, DIM * k : DIM * k + DIM] for k in range(4)]
        rows.append(col_sum(d_reduced.astype(F32)))
        rows.append(col_sum(d_normed * hat))
        rows.append(col_sum(d_normed))
        rows.append(col_sum(d_mixed.astype(F32)))
        acc_v[...] += jnp.concatenate(rows, axis=0)
        return carry

    lax.fori_loop(0, 4 // group, one, 0)

    @pl.when(step == pl.num_programs(0) - 1)
    def _():
        acc_out[...] = acc[...].astype(acc_out.dtype)

    out_ref[0] = merge_cols(o_ref, wide).astype(BF16)
    for k, ref in enumerate((dd0, dd1, dd2, dd3)):
        ref[0] = dj_ref[lax.rem(r + k, 4), :, :, HALF:].reshape(PIX, HALF).astype(BF16)
    for where, ref in own_stripes(da_keep, da_send, c):
        ref[...] = dj_ref[:, where, :, 0:HALF].reshape(PIX, HALF).astype(BF16)


def attend_back(key_ref, query_ref, q_ref, v_ref, turned_ref, up_ref, at_ref, lse_ref, base,
                delta_ref, dqt_ref, dq_ref, dk_ref, dv_ref, full, group, n):
    part = pl.ds(base, n)
    whole_part = pl.ds(base, full)
    product = up_ref[part].T.astype(F32) * at_ref[:, 0:n]
    for h in range(HEADS):
        delta_ref[h : h + 1, 0:n] = col_sum(product[SIZE * h : SIZE * h + SIZE])
    dk_ref[whole_part] = jnp.zeros((full, HALF), F32)

    def heads_of(t, carry):
        heads = [t * group + j for j in range(group)]
        keys = key_ref[part]
        keys = jnp.concatenate([keys, keys], axis=1)
        scaled, queries, values, up = query_ref[part], q_ref[part], v_ref[part], up_ref[part]
        ups = [only_head(up, h) for h in heads]
        scores = [nt(keys, only_head(scaled, h)) for h in heads]
        grads = [nt(values, u) for u in ups]
        softs = [jnp.exp2(s - lse_ref[pl.ds(h, 1), 0:n]) for h, s in zip(heads, scores)]
        backs = [(p * (g - delta_ref[pl.ds(h, 1), 0:n])).astype(BF16) for h, p, g in zip(heads, softs, grads)]
        lows = [p.astype(BF16) for p in softs]
        dv, dk = dv_ref[part], dk_ref[part]
        for p, u in zip(lows, ups):
            dv = dv + nn(p, u)
        for h, z in zip(heads, backs):
            dk = dk + nn(z, only_head(queries, h))
        dv_ref[part] = dv
        dk_ref[part] = dk
        for h, z in zip(heads, backs):
            rows = pl.ds(pl.multiple_of(h * SIZE, SIZE), SIZE)
            dqt_ref[rows, 0:n] = nn(turned_ref[rows, 0:n], z)
        return carry

    if group == HEADS:
        heads_of(0, 0)
    else:
        lax.fori_loop(0, HEADS // group, heads_of, 0)
    if n < full:
        dq_ref[whole_part] = jnp.zeros((full, HALF), F32)
    dq_ref[part] = dqt_ref[:, 0:n].T * SCALE


def prepare_back(mask, stripes, across, lanes, kern_ref, saved, up_ref, acc, key_ref, query_ref, turned_ref, dv_ref):
    q_ref, k_ref, v_ref = saved
    grid = ACROSS_GRID if across else DOWN_GRID
    key_ref[...] = valid_keys(k_ref[...], mask, stripes)
    query_ref[...] = split_queries(q_ref[...])
    turned = (k_ref[...].astype(F32) * mask).astype(BF16).T
    size = PIXELS // stripes
    for u in range(stripes):
        turned_ref[u] = turned[:, size * u : size * u + size]
    masked = v_ref[...].astype(F32) * mask
    grad = up_ref[...].astype(F32)
    back, kernel_rows, bias_row = position_back(grad.reshape(grid), masked.reshape(grid), kern_ref, lanes, across)
    dv_ref[...] = back.reshape(PIXELS, HALF)
    acc[VEC + 4 : VEC + 14, lanes] += jnp.concatenate([bias_row] + kernel_rows, axis=0)


def finish_back(x_ref, mask, lanes, weight_ref, gain_ref, shift_ref, acc, dq_ref, dk_ref, dv_ref):
    triple = jnp.concatenate([dq_ref[...], dk_ref[...] * (mask * SCALE), dv_ref[...] * mask], axis=1).astype(BF16)
    hat, rstd = normalize(x_ref[...].reshape(PIXELS, DIM).astype(F32))
    normed = (hat * gain_ref[...] + shift_ref[...]).astype(BF16)
    grads = tn(normed, triple)
    for k in range(3):
        acc[DIM * k : DIM * k + DIM, lanes] += grads[:, HALF * k : HALF * k + HALF]
    d_normed = nt(triple, weight_ref[...])
    sums = col_sum(triple.astype(F32))
    acc[VEC : VEC + 1] += col_sum(d_normed * hat)
    acc[VEC + 1 : VEC + 2] += col_sum(d_normed)
    acc[VEC + 2 : VEC + 3, lanes] += sums[:, 0:HALF]
    acc[VEC + 3 : VEC + 4, lanes] += sums[:, 2 * HALF :]
    return norm_back(d_normed * gain_ref[...], hat, rstd).astype(BF16).reshape(4, PIX, DIM)


def backward_down_kernel(count, first, begin, meta_ref, xd0, xd1, xd2, xd3, dd0, dd1, dd2, dd3,
                         q_in, k_in, v_in, at_in, lse_in, weight_ref, gain_ref, shift_ref, kern_ref,
                         *rest):
    if not begin:
        start, *rest = rest
    (pd0, pd1, pd2, pd3, acc,
                         x_ref, up_ref, key_ref, query_ref, turned_ref, dq_ref, dk_ref, dv_ref, part_ref,
                         delta_ref, dqt_ref) = rest
    meta = Meta(meta_ref, count)
    step = pl.program_id(0)
    i = first + step
    r, c = meta.row(), meta.col()
    height, width = meta.height(i), meta.width(i)

    @pl.when(step == 0)
    def _():
        acc[...] = jnp.zeros_like(acc) if begin else start[...]

    stripe = 4 * c + r
    live = (meta.keep(i) > 0) & (STRIPE * stripe < width)

    @pl.when(live)
    def _():
        mask = down_mask(height, width, stripe).reshape(PIXELS, HALF)
        lanes = slice(HALF, DIM)
        from_rows((xd0, xd1, xd2, xd3), r, x_ref)
        for k, ref in enumerate((dd0, dd1, dd2, dd3)):
            up_ref[pl.ds(pl.multiple_of(lax.rem(r + 4 - k, 4) * PIX, PIX), PIX)] = ref[0]
        prepare_back(mask, 1, False, lanes, kern_ref, (q_in.at[0], k_in.at[0], v_in.at[0]), up_ref, acc,
                     key_ref, query_ref, turned_ref, dv_ref)

        def size(n):
            attend_back(key_ref, query_ref, q_in.at[0], v_in.at[0], turned_ref.at[0], up_ref, at_in.at[0], lse_in.at[0],
                        0, delta_ref, dqt_ref, dq_ref, dk_ref, dv_ref, PIXELS, DOWN_BACK_GROUP, n)

        by_size(down_used(height), DOWN_SIZES, size)
        part_ref[...] = finish_back(x_ref, mask, lanes, weight_ref, gain_ref, shift_ref, acc, dq_ref, dk_ref, dv_ref)
        to_rows((pd0, pd1, pd2, pd3), r, part_ref)

    @pl.when(jnp.logical_not(live))
    def _():
        for ref in (pd0, pd1, pd2, pd3):
            ref[...] = jnp.zeros_like(ref)


def backward_across_kernel(count, first, begin, last, meta_ref, xa_keep, xa_recv, da_keep, da_recv,
                           q_in, k_in, v_in, at_in, lse_in, weight_ref, gain_ref, shift_ref, kern_ref,
                           *rest):
    if not begin:
        start, *rest = rest
    if last:
        extra, *rest = rest
    (pa_keep, pa_send, acc_out,
                           acc, x_ref, up_ref, key_ref, query_ref, turned_ref, dq_ref, dk_ref, dv_ref, part_ref,
                           delta_ref, dqt_ref) = rest
    meta = Meta(meta_ref, count)
    step = pl.program_id(0)
    i = first + step
    r, c = meta.row(), meta.col()
    height, width = meta.height(i), meta.width(i)

    @pl.when(step == 0)
    def _():
        acc[...] = jnp.zeros_like(acc) if begin else start[...]

    stripe = 4 * r + pair_start(c)
    live = (meta.keep(i) > 0) & (STRIPE * stripe < height)

    @pl.when(live)
    def _():
        mask = across_mask(height, width, stripe).reshape(PIXELS, HALF)
        lanes = slice(0, HALF)
        for u in range(2):
            for xs, ds, side in ((xa_keep, da_keep, c), (xa_recv, da_recv, 1 - c)):
                x_ref[2 * u + side] = xs[0, u]
                up_ref[pl.ds(pl.multiple_of((2 * u + side) * PIX, PIX), PIX)] = ds[0, u]
        prepare_back(mask, 2, True, lanes, kern_ref, (q_in.at[0], k_in.at[0], v_in.at[0]), up_ref, acc,
                     key_ref, query_ref, turned_ref, dv_ref)
        half = PIXELS // 2
        dk_ref[half:] = jnp.zeros((half, HALF), F32)
        dq_ref[half:] = jnp.zeros((half, HALF), F32)

        def stripe_of(u, carry):
            def size(n):
                base = pl.multiple_of(u * half, half)
                attend_back(key_ref, query_ref, q_in.at[0], v_in.at[0], turned_ref.at[u], up_ref,
                            at_in.at[0, u], lse_in.at[0, u], base, delta_ref, dqt_ref, dq_ref, dk_ref, dv_ref,
                            half, HEADS, n)

            by_size(across_used(width), ACROSS_SIZES, size)
            return carry

        lax.fori_loop(0, live_stripes(height, stripe), stripe_of, 0)
        part_ref[...] = finish_back(x_ref, mask, lanes, weight_ref, gain_ref, shift_ref, acc, dq_ref, dk_ref, dv_ref)
        for u in range(2):
            pa_keep[0, u] = part_ref[2 * u + c]
            pa_send[0, u] = part_ref[2 * u + 1 - c]

    @pl.when(jnp.logical_not(live))
    def _():
        pa_keep[...] = jnp.zeros_like(pa_keep)
        pa_send[...] = jnp.zeros_like(pa_send)

    @pl.when(step == pl.num_programs(0) - 1)
    def _():
        rows = acc.shape[0]
        if last:
            acc_out[0:rows] = acc[...].astype(BF16)
            acc_out[rows : rows + 16] = jnp.concatenate([extra[...], jnp.zeros_like(extra)], axis=0).astype(BF16)
            acc_out[rows + 16 :] = jnp.zeros((acc_out.shape[0] - rows - 16, DIM), BF16)
        else:
            acc_out[...] = acc[...]


def finish_kernel(count, first, meta_ref, dm_ref, pd0, pd1, pd2, pd3, pa_keep, pa_recv, out_ref, total, wide):
    meta = Meta(meta_ref, count)
    r, c = meta.row(), meta.col()
    total[...] = dm_ref[0].astype(F32).reshape(4, ROWS, SLOT, DIM)
    for k, ref in enumerate((pd0, pd1, pd2, pd3)):
        total[lax.rem(r + 4 - k, 4)] += ref[0].astype(F32).reshape(ROWS, SLOT, DIM)
    for where, ref in own_stripes(pa_keep, pa_recv, c):
        total[:, where] += ref[...].astype(F32).reshape(4, STRIPE, SLOT, DIM)
    out_ref[0] = merge_cols(total, wide).astype(BF16)


def whole(shape):
    zeros = (0,) * len(shape)
    return pl.BlockSpec(shape, lambda i, *unused: zeros)


def per_image(shape, first=0):
    zeros = (0,) * len(shape)
    return pl.BlockSpec((1,) + shape, lambda i, *unused: (first + i,) + zeros)


def call(body, name, batch, scalars, inputs, outputs, scratch, micros, held=None, waits=()):
    in_specs = [spec for spec, unused in inputs]
    out_specs = [spec for spec, unused in outputs]
    moved = sum(value.size * value.dtype.itemsize for unused, value in inputs)
    aliases = {}
    held = held or {}
    inner, skipped, extra = body, len(scalars) + len(inputs), len(held) + len(waits)

    def body(*refs):
        inner(*refs[:skipped], *refs[skipped + extra :])

    for k, place in enumerate(held):
        aliases[skipped + k] = place
    in_specs = in_specs + [pl.BlockSpec(memory_space=pl.ANY)] * extra
    inputs = inputs + [(None, value) for value in list(held.values()) + list(waits)]
    return list(pl.pallas_call(
        body,
        out_shape=[shape for unused, shape in outputs],
        grid_spec=pltpu.PrefetchScalarGridSpec(
            num_scalar_prefetch=len(scalars),
            grid=(batch,),
            in_specs=in_specs,
            out_specs=out_specs,
            scratch_shapes=scratch,
        ),
        compiler_params=pltpu.CompilerParams(
            dimension_semantics=("arbitrary",), vmem_limit_bytes=VMEM_LIMIT
        ),
        input_output_aliases=aliases,
        cost_estimate=pl.CostEstimate(flops=micros * 10**9, bytes_accessed=moved, transcendentals=0),
        name=name,
    )(*scalars, *[value for unused, value in inputs]))


def struct(shape, dtype):
    return jax.ShapeDtypeStruct(shape, dtype)


def images_out(batch, shape, dtype):
    return per_image(shape), struct((batch,) + shape, dtype)


def whole_out(shape, dtype=F32):
    return whole(shape), struct(shape, dtype)


def row_exchange(parts):
    size = lax.axis_size("row")
    return [parts[0]] + [
        lax.ppermute(parts[k], "row", [(q, (q + k) % size) for q in range(size)]) for k in range(1, size)
    ]


def col_exchange(keep, send):
    return [keep, lax.ppermute(send, "col", [(0, 1), (1, 0)])]


def together(*values):
    return lax.optimization_barrier(values)


def bits_of(size):
    found = []
    bit = 1
    while bit < size:
        found.append(bit)
        bit *= 2
    return found


def kept_total(flags):
    total = flags
    size = lax.axis_size("batch")
    for bit in bits_of(size):
        total = total + lax.ppermute(total, "batch", [(q, q ^ bit) for q in range(size)])
    return total


ALL = ("batch", "row", "col")
NEAR = ("batch", "col")


def send_shares(rows, axes):
    places = lax.axis_size(axes)
    sent = rows.astype(BF16).reshape((places, -1) + rows.shape[1:])
    return lax.all_to_all(sent, axes, 0, 0)


def sum_shares(received):
    return jnp.sum(received.astype(F32), axis=0).astype(BF16)


def gather_shares(share, axes):
    sent = jnp.broadcast_to(share[None], (lax.axis_size(axes),) + share.shape)
    return lax.all_to_all(sent, axes, 0, 0).reshape((-1,) + share.shape[1:])


def send_rows(share):
    size = lax.axis_size("row")
    return [lax.ppermute(share, "row", [(q, (q + k) % size) for q in range(size)]) for k in range(1, size)]


def per_device(batch, devices, tokens, heights, widths, keep_flags, out_grad, first_gain, first_shift, triple_weight,
               query_value_bias, position_kernel, position_bias, mixing_weight, mixing_bias, second_gain, second_shift,
               expand_weight, expand_bias, reduce_weight, reduce_bias):
    count = tokens.shape[0]
    chunks = count // batch
    r, c = lax.axis_index("row"), lax.axis_index("col")
    meta = jnp.concatenate(
        [heights, widths, keep_flags[:, 0], keep_flags[:, 1], jnp.stack([r, c]).astype(jnp.int32)]
    )
    kept = kept_total(jnp.sum(keep_flags.astype(F32), axis=0))
    share = kept / (count * lax.axis_size("batch"))
    factors = (keep_flags.astype(F32) / share).reshape(-1)

    def branch_weight(lo):
        return jnp.concatenate([triple_weight[:, DIM * k + lo : DIM * k + lo + HALF] for k in range(3)], axis=1)

    wa, wd = branch_weight(0), branch_weight(HALF)
    zeros = jnp.zeros((HALF,), F32)
    ba = jnp.concatenate([query_value_bias[0, :HALF], zeros, query_value_bias[1, :HALF]])[None]
    bd = jnp.concatenate([query_value_bias[0, HALF:], zeros, query_value_bias[1, HALF:]])[None]
    gain1, shift1 = first_gain[None], first_shift[None]
    gain2, shift2 = second_gain[None], second_shift[None]
    kern = jnp.pad(position_kernel.reshape(9, DIM), ((0, 7), (0, 0)))
    pos = position_bias[None]

    def full(value):
        return whole(value.shape), value

    def chunk_in(value):
        return per_image(value.shape[1:]), value

    def grid_out(first):
        return per_image((ROWS, ROWS, DIM), first), struct((count, ROWS, ROWS, DIM), BF16)

    pix = (PIX, DIM)
    half = (PIX, HALF)
    pair = (2, PIX, DIM)
    pair_half = (2, PIX, HALF)

    def all_images(shape, dtype, first):
        return per_image(shape, first), struct((count,) + shape, dtype)

    blocks = pltpu.VMEM((4, PIX, DIM), BF16)
    low = pltpu.VMEM((PIXELS, HALF), BF16)
    high = pltpu.VMEM((PIXELS, HALF), F32)
    pairs = pltpu.VMEM((PIXELS, DIM), BF16)
    low_blocks = pltpu.VMEM((4, PIX, HALF), BF16)
    parts_high = pltpu.VMEM((4, ROWS, SLOT, DIM), F32)
    wide = pltpu.VMEM((ROWS, 32, DIM), F32)

    def prepare(k, waits):
        first = k * batch
        outs = call(
            functools.partial(prep_kernel, count, first), "prep", batch, [meta],
            [(per_image((ROWS, ROWS, DIM), first), tokens)],
            [images_out(batch, pix, BF16)] * 4 + [images_out(batch, pair, BF16)] * 2,
            [wide, parts_high], 2 * batch, {}, waits)
        return outs[0:4], outs[4:6]

    flat = (PIXELS, HALF)

    def across_forward(k, taken, held, waits):
        first = k * batch
        shapes = [(pair_half, BF16)] * 2 + [(flat, BF16)] * 3 + [((2, HALF, PIXELS // 2), F32), ((2, 8, PIXELS // 2), F32)]
        return call(
            functools.partial(forward_across_kernel, count, first), "across_forward", batch, [meta],
            [chunk_in(v) for v in taken] + [full(v) for v in (wa, ba, gain1, shift1, kern, pos)],
            [all_images(shape, dtype, first) for shape, dtype in shapes],
            [blocks, low, pairs, pltpu.VMEM((2, HEADS, SIZE + 16, PIXELS // 2), BF16), high, low_blocks],
            5 * batch, dict(enumerate(held)), waits)

    def down_forward(k, taken, waits):
        first = k * batch
        out = images_out(batch, flat, BF16)
        outs = call(
            functools.partial(forward_down_kernel, count, first), "down_forward", batch, [meta],
            [chunk_in(v) for v in taken] + [full(v) for v in (wd, bd, gain1, shift1, kern, pos)],
            [images_out(batch, half, BF16)] * 4
            + [out, out, out, images_out(batch, (HALF, PIXELS), F32), images_out(batch, (8, PIXELS), F32)],
            [blocks, low, pairs, pltpu.VMEM((1, HEADS, SIZE + 16, PIXELS), BF16), high, low_blocks],
            6 * batch, {}, waits)
        return outs[0:4], outs[4:]

    own0, sent0 = prepare(0, [])
    col0 = col_exchange(*sent0)
    row0 = row_exchange(own0)
    across0 = across_forward(0, col0, [], [])
    own1, sent1 = prepare(1, across0[0:1])
    col1 = col_exchange(*sent1)
    row1 = row_exchange(own1)
    joined0, saved0 = down_forward(0, row0, own1[0:1])
    across1 = across_forward(1, col1, across0, saved0[0:1])
    joined_across = col_exchange(*across1[0:2])
    joined1, saved1 = down_forward(1, row1, across1[2:3])
    row_joined0 = row_exchange(joined0)
    row_joined1 = row_exchange(joined1)

    def middle(k, own, row_joined, held, sums, waits):
        first = k * batch
        last = k == chunks - 1
        acc_shape = (DIM, 2 * HIDDEN + DIM)
        return call(
            functools.partial(middle_kernel, count, first), "middle", batch, [meta, factors],
            [chunk_in(v) for v in own + row_joined]
            + [(per_image(v.shape[1:], first), v) for v in joined_across + [out_grad]]
            + [full(v) for v in (mixing_weight, mixing_bias[None], gain2, shift2, expand_weight, expand_bias[None],
                                 reduce_weight, reduce_bias[None])]
            + [full(v) for v in sums],
            [all_images((ROWS, ROWS, DIM), BF16, first), all_images((4,) + pix, BF16, first)]
            + [images_out(batch, half, BF16)] * 4 + [images_out(batch, pair_half, BF16)] * 2
            + [whole_out(acc_shape, BF16 if last else F32), whole_out((8, DIM))],
            [pltpu.VMEM(acc_shape, F32), pltpu.VMEM((4,) + pix, BF16), parts_high,
             pltpu.VMEM((4, ROWS, SLOT, HALF), F32), pltpu.VMEM((4,) + pix, BF16), parts_high, parts_high, wide],
            8 * batch, held, waits)

    mid0 = middle(0, own0, row_joined0, {}, [], saved1[0:1])
    row_grad0 = row_exchange(mid0[2:6])
    col_grad0 = col_exchange(*mid0[6:8])
    mid1 = middle(1, own1, row_joined1, {0: mid0[0], 1: mid0[1]}, mid0[8:10], [])
    output, middles = mid1[0:2]
    feed, row_grad0, col_grad0 = together(mid1[8], row_grad0, col_grad0)
    row_grad1 = row_exchange(mid1[2:6])
    col_grad1 = col_exchange(*mid1[6:8])
    received = send_shares(feed, NEAR)

    back_scratch = [high, high, high, blocks, pltpu.VMEM((8, PIXELS), F32), pltpu.VMEM((HALF, PIXELS), F32)]
    back_shape = (VEC + 16, DIM)

    def down_backward(k, taken, row_grad, saved, sums, waits):
        first = k * batch
        outs = call(
            functools.partial(backward_down_kernel, count, first, not sums), "down_backward", batch, [meta],
            [chunk_in(v) for v in taken + row_grad + saved] + [full(v) for v in (wd, gain1, shift1, kern)]
            + [full(v) for v in sums],
            [images_out(batch, pix, BF16)] * 4 + [whole_out(back_shape)],
            [blocks, low, low, pairs, pltpu.VMEM((1, HALF, PIXELS), BF16)] + back_scratch,
            11 * batch, {}, waits)
        return outs[0:4], outs[4:]

    def across_backward(k, taken, col_grad, sums, waits):
        first = k * batch
        last = k == chunks - 1
        out = whole_out((grad_rows, DIM), BF16) if last else whole_out(back_shape)
        outs = call(
            functools.partial(backward_across_kernel, count, first, not sums, last), "across_backward", batch, [meta],
            [chunk_in(v) for v in taken + col_grad] + [(per_image(v.shape[1:], first), v) for v in across1[2:]]
            + [full(v) for v in (wa, gain1, shift1, kern)] + [full(v) for v in sums],
            [images_out(batch, pair, BF16)] * 2 + [out],
            [pltpu.VMEM(back_shape, F32), blocks, low, low, pairs, pltpu.VMEM((2, HALF, PIXELS // 2), BF16)]
            + back_scratch, 9 * batch, {}, waits)
        return outs[0:2], outs[2]

    grad_rows = -(-(VEC + 32) // (8 * devices)) * 8 * devices
    part0, sums = across_backward(0, col0, col_grad0, [], mid1[8:9] + row_grad0[1:])
    col_part0 = col_exchange(*part0)
    received, sums, row_grad1, col_grad1 = together(received, sums, row_grad1, col_grad1)
    share = sum_shares(received)
    others = send_rows(share)
    part0, sums = down_backward(0, row0, row_grad0, saved0, [sums], row_grad1[1:] + col_grad1[1:])
    row_part0 = row_exchange(part0)
    others, sums, col_part0 = together(others, sums, col_part0)
    feed = gather_shares(sum_shares(jnp.stack([share] + others)), NEAR)
    part1, sums = down_backward(1, row1, row_grad1, saved1, sums, col_part0[1:])
    row_part1 = row_exchange(part1)
    feed, sums = together(feed, sums)
    part1, back = across_backward(1, col1, col_grad1, sums + [mid1[9]], row_part0[1:])
    col_part1 = col_exchange(*part1)
    back, row_part1, col_part0 = together(back, row_part1, col_part0)
    received = send_shares(back, ALL)

    def finish(k, row_part, col_part, held, waits):
        first = k * batch
        return call(
            functools.partial(finish_kernel, count, first), "finish", batch, [meta],
            [(per_image(middles.shape[1:], first), middles)] + [chunk_in(v) for v in row_part + col_part],
            [grid_out(first)], [parts_high, wide], 2 * batch, held, waits)

    grad0 = finish(0, row_part0, col_part0, {}, [])
    rows = gather_shares(sum_shares(received), ALL)
    tokens_grad = finish(1, row_part1, col_part1, {0: grad0[0]}, [])[0]
    back_rows = rows.astype(F32)
    feed = feed.astype(F32)

    triple_weight_grad = jnp.concatenate([back_rows[DIM * k : DIM * k + DIM] for k in range(3)], axis=1)
    vectors = back_rows[VEC : VEC + 16]
    rows = back_rows[VEC + 16 : VEC + 24]
    return (
        output,
        tokens_grad,
        vectors[0],
        vectors[1],
        triple_weight_grad,
        vectors[2:4],
        vectors[5:14].reshape(3, 3, DIM),
        vectors[4],
        feed[:, 2 * HIDDEN :],
        rows[7],
        rows[5],
        rows[6],
        feed[:, HIDDEN : 2 * HIDDEN],
        rows[0:4].reshape(HIDDEN),
        feed[:, 0:HIDDEN].T,
        rows[4],
    )


def solution(mesh):
    spread = P("batch", "row", "col", None)
    in_specs = (spread, P("batch"), P("batch"), P("batch", None), spread) + (P(),) * 14
    out_specs = (spread, spread) + (P(),) * 14
    devices = mesh.shape["batch"] * mesh.shape["row"] * mesh.shape["col"]
    return jax.shard_map(
        functools.partial(per_device, 2, devices),
        mesh=mesh, in_specs=in_specs, out_specs=out_specs, check_vma=False)
```

```python
import functools

import jax
import jax.numpy as jnp
from jax import lax
from jax.experimental import pallas as pl
from jax.experimental.pallas import tpu as pltpu
from jax.sharding import PartitionSpec as P

DIM = 256
HALF = 128
HEADS = 4
SIZE = 32
STRIPE = 7
ROWS = 28
SLOT = 8
PIX = ROWS * SLOT
HIDDEN = 1024
VEC = DIM
PACKED = 3 * DIM + HALF
F32 = jnp.float32
BF16 = jnp.bfloat16
LOG2E = 1.4426950408889634
SCALE = SIZE**-0.5
EPS = 1e-05
GELU_C = 0.7978845608028654
GELU_A = 0.044715
VMEM_LIMIT = 56 * 1024 * 1024


def nn(a, b):
    return lax.dot_general(a, b, (((1,), (0,)), ((), ())), preferred_element_type=F32)


def nt(a, b):
    return lax.dot_general(a, b, (((1,), (1,)), ((), ())), preferred_element_type=F32)


def tn(a, b):
    return lax.dot_general(a, b, (((0,), (0,)), ((), ())), preferred_element_type=F32)


def col_sum(v):
    return jnp.sum(v, axis=0, keepdims=True)


def normalize(source):
    average = jnp.mean(source, axis=-1, keepdims=True)
    centered = source - average
    spread = jnp.mean(centered * centered, axis=-1, keepdims=True)
    rstd = lax.rsqrt(spread + EPS)
    return centered * rstd, rstd


def norm_back(grad_hat, hat, rstd):
    return rstd * (
        grad_hat
        - jnp.mean(grad_hat, axis=-1, keepdims=True)
        - hat * jnp.mean(grad_hat * hat, axis=-1, keepdims=True)
    )


def head_lanes(shape):
    return lax.broadcasted_iota(jnp.int32, shape, len(shape) - 1) // SIZE


def split_cols(source, wide, parts):
    wide[:, 0:ROWS, :] = source.astype(F32)
    slot = lax.broadcasted_iota(jnp.int32, (ROWS, SLOT, DIM), 1)
    for s in range(4):
        parts[s] = jnp.where(slot < STRIPE, wide[:, STRIPE * s : STRIPE * s + SLOT, :], 0.0)


def merge_cols(parts, wide):
    for s in range(4):
        wide[:, STRIPE * s : STRIPE * s + SLOT, :] = parts[s]
    return wide[:, 0:ROWS, :]


class Meta:
    def __init__(self, ref, count):
        self.ref = ref
        self.count = count

    def height(self, i):
        return self.ref[i]

    def width(self, i):
        return self.ref[self.count + i]

    def keep(self, i):
        return self.ref[2 * self.count + i]

    def feed(self, i):
        return self.ref[3 * self.count + i]

    def row(self):
        return self.ref[4 * self.count]

    def col(self):
        return self.ref[4 * self.count + 1]


def pair_start(owner):
    return 2 * (1 - owner)


def from_rows(refs, r, out):
    for k, ref in enumerate(refs):
        out[lax.rem(r + 4 - k, 4)] = ref[0]


def to_rows(refs, r, source):
    for k, ref in enumerate(refs):
        ref[0] = source[lax.rem(r + k, 4)]


def own_stripes(keep_ref, other_ref, c):
    for ref, owner in ((keep_ref, c), (other_ref, 1 - c)):
        for u in range(2):
            yield pl.ds(STRIPE * (pair_start(owner) + u), STRIPE), ref.at[0, u]


def fetch(source, target, sem):
    return pltpu.make_async_copy(source, target, sem)


def prep_kernel(count, first, meta_ref, tok_ref, d0, d1, d2, d3, keep_ref, send_ref, wide, parts):
    meta = Meta(meta_ref, count)
    split_cols(tok_ref[0], wide, parts)
    r, c = meta.row(), meta.col()
    for k, ref in enumerate((d0, d1, d2, d3)):
        ref[0] = parts[lax.rem(r + k, 4)].reshape(PIX, DIM).astype(BF16)
    for where, ref in own_stripes(keep_ref, send_ref, c):
        ref[...] = parts[:, where].reshape(PIX, DIM).astype(BF16)


def down_mask(height, width, stripe):
    shape = (4 * ROWS, SLOT, HALF)
    row = lax.broadcasted_iota(jnp.int32, shape, 0)
    j = lax.broadcasted_iota(jnp.int32, shape, 1)
    limit = jnp.minimum(STRIPE, width - STRIPE * stripe)
    return jnp.where((row < height) & (j < limit), 1.0, 0.0)


def across_mask(height, width, stripe):
    shape = (2, 8, STRIPE, SLOT, HALF)
    u = lax.broadcasted_iota(jnp.int32, shape, 0)
    b = lax.broadcasted_iota(jnp.int32, shape, 1)
    row = lax.broadcasted_iota(jnp.int32, shape, 2)
    j = lax.broadcasted_iota(jnp.int32, shape, 3)
    good = (STRIPE * u + row < height - STRIPE * stripe) & (j < STRIPE) & (b * STRIPE + j < width)
    return jnp.where(good, 1.0, 0.0)


def down_flags(height, width, stripe):
    at = lax.broadcasted_iota(jnp.int32, (16, PIXELS), 1)
    limit = jnp.minimum(STRIPE, width - STRIPE * stripe)
    good = (at < SLOT * height) & (lax.rem(at, SLOT) < limit)
    return jnp.where(good, 1.0, 0.0).astype(BF16)


def across_flags(height, width, stripe):
    at = lax.broadcasted_iota(jnp.int32, (16, PIXELS), 1)
    size = STRIPE * SLOT
    u = jnp.where(at < PIXELS // 2, 0, 1)
    b = jnp.zeros_like(at)
    for k in range(1, 16):
        b = jnp.where(at >= size * k, k, b)
    rest = at - size * b
    j = lax.rem(rest, SLOT)
    row = (rest - j) // SLOT + STRIPE * u
    col = STRIPE * (b - SLOT * u) + j
    good = (row < height - STRIPE * stripe) & (j < STRIPE) & (col < width)
    return jnp.where(good, 1.0, 0.0).astype(BF16)


def moved_rows(v, axis, step):
    if step == 0:
        return v
    size = v.shape[axis]
    zero_shape = v.shape[:axis] + (1,) + v.shape[axis + 1 :]
    zero = jnp.zeros(zero_shape, v.dtype)
    if step > 0:
        return jnp.concatenate([lax.slice_in_dim(v, 1, size, axis=axis), zero], axis=axis)
    return jnp.concatenate([zero, lax.slice_in_dim(v, 0, size - 1, axis=axis)], axis=axis)


def roll8(v, shift):
    shape = v.shape
    flat = v.reshape(-1, SLOT, HALF)
    return pltpu.roll(flat, shift, 1).reshape(shape)


def moved_cols_down(v, step):
    if step == 0:
        return v
    return roll8(v, 1 if step < 0 else SLOT - 1)


def moved_cols_across(v, step):
    if step == 0:
        return v
    slot = lax.broadcasted_iota(jnp.int32, v.shape, 3)
    if step < 0:
        return jnp.where(slot == 0, moved_rows(roll8(v, 2), 1, -1), roll8(v, 1))
    return jnp.where(slot == STRIPE - 1, moved_rows(roll8(v, SLOT - 2), 1, 1), roll8(v, SLOT - 1))


def taps(v, across):
    moved_cols = moved_cols_across if across else moved_cols_down
    row_axis = 2 if across else 0
    for b in range(3):
        side = moved_cols(v, b - 1)
        for a in range(3):
            yield a, b, moved_rows(side, row_axis, a - 1)


def position_term(v, kern_ref, bias_ref, lanes, across):
    total = bias_ref[0:1, lanes]
    for a, b, moved in taps(v, across):
        total = total + moved * kern_ref[3 * a + b : 3 * a + b + 1, lanes]
    return total


def position_back(grad, v, kern_ref, lanes, across):
    total = 0.0
    for a, b, moved in taps(grad, across):
        k = 3 * (2 - a) + (2 - b)
        total = total + moved * kern_ref[k : k + 1, lanes]
    kernel_grads = []
    flat = grad.reshape(-1, HALF)
    found = {}
    for a, b, moved in taps(v, across):
        found[3 * a + b] = col_sum(flat * moved.reshape(-1, HALF))
    for k in range(9):
        kernel_grads.append(found[k])
    return total, kernel_grads, col_sum(flat)


DOWN_GRID = (4 * ROWS, SLOT, HALF)
ACROSS_GRID = (2, 8, STRIPE, SLOT, HALF)
DOWN_SIZES = (640, 768, 896)
ACROSS_SIZES = (336, 448)
DOWN_GROUP = 4
MIDDLE_GROUP = 4
HIDDEN_TILE = 512
DOWN_BACK_GROUP = 2
PIXELS = 4 * PIX


def by_size(used, sizes, body):
    below = None
    for n in sizes:
        fits = used <= n
        if n == sizes[-1]:
            fits = True if below is None else used > below
        elif below is not None:
            fits = fits & (used > below)
        pl.when(fits)(functools.partial(body, n))
        below = n


def project(x_ref, weight_ref, bias_ref, gain_ref, shift_ref):
    hat, unused = normalize(x_ref[...].reshape(PIXELS, DIM).astype(F32))
    normed = (hat * gain_ref[...] + shift_ref[...]).astype(BF16)
    return (nn(normed, weight_ref[...]) + bias_ref[...]).astype(BF16)


def split_queries(query):
    scaled = query.astype(F32) * (SCALE * LOG2E)
    high = scaled.astype(BF16)
    low = (scaled - high.astype(F32)).astype(BF16)
    return jnp.concatenate([high, low], axis=1)


def valid_keys(keys, mask, stripes):
    size = PIXELS // stripes
    keys = keys.astype(F32)
    fixed = [
        jnp.where(
            mask[size * u : size * u + size] > 0.0, keys[size * u : size * u + size], keys[size * u : size * u + 1]
        )
        for u in range(stripes)
    ]
    return jnp.concatenate(fixed, axis=0).astype(BF16)


def only_head(value, h):
    lane = lax.broadcasted_iota(jnp.int32, value.shape, 1)
    return jnp.where(lax.rem(lane, HALF) // SIZE == h, value, jnp.zeros_like(value))


def attend(key_ref, query_ref, turned_ref, base, at_out, lse_out, a_ref, turned_a, full, group, n):
    part = pl.ds(base, n)
    whole_part = pl.ds(base, full)

    def heads_of(t, carry):
        heads = [t * group + j for j in range(group)]
        keys = key_ref[part]
        keys = jnp.concatenate([keys, keys], axis=1)
        queries = query_ref[part]
        scores = [nt(keys, only_head(queries, h)) for h in heads]
        tops = [jnp.max(s, axis=0, keepdims=True) for s in scores]
        weights = [jnp.exp2(s - top).astype(BF16) for s, top in zip(scores, tops)]
        outs = [nn(turned_ref[h, :, 0:n], w) for h, w in zip(heads, weights)]
        for h, out, top in zip(heads, outs, tops):
            total = out[SIZE : SIZE + 1]
            turned_a[pl.ds(pl.multiple_of(h * SIZE, SIZE), SIZE), 0:n] = out[0:SIZE] / total
            lse_out[pl.ds(h, 1), 0:n] = top + jnp.log2(total)
        return carry

    if group == HEADS:
        heads_of(0, 0)
    else:
        lax.fori_loop(0, HEADS // group, heads_of, 0)
    if n < full:
        a_ref[whole_part] = jnp.zeros((full, HALF), F32)
    at_out[:, 0:n] = turned_a[:, 0:n].astype(BF16)
    a_ref[part] = turned_a[:, 0:n].T


def prepare_forward(x_ref, mask, flags, stripes, weight_ref, bias_ref, gain_ref, shift_ref, saved, key_ref, query_ref, turned_ref):
    q_out, k_out, v_out = saved
    triple = project(x_ref, weight_ref, bias_ref, gain_ref, shift_ref)
    q_out[...] = triple[:, 0:HALF]
    k_out[...] = triple[:, HALF : 2 * HALF]
    v_out[...] = triple[:, 2 * HALF :]
    query_ref[...] = split_queries(triple[:, 0:HALF])
    key_ref[...] = valid_keys(triple[:, HALF : 2 * HALF], mask, stripes)
    masked = triple[:, 2 * HALF :].astype(F32) * mask
    turned = masked.astype(BF16).T
    size = PIXELS // stripes
    for u in range(stripes):
        part = slice(size * u, size * u + size)
        for h in range(HEADS):
            turned_ref[u, h, 0:SIZE] = turned[SIZE * h : SIZE * h + SIZE, part]
            turned_ref[u, h, SIZE:] = flags[:, part]
    return masked


def down_used(height):
    return SLOT * height


def live_stripes(height, stripe):
    return jnp.where(STRIPE * (stripe + 1) < height, 2, 1)


def across_used(width):
    return STRIPE * SLOT * ((width + STRIPE - 1) // STRIPE)


def forward_down_kernel(count, first, meta_ref, xd0, xd1, xd2, xd3, weight_ref, bias_ref, gain_ref, shift_ref,
                        kern_ref, pos_ref, jd0, jd1, jd2, jd3, q_out, k_out, v_out, at_out, lse_out,
                        x_ref, key_ref, query_ref, turned_ref, a_ref, j_ref, turned_a):
    meta = Meta(meta_ref, count)
    i = first + pl.program_id(0)
    r, c = meta.row(), meta.col()
    height, width = meta.height(i), meta.width(i)
    stripe = 4 * c + r
    live = (meta.keep(i) > 0) & (STRIPE * stripe < width)

    @pl.when(live)
    def _():
        from_rows((xd0, xd1, xd2, xd3), r, x_ref)
        mask = down_mask(height, width, stripe)
        masked = prepare_forward(
            x_ref, mask.reshape(PIXELS, HALF), down_flags(height, width, stripe), 1, weight_ref, bias_ref, gain_ref, shift_ref,
            (q_out.at[0], k_out.at[0], v_out.at[0]), key_ref, query_ref, turned_ref)

        def size(n):
            attend(key_ref, query_ref, turned_ref.at[0], 0, at_out.at[0], lse_out.at[0], a_ref, turned_a, PIXELS, DOWN_GROUP, n)

        by_size(down_used(height), DOWN_SIZES, size)
        term = position_term(masked.reshape(DOWN_GRID), kern_ref, pos_ref, slice(HALF, DIM), False)
        total = a_ref[...] + term.reshape(PIXELS, HALF)
        j_ref[...] = total.astype(BF16).reshape(4, PIX, HALF)
        to_rows((jd0, jd1, jd2, jd3), r, j_ref)

    @pl.when(jnp.logical_not(live))
    def _():
        for ref in (jd0, jd1, jd2, jd3):
            ref[...] = jnp.zeros_like(ref)


def forward_across_kernel(count, first, meta_ref, xa_keep, xa_recv, weight_ref, bias_ref, gain_ref, shift_ref,
                          kern_ref, pos_ref, ja_keep, ja_send, q_out, k_out, v_out, at_out, lse_out,
                          x_ref, key_ref, query_ref, turned_ref, a_ref, j_ref, turned_a):
    meta = Meta(meta_ref, count)
    i = first + pl.program_id(0)
    r, c = meta.row(), meta.col()
    height, width = meta.height(i), meta.width(i)
    stripe = 4 * r + pair_start(c)
    live = (meta.keep(i) > 0) & (STRIPE * stripe < height)

    @pl.when(live)
    def _():
        mask = across_mask(height, width, stripe)
        for u in range(2):
            x_ref[2 * u + c] = xa_keep[0, u]
            x_ref[2 * u + 1 - c] = xa_recv[0, u]
        masked = prepare_forward(
            x_ref, mask.reshape(PIXELS, HALF), across_flags(height, width, stripe), 2, weight_ref, bias_ref, gain_ref, shift_ref,
            (q_out.at[0], k_out.at[0], v_out.at[0]), key_ref, query_ref, turned_ref)
        half = PIXELS // 2
        a_ref[half:] = jnp.zeros((half, HALF), F32)

        def stripe_of(u, carry):
            def size(n):
                base = pl.multiple_of(u * half, half)
                attend(key_ref, query_ref, turned_ref.at[u], base, at_out.at[0, u], lse_out.at[0, u], a_ref, turned_a, half, HEADS, n)

            by_size(across_used(width), ACROSS_SIZES, size)
            return carry

        lax.fori_loop(0, live_stripes(height, stripe), stripe_of, 0)
        term = position_term(masked.reshape(ACROSS_GRID), kern_ref, pos_ref, slice(0, HALF), True)
        j_ref[...] = (a_ref[...] + term.reshape(PIXELS, HALF)).astype(BF16).reshape(4, PIX, HALF)
        for u in range(2):
            ja_keep[0, u] = j_ref[2 * u + c]
            ja_send[0, u] = j_ref[2 * u + 1 - c]

    @pl.when(jnp.logical_not(live))
    def _():
        ja_keep[...] = jnp.zeros_like(ja_keep)
        ja_send[...] = jnp.zeros_like(ja_send)


def pixel_mask(height, width, first_block, blocks, r, c):
    shape = (blocks, ROWS, SLOT, HALF)
    s = lax.broadcasted_iota(jnp.int32, shape, 0) + first_block
    row = lax.broadcasted_iota(jnp.int32, shape, 1)
    j = lax.broadcasted_iota(jnp.int32, shape, 2)
    good = (row < height - ROWS * r) & (j < STRIPE) & (s * STRIPE + j < width - ROWS * c)
    mask = jnp.where(good, 1.0, 0.0).reshape(blocks * PIX, HALF)
    return jnp.concatenate([mask, mask], axis=1)


def gelu_pair(pre, d_act):
    square = pre * pre
    bend = jnp.tanh(pre * (GELU_C + (GELU_C * GELU_A) * square))
    half_one = 0.5 + 0.5 * bend
    slope = half_one + (0.5 * pre) * (1.0 - bend * bend) * (GELU_C + (3.0 * GELU_C * GELU_A) * square)
    return (pre * half_one).astype(BF16), (d_act * slope).astype(BF16)


def middle_kernel(count, first, meta_ref, fact_ref, xd0, xd1, xd2, xd3, jd0, jd1, jd2, jd3, ja_keep, ja_recv, grad_ref,
                  wm_ref, bm_ref, gain_ref, shift_ref, we_ref, be_ref, wr_ref, br_ref, *rest):
    if first > 0:
        start, start_v, *rest = rest
        *rest, early, sem = rest
    (out_ref, dm_ref, dd0, dd1, dd2, dd3, da_keep, da_send, acc_out, acc_v, acc,
     x_ref, g_ref, ja_ref, j_ref, o_ref, dj_ref, wide) = rest
    meta = Meta(meta_ref, count)
    step = pl.program_id(0)
    i = first + step
    r, c = meta.row(), meta.col()
    height, width = meta.height(i), meta.width(i)
    attend_factor = fact_ref[2 * i]
    feed_factor = fact_ref[2 * i + 1]

    @pl.when(step == 0)
    def _():
        if first > 0:
            fetch(start, early, sem).start()
        acc[...] = jnp.zeros_like(acc)
        acc_v[...] = start_v[...] if first > 0 else jnp.zeros_like(acc_v)

    split_cols(grad_ref[0], wide, g_ref)
    for k, (xs, js) in enumerate(((xd0, jd0), (xd1, jd1), (xd2, jd2), (xd3, jd3))):
        x_ref[lax.rem(r + k, 4)] = xs[0]
        j_ref[lax.rem(r + 4 - k, 4), :, HALF:] = js[0]
    for where, ref in own_stripes(ja_keep, ja_recv, c):
        ja_ref[:, where] = ref[...].astype(F32).reshape(4, STRIPE, SLOT, HALF)
    j_ref[:, :, 0:HALF] = ja_ref[...].reshape(4, PIX, HALF).astype(BF16)

    group = MIDDLE_GROUP
    size = group * PIX

    def one(b, carry):
        where = pl.ds(group * b, group)
        mask = pixel_mask(height, width, group * b, group, r, c)
        scale_attend = mask * attend_factor
        scale_feed = mask * feed_factor
        x = x_ref[where].reshape(size, DIM).astype(F32)
        joined = j_ref[where].reshape(size, DIM)
        g = g_ref[where].reshape(size, DIM)
        mixed = nn(joined, wm_ref[...]) + bm_ref[...]
        middle = x + scale_attend * mixed
        hat, rstd = normalize(middle)
        normed = (hat * gain_ref[...] + shift_ref[...]).astype(BF16)
        d_reduced = (scale_feed * g).astype(BF16)
        turned_grad, turned_normed = d_reduced.T, normed.T
        tiles = HIDDEN // HIDDEN_TILE
        first_dots, hidden = {}, {}
        reduced, d_normed, sums = br_ref[...], 0.0, []
        for t in range(tiles + 2):
            if t < tiles:
                cols = slice(HIDDEN_TILE * t, HIDDEN_TILE * t + HIDDEN_TILE)
                first_dots[t] = nn(normed, we_ref[:, cols]), nt(d_reduced, wr_ref[cols])
            if 1 <= t <= tiles:
                j = t - 1
                cols = slice(HIDDEN_TILE * j, HIDDEN_TILE * j + HIDDEN_TILE)
                pre, d_act = first_dots.pop(j)
                hidden[j] = gelu_pair(pre + be_ref[:, cols], d_act)
            if t >= 2:
                j = t - 2
                cols = slice(HIDDEN_TILE * j, HIDDEN_TILE * j + HIDDEN_TILE)
                wide_cols = slice(HIDDEN + HIDDEN_TILE * j, HIDDEN + HIDDEN_TILE * j + HIDDEN_TILE)
                act, d_hidden = hidden.pop(j)
                reduced = reduced + nn(act, wr_ref[cols])
                d_normed = d_normed + nt(d_hidden, we_ref[:, cols])
                acc[:, cols] += nn(turned_grad, act)
                acc[:, wide_cols] += nn(turned_normed, d_hidden)
                sums.append(col_sum(d_hidden.astype(F32)))
        d_hidden_sum = jnp.concatenate(sums, axis=1)
        o_ref[where] = (middle + scale_feed * reduced).reshape(group, ROWS, SLOT, DIM)
        d_middle = g + norm_back(d_normed * gain_ref[...], hat, rstd)
        dm_ref[0, where] = d_middle.astype(BF16).reshape(group, PIX, DIM)
        d_mixed = (scale_attend * d_middle).astype(BF16)
        acc[:, 2 * HIDDEN :] += tn(joined, d_mixed)
        dj_ref[where] = nt(d_mixed, wm_ref[...]).reshape(group, ROWS, SLOT, DIM)
        rows = [d_hidden_sum[:, DIM * k : DIM * k + DIM] for k in range(4)]
        rows.append(col_sum(d_reduced.astype(F32)))
        rows.append(col_sum(d_normed * hat))
        rows.append(col_sum(d_normed))
        rows.append(col_sum(d_mixed.astype(F32)))
        acc_v[...] += jnp.concatenate(rows, axis=0)
        return carry

    lax.fori_loop(0, 4 // group, one, 0)

    @pl.when(step == pl.num_programs(0) - 1)
    def _():
        if first > 0:
            fetch(start, early, sem).wait()
            acc_out[...] = (acc[...] + early[...].astype(F32)).astype(BF16)
        else:
            acc_out[...] = acc[...].astype(BF16)

    out_ref[0] = merge_cols(o_ref, wide).astype(BF16)
    for k, ref in enumerate((dd0, dd1, dd2, dd3)):
        ref[0] = dj_ref[lax.rem(r + k, 4), :, :, HALF:].reshape(PIX, HALF).astype(BF16)
    for where, ref in own_stripes(da_keep, da_send, c):
        ref[...] = dj_ref[:, where, :, 0:HALF].reshape(PIX, HALF).astype(BF16)


def attend_back(key_ref, query_ref, q_ref, v_ref, turned_ref, up_ref, at_ref, lse_ref, base,
                delta_ref, dqt_ref, dq_ref, dk_ref, dv_ref, full, group, n):
    part = pl.ds(base, n)
    whole_part = pl.ds(base, full)
    product = up_ref[part].T.astype(F32) * at_ref[:, 0:n].astype(F32)
    for h in range(HEADS):
        delta_ref[h : h + 1, 0:n] = col_sum(product[SIZE * h : SIZE * h + SIZE])
    dk_ref[whole_part] = jnp.zeros((full, HALF), F32)

    def heads_of(t, carry):
        heads = [t * group + j for j in range(group)]
        keys = key_ref[part]
        keys = jnp.concatenate([keys, keys], axis=1)
        scaled, queries, values, up = query_ref[part], q_ref[part], v_ref[part], up_ref[part]
        ups = [only_head(up, h) for h in heads]
        scores = [nt(keys, only_head(scaled, h)) for h in heads]
        grads = [nt(values, u) for u in ups]
        softs = [jnp.exp2(s - lse_ref[pl.ds(h, 1), 0:n]) for h, s in zip(heads, scores)]
        backs = [(p * (g - delta_ref[pl.ds(h, 1), 0:n])).astype(BF16) for h, p, g in zip(heads, softs, grads)]
        lows = [p.astype(BF16) for p in softs]
        dv, dk = dv_ref[part], dk_ref[part]
        for p, u in zip(lows, ups):
            dv = dv + nn(p, u)
        for h, z in zip(heads, backs):
            dk = dk + nn(z, only_head(queries, h))
        dv_ref[part] = dv
        dk_ref[part] = dk
        for h, z in zip(heads, backs):
            rows = pl.ds(pl.multiple_of(h * SIZE, SIZE), SIZE)
            dqt_ref[rows, 0:n] = nn(turned_ref[rows, 0:n], z)
        return carry

    if group == HEADS:
        heads_of(0, 0)
    else:
        lax.fori_loop(0, HEADS // group, heads_of, 0)
    if n < full:
        dq_ref[whole_part] = jnp.zeros((full, HALF), F32)
    dq_ref[part] = dqt_ref[:, 0:n].T * SCALE


def prepare_back(mask, stripes, across, lanes, kern_ref, saved, up_ref, acc, key_ref, query_ref, turned_ref, dv_ref):
    q_ref, k_ref, v_ref = saved
    grid = ACROSS_GRID if across else DOWN_GRID
    key_ref[...] = valid_keys(k_ref[...], mask, stripes)
    query_ref[...] = split_queries(q_ref[...])
    turned = (k_ref[...].astype(F32) * mask).astype(BF16).T
    size = PIXELS // stripes
    for u in range(stripes):
        turned_ref[u] = turned[:, size * u : size * u + size]
    masked = v_ref[...].astype(F32) * mask
    grad = up_ref[...].astype(F32)
    back, kernel_rows, bias_row = position_back(grad.reshape(grid), masked.reshape(grid), kern_ref, lanes, across)
    dv_ref[...] = back.reshape(PIXELS, HALF)
    acc[VEC + 4 : VEC + 14, lanes] += jnp.concatenate([bias_row] + kernel_rows, axis=0)


def finish_back(x_ref, mask, lanes, weight_ref, gain_ref, shift_ref, acc, dq_ref, dk_ref, dv_ref):
    triple = jnp.concatenate([dq_ref[...], dk_ref[...] * (mask * SCALE), dv_ref[...] * mask], axis=1).astype(BF16)
    hat, rstd = normalize(x_ref[...].reshape(PIXELS, DIM).astype(F32))
    normed = (hat * gain_ref[...] + shift_ref[...]).astype(BF16)
    grads = tn(normed, triple)
    for k in range(3):
        acc[0:DIM, DIM * k + lanes.start : DIM * k + lanes.stop] += grads[:, HALF * k : HALF * k + HALF]
    d_normed = nt(triple, weight_ref[...])
    sums = col_sum(triple.astype(F32))
    acc[VEC : VEC + 1, 0:DIM] += col_sum(d_normed * hat)
    acc[VEC + 1 : VEC + 2, 0:DIM] += col_sum(d_normed)
    acc[VEC + 2 : VEC + 3, lanes] += sums[:, 0:HALF]
    acc[VEC + 3 : VEC + 4, lanes] += sums[:, 2 * HALF :]
    return norm_back(d_normed * gain_ref[...], hat, rstd).astype(BF16).reshape(4, PIX, DIM)


def backward_down_kernel(count, first, begin, meta_ref, xd0, xd1, xd2, xd3, dd0, dd1, dd2, dd3,
                         q_in, k_in, v_in, at_in, lse_in, weight_ref, gain_ref, shift_ref, kern_ref,
                         *rest):
    if not begin:
        start, *rest = rest
        *rest, early, sem = rest
    (pd0, pd1, pd2, pd3, acc,
                         x_ref, up_ref, key_ref, query_ref, turned_ref, dq_ref, dk_ref, dv_ref, part_ref,
                         delta_ref, dqt_ref) = rest
    meta = Meta(meta_ref, count)
    step = pl.program_id(0)
    i = first + step
    r, c = meta.row(), meta.col()
    height, width = meta.height(i), meta.width(i)

    @pl.when(step == 0)
    def _():
        if not begin:
            fetch(start, early, sem).start()
        acc[...] = jnp.zeros_like(acc)

    stripe = 4 * c + r
    live = (meta.keep(i) > 0) & (STRIPE * stripe < width)

    @pl.when(live)
    def _():
        mask = down_mask(height, width, stripe).reshape(PIXELS, HALF)
        lanes = slice(HALF, DIM)
        from_rows((xd0, xd1, xd2, xd3), r, x_ref)
        for k, ref in enumerate((dd0, dd1, dd2, dd3)):
            up_ref[pl.ds(pl.multiple_of(lax.rem(r + 4 - k, 4) * PIX, PIX), PIX)] = ref[0]
        prepare_back(mask, 1, False, lanes, kern_ref, (q_in.at[0], k_in.at[0], v_in.at[0]), up_ref, acc,
                     key_ref, query_ref, turned_ref, dv_ref)

        def size(n):
            attend_back(key_ref, query_ref, q_in.at[0], v_in.at[0], turned_ref.at[0], up_ref, at_in.at[0], lse_in.at[0],
                        0, delta_ref, dqt_ref, dq_ref, dk_ref, dv_ref, PIXELS, DOWN_BACK_GROUP, n)

        by_size(down_used(height), DOWN_SIZES, size)
        part_ref[...] = finish_back(x_ref, mask, lanes, weight_ref, gain_ref, shift_ref, acc, dq_ref, dk_ref, dv_ref)
        to_rows((pd0, pd1, pd2, pd3), r, part_ref)

    @pl.when(jnp.logical_not(live))
    def _():
        for ref in (pd0, pd1, pd2, pd3):
            ref[...] = jnp.zeros_like(ref)

    if not begin:

        @pl.when(step == pl.num_programs(0) - 1)
        def _():
            fetch(start, early, sem).wait()
            acc[...] += early[...]


def backward_across_kernel(count, first, begin, last, meta_ref, xa_keep, xa_recv, da_keep, da_recv,
                           q_in, k_in, v_in, at_in, lse_in, weight_ref, gain_ref, shift_ref, kern_ref,
                           *rest):
    if not begin:
        start, *rest = rest
        *rest, early, sem = rest
    if last:
        extra, *rest = rest
    (pa_keep, pa_send, acc_out,
                           acc, x_ref, up_ref, key_ref, query_ref, turned_ref, dq_ref, dk_ref, dv_ref, part_ref,
                           delta_ref, dqt_ref) = rest
    meta = Meta(meta_ref, count)
    step = pl.program_id(0)
    i = first + step
    r, c = meta.row(), meta.col()
    height, width = meta.height(i), meta.width(i)

    @pl.when(step == 0)
    def _():
        if not begin:
            fetch(start, early, sem).start()
        acc[...] = jnp.zeros_like(acc)

    stripe = 4 * r + pair_start(c)
    live = (meta.keep(i) > 0) & (STRIPE * stripe < height)

    @pl.when(live)
    def _():
        mask = across_mask(height, width, stripe).reshape(PIXELS, HALF)
        lanes = slice(0, HALF)
        for u in range(2):
            for xs, ds, side in ((xa_keep, da_keep, c), (xa_recv, da_recv, 1 - c)):
                x_ref[2 * u + side] = xs[0, u]
                up_ref[pl.ds(pl.multiple_of((2 * u + side) * PIX, PIX), PIX)] = ds[0, u]
        prepare_back(mask, 2, True, lanes, kern_ref, (q_in.at[0], k_in.at[0], v_in.at[0]), up_ref, acc,
                     key_ref, query_ref, turned_ref, dv_ref)
        half = PIXELS // 2
        dk_ref[half:] = jnp.zeros((half, HALF), F32)
        dq_ref[half:] = jnp.zeros((half, HALF), F32)

        def stripe_of(u, carry):
            def size(n):
                base = pl.multiple_of(u * half, half)
                attend_back(key_ref, query_ref, q_in.at[0], v_in.at[0], turned_ref.at[u], up_ref,
                            at_in.at[0, u], lse_in.at[0, u], base, delta_ref, dqt_ref, dq_ref, dk_ref, dv_ref,
                            half, HEADS, n)

            by_size(across_used(width), ACROSS_SIZES, size)
            return carry

        lax.fori_loop(0, live_stripes(height, stripe), stripe_of, 0)
        part_ref[...] = finish_back(x_ref, mask, lanes, weight_ref, gain_ref, shift_ref, acc, dq_ref, dk_ref, dv_ref)
        for u in range(2):
            pa_keep[0, u] = part_ref[2 * u + c]
            pa_send[0, u] = part_ref[2 * u + 1 - c]

    @pl.when(jnp.logical_not(live))
    def _():
        pa_keep[...] = jnp.zeros_like(pa_keep)
        pa_send[...] = jnp.zeros_like(pa_send)

    @pl.when(step == pl.num_programs(0) - 1)
    def _():
        if not begin:
            fetch(start, early, sem).wait()
            acc[...] += early[...]
        if last:
            acc_out[:, 0 : 3 * DIM] = acc[0:DIM].astype(BF16)
            vectors = []
            for source, count_rows in ((acc.at[VEC:, 0:DIM], 16), (extra, 8)):
                for k in range(count_rows):
                    vectors += [source[k : k + 1, 0:HALF], source[k : k + 1, HALF:DIM]]
            vectors.append(jnp.zeros((DIM - 48, HALF), F32))
            acc_out[:, 3 * DIM :] = jnp.concatenate(vectors, axis=0).astype(BF16)
        else:
            acc_out[...] = acc[...]


def finish_kernel(count, first, meta_ref, dm_ref, pd0, pd1, pd2, pd3, pa_keep, pa_recv, out_ref, total, wide):
    meta = Meta(meta_ref, count)
    r, c = meta.row(), meta.col()
    total[...] = dm_ref[0].astype(F32).reshape(4, ROWS, SLOT, DIM)
    for k, ref in enumerate((pd0, pd1, pd2, pd3)):
        total[lax.rem(r + 4 - k, 4)] += ref[0].astype(F32).reshape(ROWS, SLOT, DIM)
    for where, ref in own_stripes(pa_keep, pa_recv, c):
        total[:, where] += ref[...].astype(F32).reshape(4, STRIPE, SLOT, DIM)
    out_ref[0] = merge_cols(total, wide).astype(BF16)


def whole(shape):
    zeros = (0,) * len(shape)
    return pl.BlockSpec(shape, lambda i, *unused: zeros)


def per_image(shape, first=0):
    zeros = (0,) * len(shape)
    return pl.BlockSpec((1,) + shape, lambda i, *unused: (first + i,) + zeros)


def call(body, name, batch, scalars, inputs, outputs, scratch, micros, held=None, waits=()):
    in_specs = [spec for spec, unused in inputs]
    out_specs = [spec for spec, unused in outputs]
    moved = sum(value.size * value.dtype.itemsize for unused, value in inputs)
    aliases = {}
    held = held or {}
    inner, skipped, extra = body, len(scalars) + len(inputs), len(held) + len(waits)

    def body(*refs):
        inner(*refs[:skipped], *refs[skipped + extra :])

    for k, place in enumerate(held):
        aliases[skipped + k] = place
    in_specs = in_specs + [pl.BlockSpec(memory_space=pl.ANY)] * extra
    inputs = inputs + [(None, value) for value in list(held.values()) + list(waits)]
    return list(pl.pallas_call(
        body,
        out_shape=[shape for unused, shape in outputs],
        grid_spec=pltpu.PrefetchScalarGridSpec(
            num_scalar_prefetch=len(scalars),
            grid=(batch,),
            in_specs=in_specs,
            out_specs=out_specs,
            scratch_shapes=scratch,
        ),
        compiler_params=pltpu.CompilerParams(
            dimension_semantics=("arbitrary",), vmem_limit_bytes=VMEM_LIMIT
        ),
        input_output_aliases=aliases,
        cost_estimate=pl.CostEstimate(flops=micros * 10**9, bytes_accessed=moved, transcendentals=0),
        name=name,
    )(*scalars, *[value for unused, value in inputs]))


def struct(shape, dtype):
    return jax.ShapeDtypeStruct(shape, dtype)


def images_out(batch, shape, dtype):
    return per_image(shape), struct((batch,) + shape, dtype)


def whole_out(shape, dtype=F32):
    return whole(shape), struct(shape, dtype)


def row_exchange(parts):
    size = lax.axis_size("row")
    return [parts[0]] + [
        lax.ppermute(parts[k], "row", [(q, (q + k) % size) for q in range(size)]) for k in range(1, size)
    ]


def col_exchange(keep, send):
    return [keep, lax.ppermute(send, "col", [(0, 1), (1, 0)])]


def together(*values):
    return lax.optimization_barrier(values)


def bits_of(size):
    found = []
    bit = 1
    while bit < size:
        found.append(bit)
        bit *= 2
    return found


def kept_total(flags):
    total = flags
    size = lax.axis_size("batch")
    for bit in bits_of(size):
        total = total + lax.ppermute(total, "batch", [(q, q ^ bit) for q in range(size)])
    return total


ALL = ("batch", "row", "col")
NEAR = ("batch", "col")


def send_shares(rows, axes):
    places = lax.axis_size(axes)
    sent = rows.astype(BF16).reshape((places, -1) + rows.shape[1:])
    return lax.all_to_all(sent, axes, 0, 0)


def sum_shares(received):
    return jnp.sum(received.astype(F32), axis=0).astype(BF16)


def gather_shares(share, axes):
    sent = jnp.broadcast_to(share[None], (lax.axis_size(axes),) + share.shape)
    return lax.all_to_all(sent, axes, 0, 0).reshape((-1,) + share.shape[1:])


def send_rows(share):
    size = lax.axis_size("row")
    return [lax.ppermute(share, "row", [(q, (q + k) % size) for q in range(size)]) for k in range(1, size)]


def per_device(batch, devices, tokens, heights, widths, keep_flags, out_grad, first_gain, first_shift, triple_weight,
               query_value_bias, position_kernel, position_bias, mixing_weight, mixing_bias, second_gain, second_shift,
               expand_weight, expand_bias, reduce_weight, reduce_bias):
    count = tokens.shape[0]
    chunks = count // batch
    r, c = lax.axis_index("row"), lax.axis_index("col")
    meta = jnp.concatenate(
        [heights, widths, keep_flags[:, 0], keep_flags[:, 1], jnp.stack([r, c]).astype(jnp.int32)]
    )
    kept = kept_total(jnp.sum(keep_flags.astype(F32), axis=0))
    share = kept / (count * lax.axis_size("batch"))
    factors = (keep_flags.astype(F32) / share).reshape(-1)

    def branch_weight(lo):
        return jnp.concatenate([triple_weight[:, DIM * k + lo : DIM * k + lo + HALF] for k in range(3)], axis=1)

    wa, wd = branch_weight(0), branch_weight(HALF)
    zeros = jnp.zeros((HALF,), F32)
    ba = jnp.concatenate([query_value_bias[0, :HALF], zeros, query_value_bias[1, :HALF]])[None]
    bd = jnp.concatenate([query_value_bias[0, HALF:], zeros, query_value_bias[1, HALF:]])[None]
    gain1, shift1 = first_gain[None], first_shift[None]
    gain2, shift2 = second_gain[None], second_shift[None]
    kern = jnp.pad(position_kernel.reshape(9, DIM), ((0, 7), (0, 0)))
    pos = position_bias[None]

    def full(value):
        return whole(value.shape), value

    def chunk_in(value):
        return per_image(value.shape[1:]), value

    def grid_out(first):
        return per_image((ROWS, ROWS, DIM), first), struct((count, ROWS, ROWS, DIM), BF16)

    pix = (PIX, DIM)
    half = (PIX, HALF)
    pair = (2, PIX, DIM)
    pair_half = (2, PIX, HALF)

    def all_images(shape, dtype, first):
        return per_image(shape, first), struct((count,) + shape, dtype)

    blocks = pltpu.VMEM((4, PIX, DIM), BF16)
    low = pltpu.VMEM((PIXELS, HALF), BF16)
    high = pltpu.VMEM((PIXELS, HALF), F32)
    pairs = pltpu.VMEM((PIXELS, DIM), BF16)
    low_blocks = pltpu.VMEM((4, PIX, HALF), BF16)
    parts_high = pltpu.VMEM((4, ROWS, SLOT, DIM), F32)
    wide = pltpu.VMEM((ROWS, 32, DIM), F32)

    def prepare(k, waits):
        first = k * batch
        outs = call(
            functools.partial(prep_kernel, count, first), "prep", batch, [meta],
            [(per_image((ROWS, ROWS, DIM), first), tokens)],
            [images_out(batch, pix, BF16)] * 4 + [images_out(batch, pair, BF16)] * 2,
            [wide, parts_high], 2 * batch, {}, waits)
        return outs[0:4], outs[4:6]

    flat = (PIXELS, HALF)

    def across_forward(k, taken, held, waits):
        first = k * batch
        shapes = [(pair_half, BF16)] * 2 + [(flat, BF16)] * 3 + [((2, HALF, PIXELS // 2), BF16), ((2, 8, PIXELS // 2), F32)]
        return call(
            functools.partial(forward_across_kernel, count, first), "across_forward", batch, [meta],
            [chunk_in(v) for v in taken] + [full(v) for v in (wa, ba, gain1, shift1, kern, pos)],
            [all_images(shape, dtype, first) for shape, dtype in shapes],
            [blocks, low, pairs, pltpu.VMEM((2, HEADS, SIZE + 16, PIXELS // 2), BF16), high, low_blocks,
             pltpu.VMEM((HALF, PIXELS // 2), F32)],
            5 * batch, dict(enumerate(held)), waits)

    def down_forward(k, taken, waits):
        first = k * batch
        out = images_out(batch, flat, BF16)
        outs = call(
            functools.partial(forward_down_kernel, count, first), "down_forward", batch, [meta],
            [chunk_in(v) for v in taken] + [full(v) for v in (wd, bd, gain1, shift1, kern, pos)],
            [images_out(batch, half, BF16)] * 4
            + [out, out, out, images_out(batch, (HALF, PIXELS), BF16), images_out(batch, (8, PIXELS), F32)],
            [blocks, low, pairs, pltpu.VMEM((1, HEADS, SIZE + 16, PIXELS), BF16), high, low_blocks,
             pltpu.VMEM((HALF, PIXELS), F32)],
            6 * batch, {}, waits)
        return outs[0:4], outs[4:]

    own0, sent0 = prepare(0, [])
    col0 = col_exchange(*sent0)
    row0 = row_exchange(own0)
    own1, sent1 = prepare(1, [factors])
    across0 = across_forward(0, col0, [], own1[0:1])
    own1, sent1, across_done = together(own1, sent1, across0[0])
    across0[0] = across_done
    col1 = col_exchange(*sent1)
    row1 = row_exchange(own1)
    joined0, saved0 = down_forward(0, row0, across0[0:1])
    across1 = across_forward(1, col1, across0, saved0[0:1])
    joined_across = col_exchange(*across1[0:2])
    joined1, saved1 = down_forward(1, row1, across1[2:3])
    row_joined0 = row_exchange(joined0)
    row_joined1 = row_exchange(joined1)

    def middle(k, own, row_joined, held, sums, waits):
        first = k * batch
        acc_shape = (DIM, 2 * HIDDEN + DIM)
        return call(
            functools.partial(middle_kernel, count, first), "middle", batch, [meta, factors],
            [chunk_in(v) for v in own + row_joined]
            + [(per_image(v.shape[1:], first), v) for v in joined_across + [out_grad]]
            + [full(v) for v in (mixing_weight, mixing_bias[None], gain2, shift2, expand_weight, expand_bias[None],
                                 reduce_weight, reduce_bias[None])]
            + ([(pl.BlockSpec(memory_space=pl.ANY), sums[0]), full(sums[1])] if sums else []),
            [all_images((ROWS, ROWS, DIM), BF16, first), all_images((4,) + pix, BF16, first)]
            + [images_out(batch, half, BF16)] * 4 + [images_out(batch, pair_half, BF16)] * 2
            + [whole_out(acc_shape, BF16), whole_out((8, DIM))],
            [pltpu.VMEM(acc_shape, F32), pltpu.VMEM((4,) + pix, BF16), parts_high,
             pltpu.VMEM((4, ROWS, SLOT, HALF), F32), pltpu.VMEM((4,) + pix, BF16), parts_high, parts_high, wide]
            + ([pltpu.VMEM(acc_shape, BF16), pltpu.SemaphoreType.DMA] if sums else []),
            8 * batch, held, waits)

    mid0 = middle(0, own0, row_joined0, {}, [], saved1[0:1])
    row_grad0 = row_exchange(mid0[2:6])
    col_grad0 = col_exchange(*mid0[6:8])
    mid1 = middle(1, own1, row_joined1, {0: mid0[0], 1: mid0[1]}, mid0[8:10], [])
    output, middles = mid1[0:2]
    feed, row_grad0, col_grad0 = together(mid1[8], row_grad0, col_grad0)
    row_grad1 = row_exchange(mid1[2:6])
    col_grad1 = col_exchange(*mid1[6:8])
    received = send_shares(feed, NEAR)

    back_scratch = [high, high, high, blocks, pltpu.VMEM((8, PIXELS), F32), pltpu.VMEM((HALF, PIXELS), F32)]
    back_shape = (VEC + 16, 3 * DIM)

    def early_scratch(sums):
        return [pltpu.VMEM(back_shape, F32), pltpu.SemaphoreType.DMA] if sums else []

    def down_backward(k, taken, row_grad, saved, sums, waits):
        first = k * batch
        outs = call(
            functools.partial(backward_down_kernel, count, first, not sums), "down_backward", batch, [meta],
            [chunk_in(v) for v in taken + row_grad + saved] + [full(v) for v in (wd, gain1, shift1, kern)]
            + [(pl.BlockSpec(memory_space=pl.ANY), v) for v in sums],
            [images_out(batch, pix, BF16)] * 4 + [whole_out(back_shape)],
            [blocks, low, low, pairs, pltpu.VMEM((1, HALF, PIXELS), BF16)] + back_scratch + early_scratch(sums),
            11 * batch, {}, waits)
        return outs[0:4], outs[4:]

    def across_backward(k, taken, col_grad, sums, waits):
        first = k * batch
        last = k == chunks - 1
        out = whole_out((DIM, PACKED), BF16) if last else whole_out(back_shape)
        outs = call(
            functools.partial(backward_across_kernel, count, first, not sums, last), "across_backward", batch, [meta],
            [chunk_in(v) for v in taken + col_grad] + [(per_image(v.shape[1:], first), v) for v in across1[2:]]
            + [full(v) for v in (wa, gain1, shift1, kern)]
            + [(pl.BlockSpec(memory_space=pl.ANY), v) for v in sums[:1]] + [full(v) for v in sums[1:]],
            [images_out(batch, pair, BF16)] * 2 + [out],
            [pltpu.VMEM(back_shape, F32), blocks, low, low, pairs, pltpu.VMEM((2, HALF, PIXELS // 2), BF16)]
            + back_scratch + early_scratch(sums), 9 * batch, {}, waits)
        return outs[0:2], outs[2]

    part0, sums = across_backward(0, col0, col_grad0, [], mid1[8:9] + row_grad0[1:])
    col_part0 = col_exchange(*part0)
    received, sums, row_grad1, col_grad1 = together(received, sums, row_grad1, col_grad1)
    share = sum_shares(received)
    others = send_rows(share)
    part0, sums = down_backward(0, row0, row_grad0, saved0, [sums], row_grad1[1:] + col_grad1[1:])
    row_part0 = row_exchange(part0)
    others, sums, col_part0 = together(others, sums, col_part0)
    feed = gather_shares(sum_shares(jnp.stack([share] + others)), NEAR)
    part1, sums = down_backward(1, row1, row_grad1, saved1, sums, col_part0[1:])
    row_part1 = row_exchange(part1)
    feed, sums = together(feed, sums)
    part1, back = across_backward(1, col1, col_grad1, sums + [mid1[9]], row_part0[1:])
    col_part1 = col_exchange(*part1)
    back, row_part1, col_part0 = together(back, row_part1, col_part0)
    received = send_shares(back, ALL)

    def finish(k, row_part, col_part, held, waits):
        first = k * batch
        return call(
            functools.partial(finish_kernel, count, first), "finish", batch, [meta],
            [(per_image(middles.shape[1:], first), middles)] + [chunk_in(v) for v in row_part + col_part],
            [grid_out(first)], [parts_high, wide], 2 * batch, held, waits)

    grad0 = finish(0, row_part0, col_part0, {}, [back])
    feed = feed.astype(F32)
    feed = [feed[:, 0:HIDDEN].T, feed[:, HIDDEN : 2 * HIDDEN], feed[:, 2 * HIDDEN :]]
    received, grad0, feed, col_part1 = together(received, grad0, feed, col_part1)
    rows = gather_shares(sum_shares(received), ALL)
    tokens_grad = finish(1, row_part1, col_part1, {0: grad0[0]}, [])[0]
    back_rows = rows.astype(F32)

    triple_weight_grad = back_rows[:, 0 : 3 * DIM]
    vectors = back_rows[0:48, 3 * DIM :].reshape(24, DIM)
    rows = vectors[16:24]
    return (
        output,
        tokens_grad,
        vectors[0],
        vectors[1],
        triple_weight_grad,
        vectors[2:4],
        vectors[5:14].reshape(3, 3, DIM),
        vectors[4],
        feed[2],
        rows[7],
        rows[5],
        rows[6],
        feed[1],
        rows[0:4].reshape(HIDDEN),
        feed[0],
        rows[4],
    )


def solution(mesh):
    spread = P("batch", "row", "col", None)
    in_specs = (spread, P("batch"), P("batch"), P("batch", None), spread) + (P(),) * 14
    out_specs = (spread, spread) + (P(),) * 14
    devices = mesh.shape["batch"] * mesh.shape["row"] * mesh.shape["col"]
    return jax.shard_map(
        functools.partial(per_device, 2, devices),
        mesh=mesh, in_specs=in_specs, out_specs=out_specs, check_vma=False)
```

```python
import functools

import jax
import jax.numpy as jnp
from jax import lax
from jax.experimental import pallas as pl
from jax.experimental.pallas import tpu as pltpu
from jax.sharding import PartitionSpec as P

DIM = 256
HALF = 128
HEADS = 4
SIZE = 32
STRIPE = 7
ROWS = 28
SLOT = 8
PIX = ROWS * SLOT
HIDDEN = 1024
VEC = DIM
PACKED = 3 * DIM + HALF
F32 = jnp.float32
BF16 = jnp.bfloat16
LOG2E = 1.4426950408889634
SCALE = SIZE**-0.5
EPS = 1e-05
GELU_C = 0.7978845608028654
GELU_A = 0.044715
VMEM_LIMIT = 56 * 1024 * 1024


def nn(a, b):
    return lax.dot_general(a, b, (((1,), (0,)), ((), ())), preferred_element_type=F32)


def nt(a, b):
    return lax.dot_general(a, b, (((1,), (1,)), ((), ())), preferred_element_type=F32)


def tn(a, b):
    return lax.dot_general(a, b, (((0,), (0,)), ((), ())), preferred_element_type=F32)


def col_sum(v):
    return jnp.sum(v, axis=0, keepdims=True)


def normalize(source):
    average = jnp.mean(source, axis=-1, keepdims=True)
    centered = source - average
    spread = jnp.mean(centered * centered, axis=-1, keepdims=True)
    rstd = lax.rsqrt(spread + EPS)
    return centered * rstd, rstd


def norm_back(grad_hat, hat, rstd):
    return rstd * (
        grad_hat
        - jnp.mean(grad_hat, axis=-1, keepdims=True)
        - hat * jnp.mean(grad_hat * hat, axis=-1, keepdims=True)
    )


def head_lanes(shape):
    return lax.broadcasted_iota(jnp.int32, shape, len(shape) - 1) // SIZE


def split_cols(source, wide, parts):
    wide[:, 0:ROWS, :] = source.astype(F32)
    slot = lax.broadcasted_iota(jnp.int32, (ROWS, SLOT, DIM), 1)
    for s in range(4):
        parts[s] = jnp.where(slot < STRIPE, wide[:, STRIPE * s : STRIPE * s + SLOT, :], 0.0)


def merge_cols(parts, wide):
    for s in range(4):
        wide[:, STRIPE * s : STRIPE * s + SLOT, :] = parts[s]
    return wide[:, 0:ROWS, :]


class Meta:
    def __init__(self, ref, count):
        self.ref = ref
        self.count = count

    def height(self, i):
        return self.ref[i]

    def width(self, i):
        return self.ref[self.count + i]

    def keep(self, i):
        return self.ref[2 * self.count + i]

    def feed(self, i):
        return self.ref[3 * self.count + i]

    def row(self):
        return self.ref[4 * self.count]

    def col(self):
        return self.ref[4 * self.count + 1]


def pair_start(owner):
    return 2 * (1 - owner)


def from_rows(refs, r, out):
    for k, ref in enumerate(refs):
        out[lax.rem(r + 4 - k, 4)] = ref[0]


def to_rows(refs, r, source):
    for k, ref in enumerate(refs):
        ref[0] = source[lax.rem(r + k, 4)]


def own_stripes(keep_ref, other_ref, c):
    for ref, owner in ((keep_ref, c), (other_ref, 1 - c)):
        for u in range(2):
            yield pl.ds(STRIPE * (pair_start(owner) + u), STRIPE), ref.at[0, u]


def fetch(source, target, sem):
    return pltpu.make_async_copy(source, target, sem)


def prep_kernel(count, first, meta_ref, tok_ref, d0, d1, d2, d3, keep_ref, send_ref, wide, parts):
    meta = Meta(meta_ref, count)
    split_cols(tok_ref[0], wide, parts)
    r, c = meta.row(), meta.col()
    for k, ref in enumerate((d0, d1, d2, d3)):
        ref[0] = parts[lax.rem(r + k, 4)].reshape(PIX, DIM).astype(BF16)
    for where, ref in own_stripes(keep_ref, send_ref, c):
        ref[...] = parts[:, where].reshape(PIX, DIM).astype(BF16)


def down_mask(height, width, stripe):
    shape = (4 * ROWS, SLOT, HALF)
    row = lax.broadcasted_iota(jnp.int32, shape, 0)
    j = lax.broadcasted_iota(jnp.int32, shape, 1)
    limit = jnp.minimum(STRIPE, width - STRIPE * stripe)
    return jnp.where((row < height) & (j < limit), 1.0, 0.0)


def across_mask(height, width, stripe):
    shape = (2, 8, STRIPE, SLOT, HALF)
    u = lax.broadcasted_iota(jnp.int32, shape, 0)
    b = lax.broadcasted_iota(jnp.int32, shape, 1)
    row = lax.broadcasted_iota(jnp.int32, shape, 2)
    j = lax.broadcasted_iota(jnp.int32, shape, 3)
    good = (STRIPE * u + row < height - STRIPE * stripe) & (j < STRIPE) & (b * STRIPE + j < width)
    return jnp.where(good, 1.0, 0.0)


def down_flags(height, width, stripe):
    at = lax.broadcasted_iota(jnp.int32, (16, PIXELS), 1)
    limit = jnp.minimum(STRIPE, width - STRIPE * stripe)
    good = (at < SLOT * height) & (lax.rem(at, SLOT) < limit)
    return jnp.where(good, 1.0, 0.0).astype(BF16)


def across_flags(height, width, stripe):
    at = lax.broadcasted_iota(jnp.int32, (16, PIXELS), 1)
    size = STRIPE * SLOT
    u = jnp.where(at < PIXELS // 2, 0, 1)
    b = jnp.zeros_like(at)
    for k in range(1, 16):
        b = jnp.where(at >= size * k, k, b)
    rest = at - size * b
    j = lax.rem(rest, SLOT)
    row = (rest - j) // SLOT + STRIPE * u
    col = STRIPE * (b - SLOT * u) + j
    good = (row < height - STRIPE * stripe) & (j < STRIPE) & (col < width)
    return jnp.where(good, 1.0, 0.0).astype(BF16)


def moved_rows(v, axis, step):
    if step == 0:
        return v
    size = v.shape[axis]
    zero_shape = v.shape[:axis] + (1,) + v.shape[axis + 1 :]
    zero = jnp.zeros(zero_shape, v.dtype)
    if step > 0:
        return jnp.concatenate([lax.slice_in_dim(v, 1, size, axis=axis), zero], axis=axis)
    return jnp.concatenate([zero, lax.slice_in_dim(v, 0, size - 1, axis=axis)], axis=axis)


def roll8(v, shift):
    shape = v.shape
    flat = v.reshape(-1, SLOT, HALF)
    return pltpu.roll(flat, shift, 1).reshape(shape)


def moved_cols_down(v, step):
    if step == 0:
        return v
    return roll8(v, 1 if step < 0 else SLOT - 1)


def moved_cols_across(v, step):
    if step == 0:
        return v
    slot = lax.broadcasted_iota(jnp.int32, v.shape, 3)
    if step < 0:
        return jnp.where(slot == 0, moved_rows(roll8(v, 2), 1, -1), roll8(v, 1))
    return jnp.where(slot == STRIPE - 1, moved_rows(roll8(v, SLOT - 2), 1, 1), roll8(v, SLOT - 1))


def taps(v, across):
    moved_cols = moved_cols_across if across else moved_cols_down
    row_axis = 2 if across else 0
    for b in range(3):
        side = moved_cols(v, b - 1)
        for a in range(3):
            yield a, b, moved_rows(side, row_axis, a - 1)


def position_term(v, kern_ref, bias_ref, lanes, across):
    total = bias_ref[0:1, lanes]
    for a, b, moved in taps(v, across):
        total = total + moved * kern_ref[3 * a + b : 3 * a + b + 1, lanes]
    return total


def position_back(grad, v, kern_ref, lanes, across):
    total = 0.0
    for a, b, moved in taps(grad, across):
        k = 3 * (2 - a) + (2 - b)
        total = total + moved * kern_ref[k : k + 1, lanes]
    kernel_grads = []
    flat = grad.reshape(-1, HALF)
    found = {}
    for a, b, moved in taps(v, across):
        found[3 * a + b] = col_sum(flat * moved.reshape(-1, HALF))
    for k in range(9):
        kernel_grads.append(found[k])
    return total, kernel_grads, col_sum(flat)


DOWN_GRID = (4 * ROWS, SLOT, HALF)
ACROSS_GRID = (2, 8, STRIPE, SLOT, HALF)
DOWN_SIZES = (640, 768, 896)
ACROSS_SIZES = (336, 448)
DOWN_GROUP = 4
MIDDLE_GROUP = 4
HIDDEN_TILE = 512
DOWN_BACK_GROUP = 2
PIXELS = 4 * PIX


def by_size(used, sizes, body):
    below = None
    for n in sizes:
        fits = used <= n
        if n == sizes[-1]:
            fits = True if below is None else used > below
        elif below is not None:
            fits = fits & (used > below)
        pl.when(fits)(functools.partial(body, n))
        below = n


def project(x_ref, weight_ref, bias_ref, gain_ref, shift_ref):
    hat, unused = normalize(x_ref[...].reshape(PIXELS, DIM).astype(F32))
    normed = (hat * gain_ref[...] + shift_ref[...]).astype(BF16)
    return (nn(normed, weight_ref[...]) + bias_ref[...]).astype(BF16)


def split_queries(query):
    scaled = query.astype(F32) * (SCALE * LOG2E)
    high = scaled.astype(BF16)
    low = (scaled - high.astype(F32)).astype(BF16)
    return jnp.concatenate([high, low], axis=1)


def valid_keys(keys, mask, stripes):
    size = PIXELS // stripes
    keys = keys.astype(F32)
    fixed = [
        jnp.where(
            mask[size * u : size * u + size] > 0.0, keys[size * u : size * u + size], keys[size * u : size * u + 1]
        )
        for u in range(stripes)
    ]
    return jnp.concatenate(fixed, axis=0).astype(BF16)


def only_head(value, h):
    lane = lax.broadcasted_iota(jnp.int32, value.shape, 1)
    return jnp.where(lax.rem(lane, HALF) // SIZE == h, value, jnp.zeros_like(value))


def attend(key_ref, query_ref, turned_ref, base, at_out, lse_out, a_ref, turned_a, full, group, n):
    part = pl.ds(base, n)
    whole_part = pl.ds(base, full)

    def heads_of(t, carry):
        heads = [t * group + j for j in range(group)]
        keys = key_ref[part]
        keys = jnp.concatenate([keys, keys], axis=1)
        queries = query_ref[part]
        scores = [nt(keys, only_head(queries, h)) for h in heads]
        tops = [jnp.max(s, axis=0, keepdims=True) for s in scores]
        weights = [jnp.exp2(s - top).astype(BF16) for s, top in zip(scores, tops)]
        outs = [nn(turned_ref[h, :, 0:n], w) for h, w in zip(heads, weights)]
        for h, out, top in zip(heads, outs, tops):
            total = out[SIZE : SIZE + 1]
            turned_a[pl.ds(pl.multiple_of(h * SIZE, SIZE), SIZE), 0:n] = out[0:SIZE] / total
            lse_out[pl.ds(h, 1), 0:n] = top + jnp.log2(total)
        return carry

    if group == HEADS:
        heads_of(0, 0)
    else:
        lax.fori_loop(0, HEADS // group, heads_of, 0)
    if n < full:
        a_ref[whole_part] = jnp.zeros((full, HALF), F32)
    at_out[:, 0:n] = turned_a[:, 0:n].astype(BF16)
    a_ref[part] = turned_a[:, 0:n].T


def prepare_forward(x_ref, mask, flags, stripes, weight_ref, bias_ref, gain_ref, shift_ref, saved, key_ref, query_ref, turned_ref):
    triple = project(x_ref, weight_ref, bias_ref, gain_ref, shift_ref)
    for k in range(3):
        saved[k] = triple[:, HALF * k : HALF * k + HALF]
    query_ref[...] = split_queries(triple[:, 0:HALF])
    key_ref[...] = valid_keys(triple[:, HALF : 2 * HALF], mask, stripes)
    masked = triple[:, 2 * HALF :].astype(F32) * mask
    turned = masked.astype(BF16).T
    size = PIXELS // stripes
    for u in range(stripes):
        part = slice(size * u, size * u + size)
        for h in range(HEADS):
            turned_ref[u, h, 0:SIZE] = turned[SIZE * h : SIZE * h + SIZE, part]
            turned_ref[u, h, SIZE:] = flags[:, part]
    return masked


def down_used(height):
    return SLOT * height


def live_stripes(height, stripe):
    return jnp.where(STRIPE * (stripe + 1) < height, 2, 1)


def across_used(width):
    return STRIPE * SLOT * ((width + STRIPE - 1) // STRIPE)


def forward_down_kernel(count, first, meta_ref, xd0, xd1, xd2, xd3, weight_ref, bias_ref, gain_ref, shift_ref,
                        kern_ref, pos_ref, jd0, jd1, jd2, jd3, q_out, k_out, v_out, at_out, lse_out,
                        x_ref, key_ref, query_ref, turned_ref, a_ref, j_ref, turned_a, saved, sems):
    meta = Meta(meta_ref, count)
    place = pl.program_id(0)
    i = first + place
    r, c = meta.row(), meta.col()
    height, width = meta.height(i), meta.width(i)
    stripe = 4 * c + r
    live = (meta.keep(i) > 0) & (STRIPE * stripe < width)

    @pl.when(live)
    def _():
        from_rows((xd0, xd1, xd2, xd3), r, x_ref)
        mask = down_mask(height, width, stripe)
        masked = prepare_forward(
            x_ref, mask.reshape(PIXELS, HALF), down_flags(height, width, stripe), 1, weight_ref, bias_ref, gain_ref, shift_ref,
            saved, key_ref, query_ref, turned_ref)
        copies = [fetch(saved.at[k], out.at[place], sems.at[k]) for k, out in enumerate((q_out, k_out, v_out))]
        for copy in copies:
            copy.start()

        def size(n):
            attend(key_ref, query_ref, turned_ref.at[0], 0, at_out.at[0], lse_out.at[0], a_ref, turned_a, PIXELS, DOWN_GROUP, n)

        by_size(down_used(height), DOWN_SIZES, size)
        term = position_term(masked.reshape(DOWN_GRID), kern_ref, pos_ref, slice(HALF, DIM), False)
        total = a_ref[...] + term.reshape(PIXELS, HALF)
        j_ref[...] = total.astype(BF16).reshape(4, PIX, HALF)
        to_rows((jd0, jd1, jd2, jd3), r, j_ref)
        for copy in copies:
            copy.wait()

    @pl.when(jnp.logical_not(live))
    def _():
        for ref in (jd0, jd1, jd2, jd3):
            ref[...] = jnp.zeros_like(ref)


def forward_across_kernel(count, first, meta_ref, xa_keep, xa_recv, weight_ref, bias_ref, gain_ref, shift_ref,
                          kern_ref, pos_ref, ja_keep, ja_send, q_out, k_out, v_out, at_out, lse_out,
                          x_ref, key_ref, query_ref, turned_ref, a_ref, j_ref, turned_a, saved, sems):
    meta = Meta(meta_ref, count)
    i = first + pl.program_id(0)
    place = i
    r, c = meta.row(), meta.col()
    height, width = meta.height(i), meta.width(i)
    stripe = 4 * r + pair_start(c)
    live = (meta.keep(i) > 0) & (STRIPE * stripe < height)

    @pl.when(live)
    def _():
        mask = across_mask(height, width, stripe)
        for u in range(2):
            x_ref[2 * u + c] = xa_keep[0, u]
            x_ref[2 * u + 1 - c] = xa_recv[0, u]
        masked = prepare_forward(
            x_ref, mask.reshape(PIXELS, HALF), across_flags(height, width, stripe), 2, weight_ref, bias_ref, gain_ref, shift_ref,
            saved, key_ref, query_ref, turned_ref)
        copies = [fetch(saved.at[k], out.at[place], sems.at[k]) for k, out in enumerate((q_out, k_out, v_out))]
        for copy in copies:
            copy.start()
        half = PIXELS // 2
        a_ref[half:] = jnp.zeros((half, HALF), F32)

        def stripe_of(u, carry):
            def size(n):
                base = pl.multiple_of(u * half, half)
                attend(key_ref, query_ref, turned_ref.at[u], base, at_out.at[0, u], lse_out.at[0, u], a_ref, turned_a, half, HEADS, n)

            by_size(across_used(width), ACROSS_SIZES, size)
            return carry

        lax.fori_loop(0, live_stripes(height, stripe), stripe_of, 0)
        term = position_term(masked.reshape(ACROSS_GRID), kern_ref, pos_ref, slice(0, HALF), True)
        j_ref[...] = (a_ref[...] + term.reshape(PIXELS, HALF)).astype(BF16).reshape(4, PIX, HALF)
        for u in range(2):
            ja_keep[0, u] = j_ref[2 * u + c]
            ja_send[0, u] = j_ref[2 * u + 1 - c]
        for copy in copies:
            copy.wait()

    @pl.when(jnp.logical_not(live))
    def _():
        ja_keep[...] = jnp.zeros_like(ja_keep)
        ja_send[...] = jnp.zeros_like(ja_send)


def pixel_mask(height, width, first_block, blocks, r, c):
    shape = (blocks, ROWS, SLOT, HALF)
    s = lax.broadcasted_iota(jnp.int32, shape, 0) + first_block
    row = lax.broadcasted_iota(jnp.int32, shape, 1)
    j = lax.broadcasted_iota(jnp.int32, shape, 2)
    good = (row < height - ROWS * r) & (j < STRIPE) & (s * STRIPE + j < width - ROWS * c)
    mask = jnp.where(good, 1.0, 0.0).reshape(blocks * PIX, HALF)
    return jnp.concatenate([mask, mask], axis=1)


def gelu_pair(pre, d_act):
    square = pre * pre
    bend = jnp.tanh(pre * (GELU_C + (GELU_C * GELU_A) * square))
    half_one = 0.5 + 0.5 * bend
    slope = half_one + (0.5 * pre) * (1.0 - bend * bend) * (GELU_C + (3.0 * GELU_C * GELU_A) * square)
    return (pre * half_one).astype(BF16), (d_act * slope).astype(BF16)


def middle_kernel(count, first, meta_ref, fact_ref, xd0, xd1, xd2, xd3, jd0, jd1, jd2, jd3, ja_keep, ja_recv, grad_ref,
                  wm_ref, bm_ref, gain_ref, shift_ref, we_ref, be_ref, wr_ref, br_ref, *rest):
    if first > 0:
        start, start_v, *rest = rest
        *rest, early, sem = rest
    (out_ref, dm_ref, dd0, dd1, dd2, dd3, da_keep, da_send, acc_out, acc_v, acc,
     x_ref, g_ref, ja_ref, j_ref, o_ref, dj_ref, wide) = rest
    meta = Meta(meta_ref, count)
    step = pl.program_id(0)
    i = first + step
    r, c = meta.row(), meta.col()
    height, width = meta.height(i), meta.width(i)
    attend_factor = fact_ref[2 * i]
    feed_factor = fact_ref[2 * i + 1]

    @pl.when(step == 0)
    def _():
        if first > 0:
            fetch(start, early, sem).start()
        acc[...] = jnp.zeros_like(acc)
        acc_v[...] = start_v[...] if first > 0 else jnp.zeros_like(acc_v)

    split_cols(grad_ref[0], wide, g_ref)
    for k, (xs, js) in enumerate(((xd0, jd0), (xd1, jd1), (xd2, jd2), (xd3, jd3))):
        x_ref[lax.rem(r + k, 4)] = xs[0]
        j_ref[lax.rem(r + 4 - k, 4), :, HALF:] = js[0]
    for where, ref in own_stripes(ja_keep, ja_recv, c):
        ja_ref[:, where] = ref[...].astype(F32).reshape(4, STRIPE, SLOT, HALF)
    j_ref[:, :, 0:HALF] = ja_ref[...].reshape(4, PIX, HALF).astype(BF16)

    group = MIDDLE_GROUP
    size = group * PIX

    def one(b, carry):
        where = pl.ds(group * b, group)
        mask = pixel_mask(height, width, group * b, group, r, c)
        scale_attend = mask * attend_factor
        scale_feed = mask * feed_factor
        x = x_ref[where].reshape(size, DIM).astype(F32)
        joined = j_ref[where].reshape(size, DIM)
        g = g_ref[where].reshape(size, DIM)
        mixed = nn(joined, wm_ref[...]) + bm_ref[...]
        middle = x + scale_attend * mixed
        hat, rstd = normalize(middle)
        normed = (hat * gain_ref[...] + shift_ref[...]).astype(BF16)
        d_reduced = (scale_feed * g).astype(BF16)
        turned_grad, turned_normed = d_reduced.T, normed.T
        tiles = HIDDEN // HIDDEN_TILE
        first_dots, hidden = {}, {}
        reduced, d_normed, sums = br_ref[...], 0.0, []
        for t in range(tiles + 2):
            if t < tiles:
                cols = slice(HIDDEN_TILE * t, HIDDEN_TILE * t + HIDDEN_TILE)
                first_dots[t] = nn(normed, we_ref[:, cols]), nt(d_reduced, wr_ref[cols])
            if 1 <= t <= tiles:
                j = t - 1
                cols = slice(HIDDEN_TILE * j, HIDDEN_TILE * j + HIDDEN_TILE)
                pre, d_act = first_dots.pop(j)
                hidden[j] = gelu_pair(pre + be_ref[:, cols], d_act)
            if t >= 2:
                j = t - 2
                cols = slice(HIDDEN_TILE * j, HIDDEN_TILE * j + HIDDEN_TILE)
                wide_cols = slice(HIDDEN + HIDDEN_TILE * j, HIDDEN + HIDDEN_TILE * j + HIDDEN_TILE)
                act, d_hidden = hidden.pop(j)
                reduced = reduced + nn(act, wr_ref[cols])
                d_normed = d_normed + nt(d_hidden, we_ref[:, cols])
                acc[:, cols] += nn(turned_grad, act)
                acc[:, wide_cols] += nn(turned_normed, d_hidden)
                sums.append(col_sum(d_hidden.astype(F32)))
        d_hidden_sum = jnp.concatenate(sums, axis=1)
        o_ref[where] = (middle + scale_feed * reduced).reshape(group, ROWS, SLOT, DIM)
        d_middle = g + norm_back(d_normed * gain_ref[...], hat, rstd)
        dm_ref[0, where] = d_middle.astype(BF16).reshape(group, PIX, DIM)
        d_mixed = (scale_attend * d_middle).astype(BF16)
        acc[:, 2 * HIDDEN :] += tn(joined, d_mixed)
        dj_ref[where] = nt(d_mixed, wm_ref[...]).reshape(group, ROWS, SLOT, DIM)
        rows = [d_hidden_sum[:, DIM * k : DIM * k + DIM] for k in range(4)]
        rows.append(col_sum(d_reduced.astype(F32)))
        rows.append(col_sum(d_normed * hat))
        rows.append(col_sum(d_normed))
        rows.append(col_sum(d_mixed.astype(F32)))
        acc_v[...] += jnp.concatenate(rows, axis=0)
        return carry

    lax.fori_loop(0, 4 // group, one, 0)

    @pl.when(step == pl.num_programs(0) - 1)
    def _():
        if first > 0:
            fetch(start, early, sem).wait()
            acc_out[...] = (acc[...] + early[...].astype(F32)).astype(BF16)
        else:
            acc_out[...] = acc[...].astype(BF16)

    out_ref[0] = merge_cols(o_ref, wide).astype(BF16)
    for k, ref in enumerate((dd0, dd1, dd2, dd3)):
        ref[0] = dj_ref[lax.rem(r + k, 4), :, :, HALF:].reshape(PIX, HALF).astype(BF16)
    for where, ref in own_stripes(da_keep, da_send, c):
        ref[...] = dj_ref[:, where, :, 0:HALF].reshape(PIX, HALF).astype(BF16)


def attend_back(key_ref, query_ref, q_ref, v_ref, turned_ref, up_ref, at_ref, lse_ref, base,
                delta_ref, dqt_ref, dq_ref, dk_ref, dv_ref, full, group, n):
    part = pl.ds(base, n)
    whole_part = pl.ds(base, full)
    product = up_ref[part].T.astype(F32) * at_ref[:, 0:n].astype(F32)
    for h in range(HEADS):
        delta_ref[h : h + 1, 0:n] = col_sum(product[SIZE * h : SIZE * h + SIZE])
    dk_ref[whole_part] = jnp.zeros((full, HALF), F32)

    def heads_of(t, carry):
        heads = [t * group + j for j in range(group)]
        keys = key_ref[part]
        keys = jnp.concatenate([keys, keys], axis=1)
        scaled, queries, values, up = query_ref[part], q_ref[part], v_ref[part], up_ref[part]
        ups = jnp.concatenate([only_head(up, h) for h in heads], axis=0)
        all_scaled = jnp.concatenate([only_head(scaled, h) for h in heads], axis=0)
        all_queries = jnp.concatenate([only_head(queries, h) for h in heads], axis=0)
        sums = jnp.concatenate([lse_ref[pl.ds(h, 1), 0:n] for h in heads], axis=1)
        deltas = jnp.concatenate([delta_ref[pl.ds(h, 1), 0:n] for h in heads], axis=1)
        soft = jnp.exp2(nt(keys, all_scaled) - sums)
        back = (soft * (nt(values, ups) - deltas)).astype(BF16)
        dv_ref[part] += nn(soft.astype(BF16), ups)
        dk_ref[part] += nn(back, all_queries)
        for j, h in enumerate(heads):
            rows = pl.ds(pl.multiple_of(h * SIZE, SIZE), SIZE)
            dqt_ref[rows, 0:n] = nn(turned_ref[rows, 0:n], back[:, n * j : n * j + n])
        return carry

    if group == HEADS:
        heads_of(0, 0)
    else:
        lax.fori_loop(0, HEADS // group, heads_of, 0)
    if n < full:
        dq_ref[whole_part] = jnp.zeros((full, HALF), F32)
    dq_ref[part] = dqt_ref[:, 0:n].T * SCALE


def prepare_back(mask, stripes, across, lanes, kern_ref, saved, up_ref, acc, key_ref, query_ref, turned_ref, dv_ref):
    q_ref, k_ref, v_ref = saved
    grid = ACROSS_GRID if across else DOWN_GRID
    key_ref[...] = valid_keys(k_ref[...], mask, stripes)
    query_ref[...] = split_queries(q_ref[...])
    turned = (k_ref[...].astype(F32) * mask).astype(BF16).T
    size = PIXELS // stripes
    for u in range(stripes):
        turned_ref[u] = turned[:, size * u : size * u + size]
    masked = v_ref[...].astype(F32) * mask
    grad = up_ref[...].astype(F32)
    back, kernel_rows, bias_row = position_back(grad.reshape(grid), masked.reshape(grid), kern_ref, lanes, across)
    dv_ref[...] = back.reshape(PIXELS, HALF)
    acc[VEC + 4 : VEC + 14, lanes] += jnp.concatenate([bias_row] + kernel_rows, axis=0)


def finish_back(x_ref, mask, lanes, weight_ref, gain_ref, shift_ref, acc, dq_ref, dk_ref, dv_ref):
    triple = jnp.concatenate([dq_ref[...], dk_ref[...] * (mask * SCALE), dv_ref[...] * mask], axis=1).astype(BF16)
    hat, rstd = normalize(x_ref[...].reshape(PIXELS, DIM).astype(F32))
    normed = (hat * gain_ref[...] + shift_ref[...]).astype(BF16)
    grads = tn(normed, triple)
    for k in range(3):
        acc[0:DIM, DIM * k + lanes.start : DIM * k + lanes.stop] += grads[:, HALF * k : HALF * k + HALF]
    d_normed = nt(triple, weight_ref[...])
    sums = col_sum(triple.astype(F32))
    acc[VEC : VEC + 1, 0:DIM] += col_sum(d_normed * hat)
    acc[VEC + 1 : VEC + 2, 0:DIM] += col_sum(d_normed)
    acc[VEC + 2 : VEC + 3, lanes] += sums[:, 0:HALF]
    acc[VEC + 3 : VEC + 4, lanes] += sums[:, 2 * HALF :]
    return norm_back(d_normed * gain_ref[...], hat, rstd).astype(BF16).reshape(4, PIX, DIM)


def backward_down_kernel(count, first, begin, meta_ref, xd0, xd1, xd2, xd3, dd0, dd1, dd2, dd3,
                         q_in, k_in, v_in, at_in, lse_in, weight_ref, gain_ref, shift_ref, kern_ref,
                         *rest):
    if not begin:
        start, *rest = rest
        *rest, early, sem = rest
    (pd0, pd1, pd2, pd3, acc,
                         x_ref, up_ref, key_ref, query_ref, turned_ref, dq_ref, dk_ref, dv_ref, part_ref,
                         delta_ref, dqt_ref) = rest
    meta = Meta(meta_ref, count)
    step = pl.program_id(0)
    i = first + step
    r, c = meta.row(), meta.col()
    height, width = meta.height(i), meta.width(i)

    @pl.when(step == 0)
    def _():
        if not begin:
            fetch(start, early, sem).start()
        acc[...] = jnp.zeros_like(acc)

    stripe = 4 * c + r
    live = (meta.keep(i) > 0) & (STRIPE * stripe < width)

    @pl.when(live)
    def _():
        mask = down_mask(height, width, stripe).reshape(PIXELS, HALF)
        lanes = slice(HALF, DIM)
        from_rows((xd0, xd1, xd2, xd3), r, x_ref)
        for k, ref in enumerate((dd0, dd1, dd2, dd3)):
            up_ref[pl.ds(pl.multiple_of(lax.rem(r + 4 - k, 4) * PIX, PIX), PIX)] = ref[0]
        prepare_back(mask, 1, False, lanes, kern_ref, (q_in.at[0], k_in.at[0], v_in.at[0]), up_ref, acc,
                     key_ref, query_ref, turned_ref, dv_ref)

        def size(n):
            attend_back(key_ref, query_ref, q_in.at[0], v_in.at[0], turned_ref.at[0], up_ref, at_in.at[0], lse_in.at[0],
                        0, delta_ref, dqt_ref, dq_ref, dk_ref, dv_ref, PIXELS, DOWN_BACK_GROUP, n)

        by_size(down_used(height), DOWN_SIZES, size)
        part_ref[...] = finish_back(x_ref, mask, lanes, weight_ref, gain_ref, shift_ref, acc, dq_ref, dk_ref, dv_ref)
        to_rows((pd0, pd1, pd2, pd3), r, part_ref)

    @pl.when(jnp.logical_not(live))
    def _():
        for ref in (pd0, pd1, pd2, pd3):
            ref[...] = jnp.zeros_like(ref)

    if not begin:

        @pl.when(step == pl.num_programs(0) - 1)
        def _():
            fetch(start, early, sem).wait()
            acc[...] += early[...]


def backward_across_kernel(count, first, begin, last, meta_ref, xa_keep, xa_recv, da_keep, da_recv,
                           q_in, k_in, v_in, at_in, lse_in, weight_ref, gain_ref, shift_ref, kern_ref,
                           *rest):
    if not begin:
        start, *rest = rest
        *rest, early, sem = rest
    if last:
        extra, *rest = rest
    (pa_keep, pa_send, acc_out,
                           acc, x_ref, up_ref, key_ref, query_ref, turned_ref, dq_ref, dk_ref, dv_ref, part_ref,
                           delta_ref, dqt_ref) = rest
    meta = Meta(meta_ref, count)
    step = pl.program_id(0)
    i = first + step
    r, c = meta.row(), meta.col()
    height, width = meta.height(i), meta.width(i)

    @pl.when(step == 0)
    def _():
        if not begin:
            fetch(start, early, sem).start()
        acc[...] = jnp.zeros_like(acc)

    stripe = 4 * r + pair_start(c)
    live = (meta.keep(i) > 0) & (STRIPE * stripe < height)

    @pl.when(live)
    def _():
        mask = across_mask(height, width, stripe).reshape(PIXELS, HALF)
        lanes = slice(0, HALF)
        for u in range(2):
            for xs, ds, side in ((xa_keep, da_keep, c), (xa_recv, da_recv, 1 - c)):
                x_ref[2 * u + side] = xs[0, u]
                up_ref[pl.ds(pl.multiple_of((2 * u + side) * PIX, PIX), PIX)] = ds[0, u]
        prepare_back(mask, 2, True, lanes, kern_ref, (q_in.at[0], k_in.at[0], v_in.at[0]), up_ref, acc,
                     key_ref, query_ref, turned_ref, dv_ref)
        half = PIXELS // 2
        dk_ref[half:] = jnp.zeros((half, HALF), F32)
        dq_ref[half:] = jnp.zeros((half, HALF), F32)

        def stripe_of(u, carry):
            def size(n):
                base = pl.multiple_of(u * half, half)
                attend_back(key_ref, query_ref, q_in.at[0], v_in.at[0], turned_ref.at[u], up_ref,
                            at_in.at[0, u], lse_in.at[0, u], base, delta_ref, dqt_ref, dq_ref, dk_ref, dv_ref,
                            half, HEADS, n)

            by_size(across_used(width), ACROSS_SIZES, size)
            return carry

        lax.fori_loop(0, live_stripes(height, stripe), stripe_of, 0)
        part_ref[...] = finish_back(x_ref, mask, lanes, weight_ref, gain_ref, shift_ref, acc, dq_ref, dk_ref, dv_ref)
        for u in range(2):
            pa_keep[0, u] = part_ref[2 * u + c]
            pa_send[0, u] = part_ref[2 * u + 1 - c]

    @pl.when(jnp.logical_not(live))
    def _():
        pa_keep[...] = jnp.zeros_like(pa_keep)
        pa_send[...] = jnp.zeros_like(pa_send)

    @pl.when(step == pl.num_programs(0) - 1)
    def _():
        if not begin:
            fetch(start, early, sem).wait()
            acc[...] += early[...]
        if last:
            acc_out[:, 0 : 3 * DIM] = acc[0:DIM].astype(BF16)
            vectors = []
            for source, count_rows in ((acc.at[VEC:, 0:DIM], 16), (extra, 8)):
                for k in range(count_rows):
                    vectors += [source[k : k + 1, 0:HALF], source[k : k + 1, HALF:DIM]]
            vectors.append(jnp.zeros((DIM - 48, HALF), F32))
            acc_out[:, 3 * DIM :] = jnp.concatenate(vectors, axis=0).astype(BF16)
        else:
            acc_out[...] = acc[...]


def finish_kernel(count, first, meta_ref, dm_ref, pd0, pd1, pd2, pd3, pa_keep, pa_recv, out_ref, total, wide):
    meta = Meta(meta_ref, count)
    r, c = meta.row(), meta.col()
    total[...] = dm_ref[0].astype(F32).reshape(4, ROWS, SLOT, DIM)
    for k, ref in enumerate((pd0, pd1, pd2, pd3)):
        total[lax.rem(r + 4 - k, 4)] += ref[0].astype(F32).reshape(ROWS, SLOT, DIM)
    for where, ref in own_stripes(pa_keep, pa_recv, c):
        total[:, where] += ref[...].astype(F32).reshape(4, STRIPE, SLOT, DIM)
    out_ref[0] = merge_cols(total, wide).astype(BF16)


def whole(shape):
    zeros = (0,) * len(shape)
    return pl.BlockSpec(shape, lambda i, *unused: zeros)


def per_image(shape, first=0):
    zeros = (0,) * len(shape)
    return pl.BlockSpec((1,) + shape, lambda i, *unused: (first + i,) + zeros)


def call(body, name, batch, scalars, inputs, outputs, scratch, micros, held=None, waits=()):
    in_specs = [spec for spec, unused in inputs]
    out_specs = [spec for spec, unused in outputs]
    moved = sum(value.size * value.dtype.itemsize for unused, value in inputs)
    aliases = {}
    held = held or {}
    inner, skipped, extra = body, len(scalars) + len(inputs), len(held) + len(waits)

    def body(*refs):
        inner(*refs[:skipped], *refs[skipped + extra :])

    for k, place in enumerate(held):
        aliases[skipped + k] = place
    in_specs = in_specs + [pl.BlockSpec(memory_space=pl.ANY)] * extra
    inputs = inputs + [(None, value) for value in list(held.values()) + list(waits)]
    return list(pl.pallas_call(
        body,
        out_shape=[shape for unused, shape in outputs],
        grid_spec=pltpu.PrefetchScalarGridSpec(
            num_scalar_prefetch=len(scalars),
            grid=(batch,),
            in_specs=in_specs,
            out_specs=out_specs,
            scratch_shapes=scratch,
        ),
        compiler_params=pltpu.CompilerParams(
            dimension_semantics=("arbitrary",), vmem_limit_bytes=VMEM_LIMIT
        ),
        input_output_aliases=aliases,
        cost_estimate=pl.CostEstimate(flops=micros * 10**9, bytes_accessed=moved, transcendentals=0),
        name=name,
    )(*scalars, *[value for unused, value in inputs]))


def struct(shape, dtype):
    return jax.ShapeDtypeStruct(shape, dtype)


def images_out(batch, shape, dtype):
    return per_image(shape), struct((batch,) + shape, dtype)


def whole_out(shape, dtype=F32):
    return whole(shape), struct(shape, dtype)


def row_exchange(parts):
    size = lax.axis_size("row")
    return [parts[0]] + [
        lax.ppermute(parts[k], "row", [(q, (q + k) % size) for q in range(size)]) for k in range(1, size)
    ]


def col_exchange(keep, send):
    return [keep, lax.ppermute(send, "col", [(0, 1), (1, 0)])]


def together(*values):
    return lax.optimization_barrier(values)


def bits_of(size):
    found = []
    bit = 1
    while bit < size:
        found.append(bit)
        bit *= 2
    return found


def kept_total(flags):
    total = flags
    size = lax.axis_size("batch")
    for bit in bits_of(size):
        total = total + lax.ppermute(total, "batch", [(q, q ^ bit) for q in range(size)])
    return total


ALL = ("batch", "row", "col")
NEAR = ("batch", "col")


def send_shares(rows, axes):
    places = lax.axis_size(axes)
    sent = rows.astype(BF16).reshape((places, -1) + rows.shape[1:])
    return lax.all_to_all(sent, axes, 0, 0)


def sum_shares(received):
    return jnp.sum(received.astype(F32), axis=0).astype(BF16)


def spread_share(share, axes):
    return jnp.broadcast_to(share[None], (lax.axis_size(axes),) + share.shape)


def gather_spread(sent, axes):
    return lax.all_to_all(sent, axes, 0, 0).reshape((-1,) + sent.shape[2:])


def send_rows(share):
    size = lax.axis_size("row")
    return [lax.ppermute(share, "row", [(q, (q + k) % size) for q in range(size)]) for k in range(1, size)]


def per_device(batch, devices, tokens, heights, widths, keep_flags, out_grad, first_gain, first_shift, triple_weight,
               query_value_bias, position_kernel, position_bias, mixing_weight, mixing_bias, second_gain, second_shift,
               expand_weight, expand_bias, reduce_weight, reduce_bias):
    count = tokens.shape[0]
    chunks = count // batch
    r, c = lax.axis_index("row"), lax.axis_index("col")
    meta = jnp.concatenate(
        [heights, widths, keep_flags[:, 0], keep_flags[:, 1], jnp.stack([r, c]).astype(jnp.int32)]
    )
    def full(value):
        return whole(value.shape), value

    def chunk_in(value):
        return per_image(value.shape[1:]), value

    def grid_out(first):
        return per_image((ROWS, ROWS, DIM), first), struct((count, ROWS, ROWS, DIM), BF16)

    pix = (PIX, DIM)
    half = (PIX, HALF)
    pair = (2, PIX, DIM)
    pair_half = (2, PIX, HALF)

    def all_images(shape, dtype, first):
        return per_image(shape, first), struct((count,) + shape, dtype)

    blocks = pltpu.VMEM((4, PIX, DIM), BF16)
    low = pltpu.VMEM((PIXELS, HALF), BF16)
    high = pltpu.VMEM((PIXELS, HALF), F32)
    pairs = pltpu.VMEM((PIXELS, DIM), BF16)
    low_blocks = pltpu.VMEM((4, PIX, HALF), BF16)
    parts_high = pltpu.VMEM((4, ROWS, SLOT, DIM), F32)
    wide = pltpu.VMEM((ROWS, 32, DIM), F32)

    def prepare(k, waits):
        first = k * batch
        outs = call(
            functools.partial(prep_kernel, count, first), "prep", batch, [meta],
            [(per_image((ROWS, ROWS, DIM), first), tokens)],
            [images_out(batch, pix, BF16)] * 4 + [images_out(batch, pair, BF16)] * 2,
            [wide, parts_high], 2 * batch, {}, waits)
        return outs[0:4], outs[4:6]

    flat = (PIXELS, HALF)
    save_scratch = [pltpu.VMEM((3, PIXELS, HALF), BF16), pltpu.SemaphoreType.DMA((3,))]

    def across_forward(k, taken, held, waits):
        first = k * batch
        shapes = [(pair_half, BF16)] * 2 + [(flat, BF16)] * 3 + [((2, HALF, PIXELS // 2), BF16), ((2, 8, PIXELS // 2), F32)]
        return call(
            functools.partial(forward_across_kernel, count, first), "across_forward", batch, [meta],
            [chunk_in(v) for v in taken] + [full(v) for v in (wa, ba, gain1, shift1, kern, pos)],
            [
                (pl.BlockSpec(memory_space=pl.ANY) if 2 <= k < 5 else per_image(shape, first), struct((count,) + shape, dtype))
                for k, (shape, dtype) in enumerate(shapes)
            ],
            [blocks, low, pairs, pltpu.VMEM((2, HEADS, SIZE + 16, PIXELS // 2), BF16), high, low_blocks,
             pltpu.VMEM((HALF, PIXELS // 2), F32)] + save_scratch,
            5 * batch, dict(enumerate(held)), waits)

    def down_forward(k, taken, waits):
        first = k * batch
        out = pl.BlockSpec(memory_space=pl.ANY), struct((batch,) + flat, BF16)
        outs = call(
            functools.partial(forward_down_kernel, count, first), "down_forward", batch, [meta],
            [chunk_in(v) for v in taken] + [full(v) for v in (wd, bd, gain1, shift1, kern, pos)],
            [images_out(batch, half, BF16)] * 4
            + [out, out, out, images_out(batch, (HALF, PIXELS), BF16), images_out(batch, (8, PIXELS), F32)],
            [blocks, low, pairs, pltpu.VMEM((1, HEADS, SIZE + 16, PIXELS), BF16), high, low_blocks,
             pltpu.VMEM((HALF, PIXELS), F32)] + save_scratch,
            6 * batch, {}, waits)
        return outs[0:4], outs[4:]

    own0, sent0 = prepare(0, [])
    own0, keep_flags, triple_weight, query_value_bias, position_kernel = together(
        own0, keep_flags, triple_weight, query_value_bias, position_kernel
    )
    kept = kept_total(jnp.sum(keep_flags.astype(F32), axis=0))
    share = kept / (count * lax.axis_size("batch"))
    factors = (keep_flags.astype(F32) / share).reshape(-1)

    def branch_weight(lo):
        return jnp.concatenate([triple_weight[:, DIM * k + lo : DIM * k + lo + HALF] for k in range(3)], axis=1)

    wa, wd = branch_weight(0), branch_weight(HALF)
    zeros = jnp.zeros((HALF,), F32)
    ba = jnp.concatenate([query_value_bias[0, :HALF], zeros, query_value_bias[1, :HALF]])[None]
    bd = jnp.concatenate([query_value_bias[0, HALF:], zeros, query_value_bias[1, HALF:]])[None]
    gain1, shift1 = first_gain[None], first_shift[None]
    gain2, shift2 = second_gain[None], second_shift[None]
    kern = jnp.pad(position_kernel.reshape(9, DIM), ((0, 7), (0, 0)))
    pos = position_bias[None]

    col0 = col_exchange(*sent0)
    row0 = row_exchange(own0)
    own1, sent1 = prepare(1, [factors])
    across0 = across_forward(0, col0, [], own1[0:1])
    own1, sent1, across_done = together(own1, sent1, across0[0])
    across0[0] = across_done
    col1 = col_exchange(*sent1)
    row1 = row_exchange(own1)
    joined0, saved0 = down_forward(0, row0, across0[0:1])
    across1 = across_forward(1, col1, across0, saved0[0:1])
    joined_across = col_exchange(*across1[0:2])
    joined1, saved1 = down_forward(1, row1, across1[2:3])
    row_joined0 = row_exchange(joined0)
    row_joined1 = row_exchange(joined1)

    def middle(k, own, row_joined, held, sums, waits):
        first = k * batch
        acc_shape = (DIM, 2 * HIDDEN + DIM)
        return call(
            functools.partial(middle_kernel, count, first), "middle", batch, [meta, factors],
            [chunk_in(v) for v in own + row_joined]
            + [(per_image(v.shape[1:], first), v) for v in joined_across + [out_grad]]
            + [full(v) for v in (mixing_weight, mixing_bias[None], gain2, shift2, expand_weight, expand_bias[None],
                                 reduce_weight, reduce_bias[None])]
            + ([(pl.BlockSpec(memory_space=pl.ANY), sums[0]), full(sums[1])] if sums else []),
            [all_images((ROWS, ROWS, DIM), BF16, first), all_images((4,) + pix, BF16, first)]
            + [images_out(batch, half, BF16)] * 4 + [images_out(batch, pair_half, BF16)] * 2
            + [whole_out(acc_shape, BF16), whole_out((8, DIM))],
            [pltpu.VMEM(acc_shape, F32), pltpu.VMEM((4,) + pix, BF16), parts_high,
             pltpu.VMEM((4, ROWS, SLOT, HALF), F32), pltpu.VMEM((4,) + pix, BF16), parts_high, parts_high, wide]
            + ([pltpu.VMEM(acc_shape, BF16), pltpu.SemaphoreType.DMA] if sums else []),
            8 * batch, held, waits)

    mid0 = middle(0, own0, row_joined0, {}, [], saved1[0:1])
    row_grad0 = row_exchange(mid0[2:6])
    col_grad0 = col_exchange(*mid0[6:8])
    mid1 = middle(1, own1, row_joined1, {0: mid0[0], 1: mid0[1]}, mid0[8:10], [])
    output, middles = mid1[0:2]
    feed, row_grad0, col_grad0 = together(mid1[8], row_grad0, col_grad0)
    row_grad1 = row_exchange(mid1[2:6])
    col_grad1 = col_exchange(*mid1[6:8])
    received = send_shares(feed, NEAR)

    back_scratch = [high, high, high, blocks, pltpu.VMEM((8, PIXELS), F32), pltpu.VMEM((HALF, PIXELS), F32)]
    back_shape = (VEC + 16, 3 * DIM)

    def early_scratch(sums):
        return [pltpu.VMEM(back_shape, F32), pltpu.SemaphoreType.DMA] if sums else []

    def down_backward(k, taken, row_grad, saved, sums, waits):
        first = k * batch
        outs = call(
            functools.partial(backward_down_kernel, count, first, not sums), "down_backward", batch, [meta],
            [chunk_in(v) for v in taken + row_grad + saved] + [full(v) for v in (wd, gain1, shift1, kern)]
            + [(pl.BlockSpec(memory_space=pl.ANY), v) for v in sums],
            [images_out(batch, pix, BF16)] * 4 + [whole_out(back_shape)],
            [blocks, low, low, pairs, pltpu.VMEM((1, HALF, PIXELS), BF16)] + back_scratch + early_scratch(sums),
            11 * batch, {}, waits)
        return outs[0:4], outs[4:]

    def across_backward(k, taken, col_grad, sums, waits):
        first = k * batch
        last = k == chunks - 1
        out = whole_out((DIM, PACKED), BF16) if last else whole_out(back_shape)
        outs = call(
            functools.partial(backward_across_kernel, count, first, not sums, last), "across_backward", batch, [meta],
            [chunk_in(v) for v in taken + col_grad] + [(per_image(v.shape[1:], first), v) for v in across1[2:]]
            + [full(v) for v in (wa, gain1, shift1, kern)]
            + [(pl.BlockSpec(memory_space=pl.ANY), v) for v in sums[:1]] + [full(v) for v in sums[1:]],
            [images_out(batch, pair, BF16)] * 2 + [out],
            [pltpu.VMEM(back_shape, F32), blocks, low, low, pairs, pltpu.VMEM((2, HALF, PIXELS // 2), BF16)]
            + back_scratch + early_scratch(sums), 9 * batch, {}, waits)
        return outs[0:2], outs[2]

    part0, sums = across_backward(0, col0, col_grad0, [], mid1[8:9] + row_grad0[1:])
    col_part0 = col_exchange(*part0)
    received, sums, row_grad1, col_grad1 = together(received, sums, row_grad1, col_grad1)
    share = sum_shares(received)
    others = send_rows(share)
    part0, sums = down_backward(0, row0, row_grad0, saved0, [sums], row_grad1[1:] + col_grad1[1:])
    row_part0 = row_exchange(part0)
    others, sums, col_part0 = together(others, sums, col_part0)
    feed = gather_spread(spread_share(sum_shares(jnp.stack([share] + others)), NEAR), NEAR)
    part1, sums = down_backward(1, row1, row_grad1, saved1, sums, col_part0[1:])
    row_part1 = row_exchange(part1)
    feed, sums = together(feed, sums)
    part1, back = across_backward(1, col1, col_grad1, sums + [mid1[9]], row_part0[1:])
    col_part1 = col_exchange(*part1)
    back, row_part1, col_part0 = together(back, row_part1, col_part0)
    received = send_shares(back, ALL)

    def finish(k, row_part, col_part, held, waits):
        first = k * batch
        return call(
            functools.partial(finish_kernel, count, first), "finish", batch, [meta],
            [(per_image(middles.shape[1:], first), middles)] + [chunk_in(v) for v in row_part + col_part],
            [grid_out(first)], [parts_high, wide], 2 * batch, held, waits)

    feed = feed.astype(F32)
    feed = [feed[:, 0:HIDDEN].T, feed[:, HIDDEN : 2 * HIDDEN], feed[:, 2 * HIDDEN :]]
    grad0 = finish(0, row_part0, col_part0, {}, [back])
    sent = spread_share(sum_shares(received), ALL)
    sent, feed, grad0, col_part1 = together(sent, feed, grad0, col_part1)
    rows = gather_spread(sent, ALL)
    tokens_grad = finish(1, row_part1, col_part1, {0: grad0[0]}, [])[0]
    back_rows = rows.astype(F32)

    triple_weight_grad = back_rows[:, 0 : 3 * DIM]
    vectors = back_rows[0:48, 3 * DIM :].reshape(24, DIM)
    rows = vectors[16:24]
    return (
        output,
        tokens_grad,
        vectors[0],
        vectors[1],
        triple_weight_grad,
        vectors[2:4],
        vectors[5:14].reshape(3, 3, DIM),
        vectors[4],
        feed[2],
        rows[7],
        rows[5],
        rows[6],
        feed[1],
        rows[0:4].reshape(HIDDEN),
        feed[0],
        rows[4],
    )


def solution(mesh):
    spread = P("batch", "row", "col", None)
    in_specs = (spread, P("batch"), P("batch"), P("batch", None), spread) + (P(),) * 14
    out_specs = (spread, spread) + (P(),) * 14
    devices = mesh.shape["batch"] * mesh.shape["row"] * mesh.shape["col"]
    return jax.shard_map(
        functools.partial(per_device, 2, devices),
        mesh=mesh, in_specs=in_specs, out_specs=out_specs, check_vma=False)
```

```python
import functools

import jax
import jax.numpy as jnp
from jax import lax
from jax.experimental import pallas as pl
from jax.experimental.pallas import tpu as pltpu
from jax.sharding import PartitionSpec as P

DIM = 256
HALF = 128
HEADS = 4
SIZE = 32
STRIPE = 7
ROWS = 28
SLOT = 8
PIX = ROWS * SLOT
HIDDEN = 1024
VEC = DIM
PACKED = 3 * DIM + HALF
F32 = jnp.float32
BF16 = jnp.bfloat16
LOG2E = 1.4426950408889634
SCALE = SIZE**-0.5
EPS = 1e-05
GELU_C = 0.7978845608028654
GELU_A = 0.044715
VMEM_LIMIT = 56 * 1024 * 1024


def nn(a, b):
    return lax.dot_general(a, b, (((1,), (0,)), ((), ())), preferred_element_type=F32)


def nt(a, b):
    return lax.dot_general(a, b, (((1,), (1,)), ((), ())), preferred_element_type=F32)


def tn(a, b):
    return lax.dot_general(a, b, (((0,), (0,)), ((), ())), preferred_element_type=F32)


def col_sum(v):
    return jnp.sum(v, axis=0, keepdims=True)


def normalize(source):
    average = jnp.mean(source, axis=-1, keepdims=True)
    centered = source - average
    spread = jnp.mean(centered * centered, axis=-1, keepdims=True)
    rstd = lax.rsqrt(spread + EPS)
    return centered * rstd, rstd


def norm_back(grad_hat, hat, rstd):
    return rstd * (
        grad_hat
        - jnp.mean(grad_hat, axis=-1, keepdims=True)
        - hat * jnp.mean(grad_hat * hat, axis=-1, keepdims=True)
    )


def head_lanes(shape):
    return lax.broadcasted_iota(jnp.int32, shape, len(shape) - 1) // SIZE


def split_cols(source, wide, parts):
    wide[:, 0:ROWS, :] = source.astype(F32)
    slot = lax.broadcasted_iota(jnp.int32, (ROWS, SLOT, DIM), 1)
    for s in range(4):
        parts[s] = jnp.where(slot < STRIPE, wide[:, STRIPE * s : STRIPE * s + SLOT, :], 0.0)


def merge_cols(parts, wide):
    for s in range(4):
        wide[:, STRIPE * s : STRIPE * s + SLOT, :] = parts[s]
    return wide[:, 0:ROWS, :]


class Meta:
    def __init__(self, ref, count):
        self.ref = ref
        self.count = count

    def height(self, i):
        return self.ref[i]

    def width(self, i):
        return self.ref[self.count + i]

    def keep(self, i):
        return self.ref[2 * self.count + i]

    def feed(self, i):
        return self.ref[3 * self.count + i]

    def row(self):
        return self.ref[4 * self.count]

    def col(self):
        return self.ref[4 * self.count + 1]


def pair_start(owner):
    return 2 * (1 - owner)


def from_rows(refs, r, out):
    for k, ref in enumerate(refs):
        out[lax.rem(r + 4 - k, 4)] = ref[0]


def to_rows(refs, r, source):
    for k, ref in enumerate(refs):
        ref[0] = source[lax.rem(r + k, 4)]


def own_stripes(keep_ref, other_ref, c):
    for ref, owner in ((keep_ref, c), (other_ref, 1 - c)):
        for u in range(2):
            yield pl.ds(STRIPE * (pair_start(owner) + u), STRIPE), ref.at[0, u]


def fetch(source, target, sem):
    return pltpu.make_async_copy(source, target, sem)


def prep_kernel(count, first, meta_ref, tok_ref, d0, d1, d2, d3, keep_ref, send_ref, wide, parts):
    meta = Meta(meta_ref, count)
    split_cols(tok_ref[0], wide, parts)
    r, c = meta.row(), meta.col()
    for k, ref in enumerate((d0, d1, d2, d3)):
        ref[0] = parts[lax.rem(r + k, 4)].reshape(PIX, DIM).astype(BF16)
    for where, ref in own_stripes(keep_ref, send_ref, c):
        ref[...] = parts[:, where].reshape(PIX, DIM).astype(BF16)


def down_mask(height, width, stripe):
    shape = (4 * ROWS, SLOT, HALF)
    row = lax.broadcasted_iota(jnp.int32, shape, 0)
    j = lax.broadcasted_iota(jnp.int32, shape, 1)
    limit = jnp.minimum(STRIPE, width - STRIPE * stripe)
    return jnp.where((row < height) & (j < limit), 1.0, 0.0)


def across_mask(height, width, stripe):
    shape = (2, 8, STRIPE, SLOT, HALF)
    u = lax.broadcasted_iota(jnp.int32, shape, 0)
    b = lax.broadcasted_iota(jnp.int32, shape, 1)
    row = lax.broadcasted_iota(jnp.int32, shape, 2)
    j = lax.broadcasted_iota(jnp.int32, shape, 3)
    good = (STRIPE * u + row < height - STRIPE * stripe) & (j < STRIPE) & (b * STRIPE + j < width)
    return jnp.where(good, 1.0, 0.0)


def down_flags(height, width, stripe):
    at = lax.broadcasted_iota(jnp.int32, (16, PIXELS), 1)
    limit = jnp.minimum(STRIPE, width - STRIPE * stripe)
    good = (at < SLOT * height) & (lax.rem(at, SLOT) < limit)
    return jnp.where(good, 1.0, 0.0).astype(BF16)


def across_flags(height, width, stripe):
    at = lax.broadcasted_iota(jnp.int32, (16, PIXELS), 1)
    size = STRIPE * SLOT
    u = jnp.where(at < PIXELS // 2, 0, 1)
    b = jnp.zeros_like(at)
    for k in range(1, 16):
        b = jnp.where(at >= size * k, k, b)
    rest = at - size * b
    j = lax.rem(rest, SLOT)
    row = (rest - j) // SLOT + STRIPE * u
    col = STRIPE * (b - SLOT * u) + j
    good = (row < height - STRIPE * stripe) & (j < STRIPE) & (col < width)
    return jnp.where(good, 1.0, 0.0).astype(BF16)


def moved_rows(v, axis, step):
    if step == 0:
        return v
    size = v.shape[axis]
    zero_shape = v.shape[:axis] + (1,) + v.shape[axis + 1 :]
    zero = jnp.zeros(zero_shape, v.dtype)
    if step > 0:
        return jnp.concatenate([lax.slice_in_dim(v, 1, size, axis=axis), zero], axis=axis)
    return jnp.concatenate([zero, lax.slice_in_dim(v, 0, size - 1, axis=axis)], axis=axis)


def roll8(v, shift):
    shape = v.shape
    flat = v.reshape(-1, SLOT, HALF)
    return pltpu.roll(flat, shift, 1).reshape(shape)


def moved_cols_down(v, step):
    if step == 0:
        return v
    return roll8(v, 1 if step < 0 else SLOT - 1)


def moved_cols_across(v, step):
    if step == 0:
        return v
    slot = lax.broadcasted_iota(jnp.int32, v.shape, 3)
    if step < 0:
        return jnp.where(slot == 0, moved_rows(roll8(v, 2), 1, -1), roll8(v, 1))
    return jnp.where(slot == STRIPE - 1, moved_rows(roll8(v, SLOT - 2), 1, 1), roll8(v, SLOT - 1))


def taps(v, across):
    moved_cols = moved_cols_across if across else moved_cols_down
    row_axis = 2 if across else 0
    for b in range(3):
        side = moved_cols(v, b - 1)
        for a in range(3):
            yield a, b, moved_rows(side, row_axis, a - 1)


def position_term(v, kern_ref, bias_ref, lanes, across):
    total = bias_ref[0:1, lanes]
    for a, b, moved in taps(v, across):
        total = total + moved * kern_ref[3 * a + b : 3 * a + b + 1, lanes]
    return total


def position_back(grad, v, kern_ref, lanes, across):
    total = 0.0
    for a, b, moved in taps(grad, across):
        k = 3 * (2 - a) + (2 - b)
        total = total + moved * kern_ref[k : k + 1, lanes]
    kernel_grads = []
    flat = grad.reshape(-1, HALF)
    found = {}
    for a, b, moved in taps(v, across):
        found[3 * a + b] = col_sum(flat * moved.reshape(-1, HALF))
    for k in range(9):
        kernel_grads.append(found[k])
    return total, kernel_grads, col_sum(flat)


DOWN_GRID = (4 * ROWS, SLOT, HALF)
ACROSS_GRID = (2, 8, STRIPE, SLOT, HALF)
DOWN_SIZES = (640, 768, 896)
ACROSS_SIZES = (280, 336, 392, 448)
DOWN_GROUP = 4
MIDDLE_GROUP = 4
HIDDEN_TILE = 512
DOWN_BACK_GROUP = 2
PIXELS = 4 * PIX


def by_size(used, sizes, body):
    below = None
    for n in sizes:
        fits = used <= n
        if n == sizes[-1]:
            fits = True if below is None else used > below
        elif below is not None:
            fits = fits & (used > below)
        pl.when(fits)(functools.partial(body, n))
        below = n


def project(x_ref, weight_ref, bias_ref, gain_ref, shift_ref):
    hat, unused = normalize(x_ref[...].reshape(PIXELS, DIM).astype(F32))
    normed = (hat * gain_ref[...] + shift_ref[...]).astype(BF16)
    return (nn(normed, weight_ref[...]) + bias_ref[...]).astype(BF16)


def split_queries(query):
    scaled = query.astype(F32) * (SCALE * LOG2E)
    high = scaled.astype(BF16)
    low = (scaled - high.astype(F32)).astype(BF16)
    return jnp.concatenate([high, low], axis=1)


def valid_keys(keys, mask, stripes):
    size = PIXELS // stripes
    keys = keys.astype(F32)
    fixed = [
        jnp.where(
            mask[size * u : size * u + size] > 0.0, keys[size * u : size * u + size], keys[size * u : size * u + 1]
        )
        for u in range(stripes)
    ]
    return jnp.concatenate(fixed, axis=0).astype(BF16)


def only_head(value, h):
    lane = lax.broadcasted_iota(jnp.int32, value.shape, 1)
    return jnp.where(lax.rem(lane, HALF) // SIZE == h, value, jnp.zeros_like(value))


def attend(key_ref, query_ref, turned_ref, base, at_out, lse_out, a_ref, turned_a, full, group, n):
    part = pl.ds(base, n)
    whole_part = pl.ds(base, full)

    def heads_of(t, carry):
        heads = [t * group + j for j in range(group)]
        keys = key_ref[part]
        keys = jnp.concatenate([keys, keys], axis=1)
        queries = query_ref[part]
        scores = [nt(keys, only_head(queries, h)) for h in heads]
        tops = [jnp.max(s, axis=0, keepdims=True) for s in scores]
        weights = [jnp.exp2(s - top).astype(BF16) for s, top in zip(scores, tops)]
        outs = [nn(turned_ref[h, :, 0:n], w) for h, w in zip(heads, weights)]
        for h, out, top in zip(heads, outs, tops):
            total = out[SIZE : SIZE + 1]
            turned_a[pl.ds(pl.multiple_of(h * SIZE, SIZE), SIZE), 0:n] = out[0:SIZE] / total
            lse_out[pl.ds(h, 1), 0:n] = top + jnp.log2(total)
        return carry

    if group == HEADS:
        heads_of(0, 0)
    else:
        lax.fori_loop(0, HEADS // group, heads_of, 0)
    if n < full:
        a_ref[whole_part] = jnp.zeros((full, HALF), F32)
    at_out[:, 0:n] = turned_a[:, 0:n].astype(BF16)
    a_ref[part] = turned_a[:, 0:n].T


def prepare_forward(x_ref, mask, flags, stripes, weight_ref, bias_ref, gain_ref, shift_ref, saved, key_ref, query_ref, turned_ref):
    triple = project(x_ref, weight_ref, bias_ref, gain_ref, shift_ref)
    for k in range(3):
        saved[k] = triple[:, HALF * k : HALF * k + HALF]
    query_ref[...] = split_queries(triple[:, 0:HALF])
    key_ref[...] = valid_keys(triple[:, HALF : 2 * HALF], mask, stripes)
    masked = triple[:, 2 * HALF :].astype(F32) * mask
    turned = masked.astype(BF16).T
    size = PIXELS // stripes
    for u in range(stripes):
        part = slice(size * u, size * u + size)
        for h in range(HEADS):
            turned_ref[u, h, 0:SIZE] = turned[SIZE * h : SIZE * h + SIZE, part]
            turned_ref[u, h, SIZE:] = flags[:, part]
    return masked


def down_used(height):
    return SLOT * height


def live_stripes(height, stripe):
    return jnp.where(STRIPE * (stripe + 1) < height, 2, 1)


def across_used(width):
    return STRIPE * SLOT * ((width + STRIPE - 1) // STRIPE)


def forward_down_kernel(count, first, meta_ref, xd0, xd1, xd2, xd3, weight_ref, bias_ref, gain_ref, shift_ref,
                        kern_ref, pos_ref, jd0, jd1, jd2, jd3, q_out, k_out, v_out, at_out, lse_out,
                        x_ref, key_ref, query_ref, turned_ref, a_ref, j_ref, turned_a, saved, sems):
    meta = Meta(meta_ref, count)
    place = pl.program_id(0)
    i = first + place
    r, c = meta.row(), meta.col()
    height, width = meta.height(i), meta.width(i)
    stripe = 4 * c + r
    live = (meta.keep(i) > 0) & (STRIPE * stripe < width)

    @pl.when(live)
    def _():
        from_rows((xd0, xd1, xd2, xd3), r, x_ref)
        mask = down_mask(height, width, stripe)
        masked = prepare_forward(
            x_ref, mask.reshape(PIXELS, HALF), down_flags(height, width, stripe), 1, weight_ref, bias_ref, gain_ref, shift_ref,
            saved, key_ref, query_ref, turned_ref)
        copies = [fetch(saved.at[k], out.at[place], sems.at[k]) for k, out in enumerate((q_out, k_out, v_out))]
        for copy in copies:
            copy.start()

        def size(n):
            attend(key_ref, query_ref, turned_ref.at[0], 0, at_out.at[0], lse_out.at[0], a_ref, turned_a, PIXELS, DOWN_GROUP, n)

        by_size(down_used(height), DOWN_SIZES, size)
        term = position_term(masked.reshape(DOWN_GRID), kern_ref, pos_ref, slice(HALF, DIM), False)
        total = a_ref[...] + term.reshape(PIXELS, HALF)
        j_ref[...] = total.astype(BF16).reshape(4, PIX, HALF)
        to_rows((jd0, jd1, jd2, jd3), r, j_ref)
        for copy in copies:
            copy.wait()

    @pl.when(jnp.logical_not(live))
    def _():
        for ref in (jd0, jd1, jd2, jd3):
            ref[...] = jnp.zeros_like(ref)


def forward_across_kernel(count, first, meta_ref, xa_keep, xa_recv, weight_ref, bias_ref, gain_ref, shift_ref,
                          kern_ref, pos_ref, ja_keep, ja_send, q_out, k_out, v_out, at_out, lse_out,
                          x_ref, key_ref, query_ref, turned_ref, a_ref, j_ref, turned_a, saved, sems):
    meta = Meta(meta_ref, count)
    i = first + pl.program_id(0)
    place = i
    r, c = meta.row(), meta.col()
    height, width = meta.height(i), meta.width(i)
    stripe = 4 * r + pair_start(c)
    live = (meta.keep(i) > 0) & (STRIPE * stripe < height)

    @pl.when(live)
    def _():
        mask = across_mask(height, width, stripe)
        for u in range(2):
            x_ref[2 * u + c] = xa_keep[0, u]
            x_ref[2 * u + 1 - c] = xa_recv[0, u]
        masked = prepare_forward(
            x_ref, mask.reshape(PIXELS, HALF), across_flags(height, width, stripe), 2, weight_ref, bias_ref, gain_ref, shift_ref,
            saved, key_ref, query_ref, turned_ref)
        copies = [fetch(saved.at[k], out.at[place], sems.at[k]) for k, out in enumerate((q_out, k_out, v_out))]
        for copy in copies:
            copy.start()
        half = PIXELS // 2
        a_ref[half:] = jnp.zeros((half, HALF), F32)

        def stripe_of(u, carry):
            def size(n):
                base = pl.multiple_of(u * half, half)
                attend(key_ref, query_ref, turned_ref.at[u], base, at_out.at[0, u], lse_out.at[0, u], a_ref, turned_a, half, HEADS, n)

            by_size(across_used(width), ACROSS_SIZES, size)
            return carry

        lax.fori_loop(0, live_stripes(height, stripe), stripe_of, 0)
        term = position_term(masked.reshape(ACROSS_GRID), kern_ref, pos_ref, slice(0, HALF), True)
        j_ref[...] = (a_ref[...] + term.reshape(PIXELS, HALF)).astype(BF16).reshape(4, PIX, HALF)
        for u in range(2):
            ja_keep[0, u] = j_ref[2 * u + c]
            ja_send[0, u] = j_ref[2 * u + 1 - c]
        for copy in copies:
            copy.wait()

    @pl.when(jnp.logical_not(live))
    def _():
        ja_keep[...] = jnp.zeros_like(ja_keep)
        ja_send[...] = jnp.zeros_like(ja_send)


def pixel_mask(height, width, first_block, blocks, r, c):
    shape = (blocks, ROWS, SLOT, HALF)
    s = lax.broadcasted_iota(jnp.int32, shape, 0) + first_block
    row = lax.broadcasted_iota(jnp.int32, shape, 1)
    j = lax.broadcasted_iota(jnp.int32, shape, 2)
    good = (row < height - ROWS * r) & (j < STRIPE) & (s * STRIPE + j < width - ROWS * c)
    mask = jnp.where(good, 1.0, 0.0).reshape(blocks * PIX, HALF)
    return jnp.concatenate([mask, mask], axis=1)


def gelu_pair(pre, d_act):
    square = pre * pre
    bend = jnp.tanh(pre * (GELU_C + (GELU_C * GELU_A) * square))
    half_one = 0.5 + 0.5 * bend
    slope = half_one + (0.5 * pre) * (1.0 - bend * bend) * (GELU_C + (3.0 * GELU_C * GELU_A) * square)
    return (pre * half_one).astype(BF16), (d_act * slope).astype(BF16)


def middle_kernel(count, first, meta_ref, fact_ref, xd0, xd1, xd2, xd3, jd0, jd1, jd2, jd3, ja_keep, ja_recv, grad_ref,
                  wm_ref, bm_ref, gain_ref, shift_ref, we_ref, be_ref, wr_ref, br_ref, *rest):
    if first > 0:
        start, start_v, *rest = rest
        *rest, early, sem = rest
    (out_ref, dm_ref, dd0, dd1, dd2, dd3, da_keep, da_send, acc_out, acc_v, acc,
     x_ref, g_ref, ja_ref, j_ref, o_ref, dj_ref, wide) = rest
    meta = Meta(meta_ref, count)
    step = pl.program_id(0)
    i = first + step
    r, c = meta.row(), meta.col()
    height, width = meta.height(i), meta.width(i)
    attend_factor = fact_ref[2 * i]
    feed_factor = fact_ref[2 * i + 1]

    @pl.when(step == 0)
    def _():
        if first > 0:
            fetch(start, early, sem).start()
        acc[...] = jnp.zeros_like(acc)
        acc_v[...] = start_v[...] if first > 0 else jnp.zeros_like(acc_v)

    split_cols(grad_ref[0], wide, g_ref)
    for k, (xs, js) in enumerate(((xd0, jd0), (xd1, jd1), (xd2, jd2), (xd3, jd3))):
        x_ref[lax.rem(r + k, 4)] = xs[0]
        j_ref[lax.rem(r + 4 - k, 4), :, HALF:] = js[0]
    for where, ref in own_stripes(ja_keep, ja_recv, c):
        ja_ref[:, where] = ref[...].astype(F32).reshape(4, STRIPE, SLOT, HALF)
    j_ref[:, :, 0:HALF] = ja_ref[...].reshape(4, PIX, HALF).astype(BF16)

    group = MIDDLE_GROUP
    size = group * PIX

    def one(b, carry):
        where = pl.ds(group * b, group)
        mask = pixel_mask(height, width, group * b, group, r, c)
        scale_attend = mask * attend_factor
        scale_feed = mask * feed_factor
        x = x_ref[where].reshape(size, DIM).astype(F32)
        joined = j_ref[where].reshape(size, DIM)
        g = g_ref[where].reshape(size, DIM)
        mixed = nn(joined, wm_ref[...]) + bm_ref[...]
        middle = x + scale_attend * mixed
        def mixing_back(d_middle):
            dm_ref[0, where] = d_middle.astype(BF16).reshape(group, PIX, DIM)
            d_mixed = (scale_attend * d_middle).astype(BF16)
            acc[:, 2 * HIDDEN :] += tn(joined, d_mixed)
            dj_ref[where] = nt(d_mixed, wm_ref[...]).reshape(group, ROWS, SLOT, DIM)
            acc_v[7:8] += col_sum(d_mixed.astype(F32))

        fed = meta.feed(i) > 0

        @pl.when(fed)
        def _():
            hat, rstd = normalize(middle)
            normed = (hat * gain_ref[...] + shift_ref[...]).astype(BF16)
            d_reduced = (scale_feed * g).astype(BF16)
            turned_grad, turned_normed = d_reduced.T, normed.T
            tiles = HIDDEN // HIDDEN_TILE
            first_dots, hidden = {}, {}
            reduced, d_normed, sums = br_ref[...], 0.0, []
            for t in range(tiles + 2):
                if t < tiles:
                    cols = slice(HIDDEN_TILE * t, HIDDEN_TILE * t + HIDDEN_TILE)
                    first_dots[t] = nn(normed, we_ref[:, cols]), nt(d_reduced, wr_ref[cols])
                if 1 <= t <= tiles:
                    j = t - 1
                    cols = slice(HIDDEN_TILE * j, HIDDEN_TILE * j + HIDDEN_TILE)
                    pre, d_act = first_dots.pop(j)
                    hidden[j] = gelu_pair(pre + be_ref[:, cols], d_act)
                if t >= 2:
                    j = t - 2
                    cols = slice(HIDDEN_TILE * j, HIDDEN_TILE * j + HIDDEN_TILE)
                    wide_cols = slice(HIDDEN + HIDDEN_TILE * j, HIDDEN + HIDDEN_TILE * j + HIDDEN_TILE)
                    act, d_hidden = hidden.pop(j)
                    reduced = reduced + nn(act, wr_ref[cols])
                    d_normed = d_normed + nt(d_hidden, we_ref[:, cols])
                    acc[:, cols] += nn(turned_grad, act)
                    acc[:, wide_cols] += nn(turned_normed, d_hidden)
                    sums.append(col_sum(d_hidden.astype(F32)))
            d_hidden_sum = jnp.concatenate(sums, axis=1)
            o_ref[where] = (middle + scale_feed * reduced).reshape(group, ROWS, SLOT, DIM)
            d_middle = g + norm_back(d_normed * gain_ref[...], hat, rstd)
            mixing_back(d_middle)
            rows = [d_hidden_sum[:, DIM * k : DIM * k + DIM] for k in range(4)]
            rows.append(col_sum(d_reduced.astype(F32)))
            rows.append(col_sum(d_normed * hat))
            rows.append(col_sum(d_normed))
            acc_v[0:7] += jnp.concatenate(rows, axis=0)

        @pl.when(jnp.logical_not(fed))
        def _():
            o_ref[where] = middle.reshape(group, ROWS, SLOT, DIM)
            mixing_back(g)

        return carry

    lax.fori_loop(0, 4 // group, one, 0)

    @pl.when(step == pl.num_programs(0) - 1)
    def _():
        if first > 0:
            fetch(start, early, sem).wait()
            acc_out[...] = (acc[...] + early[...].astype(F32)).astype(BF16)
        else:
            acc_out[...] = acc[...].astype(BF16)

    out_ref[0] = merge_cols(o_ref, wide).astype(BF16)
    for k, ref in enumerate((dd0, dd1, dd2, dd3)):
        ref[0] = dj_ref[lax.rem(r + k, 4), :, :, HALF:].reshape(PIX, HALF).astype(BF16)
    for where, ref in own_stripes(da_keep, da_send, c):
        ref[...] = dj_ref[:, where, :, 0:HALF].reshape(PIX, HALF).astype(BF16)


def attend_back(key_ref, query_ref, q_ref, v_ref, turned_ref, up_ref, at_ref, lse_ref, base,
                delta_ref, dqt_ref, dq_ref, dk_ref, dv_ref, full, group, n):
    part = pl.ds(base, n)
    whole_part = pl.ds(base, full)
    product = up_ref[part].T.astype(F32) * at_ref[:, 0:n].astype(F32)
    for h in range(HEADS):
        delta_ref[h : h + 1, 0:n] = col_sum(product[SIZE * h : SIZE * h + SIZE])
    dk_ref[whole_part] = jnp.zeros((full, HALF), F32)

    def heads_of(t, carry):
        heads = [t * group + j for j in range(group)]
        keys = key_ref[part]
        keys = jnp.concatenate([keys, keys], axis=1)
        scaled, queries, values, up = query_ref[part], q_ref[part], v_ref[part], up_ref[part]
        ups = jnp.concatenate([only_head(up, h) for h in heads], axis=0)
        all_scaled = jnp.concatenate([only_head(scaled, h) for h in heads], axis=0)
        all_queries = jnp.concatenate([only_head(queries, h) for h in heads], axis=0)
        sums = jnp.concatenate([lse_ref[pl.ds(h, 1), 0:n] for h in heads], axis=1)
        deltas = jnp.concatenate([delta_ref[pl.ds(h, 1), 0:n] for h in heads], axis=1)
        soft = jnp.exp2(nt(keys, all_scaled) - sums)
        back = (soft * (nt(values, ups) - deltas)).astype(BF16)
        dv_ref[part] += nn(soft.astype(BF16), ups)
        dk_ref[part] += nn(back, all_queries)
        for j, h in enumerate(heads):
            rows = pl.ds(pl.multiple_of(h * SIZE, SIZE), SIZE)
            dqt_ref[rows, 0:n] = nn(turned_ref[rows, 0:n], back[:, n * j : n * j + n])
        return carry

    if group == HEADS:
        heads_of(0, 0)
    else:
        lax.fori_loop(0, HEADS // group, heads_of, 0)
    if n < full:
        dq_ref[whole_part] = jnp.zeros((full, HALF), F32)
    dq_ref[part] = dqt_ref[:, 0:n].T * SCALE


def prepare_back(mask, stripes, across, lanes, kern_ref, saved, up_ref, acc, key_ref, query_ref, turned_ref, dv_ref):
    q_ref, k_ref, v_ref = saved
    grid = ACROSS_GRID if across else DOWN_GRID
    key_ref[...] = valid_keys(k_ref[...], mask, stripes)
    query_ref[...] = split_queries(q_ref[...])
    turned = (k_ref[...].astype(F32) * mask).astype(BF16).T
    size = PIXELS // stripes
    for u in range(stripes):
        turned_ref[u] = turned[:, size * u : size * u + size]
    masked = v_ref[...].astype(F32) * mask
    grad = up_ref[...].astype(F32)
    back, kernel_rows, bias_row = position_back(grad.reshape(grid), masked.reshape(grid), kern_ref, lanes, across)
    dv_ref[...] = back.reshape(PIXELS, HALF)
    acc[VEC + 4 : VEC + 14, lanes] += jnp.concatenate([bias_row] + kernel_rows, axis=0)


def finish_back(x_ref, mask, lanes, weight_ref, gain_ref, shift_ref, acc, dq_ref, dk_ref, dv_ref):
    triple = jnp.concatenate([dq_ref[...], dk_ref[...] * (mask * SCALE), dv_ref[...] * mask], axis=1).astype(BF16)
    hat, rstd = normalize(x_ref[...].reshape(PIXELS, DIM).astype(F32))
    normed = (hat * gain_ref[...] + shift_ref[...]).astype(BF16)
    grads = tn(normed, triple)
    for k in range(3):
        acc[0:DIM, DIM * k + lanes.start : DIM * k + lanes.stop] += grads[:, HALF * k : HALF * k + HALF]
    d_normed = nt(triple, weight_ref[...])
    sums = col_sum(triple.astype(F32))
    acc[VEC : VEC + 1, 0:DIM] += col_sum(d_normed * hat)
    acc[VEC + 1 : VEC + 2, 0:DIM] += col_sum(d_normed)
    acc[VEC + 2 : VEC + 3, lanes] += sums[:, 0:HALF]
    acc[VEC + 3 : VEC + 4, lanes] += sums[:, 2 * HALF :]
    return norm_back(d_normed * gain_ref[...], hat, rstd).astype(BF16).reshape(4, PIX, DIM)


def backward_down_kernel(count, first, begin, meta_ref, xd0, xd1, xd2, xd3, dd0, dd1, dd2, dd3,
                         q_in, k_in, v_in, at_in, lse_in, weight_ref, gain_ref, shift_ref, kern_ref,
                         *rest):
    if not begin:
        start, *rest = rest
        *rest, early, sem = rest
    (pd0, pd1, pd2, pd3, acc,
                         x_ref, up_ref, key_ref, query_ref, turned_ref, dq_ref, dk_ref, dv_ref, part_ref,
                         delta_ref, dqt_ref) = rest
    meta = Meta(meta_ref, count)
    step = pl.program_id(0)
    i = first + step
    r, c = meta.row(), meta.col()
    height, width = meta.height(i), meta.width(i)

    @pl.when(step == 0)
    def _():
        if not begin:
            fetch(start, early, sem).start()
        acc[...] = jnp.zeros_like(acc)

    stripe = 4 * c + r
    live = (meta.keep(i) > 0) & (STRIPE * stripe < width)

    @pl.when(live)
    def _():
        mask = down_mask(height, width, stripe).reshape(PIXELS, HALF)
        lanes = slice(HALF, DIM)
        from_rows((xd0, xd1, xd2, xd3), r, x_ref)
        for k, ref in enumerate((dd0, dd1, dd2, dd3)):
            up_ref[pl.ds(pl.multiple_of(lax.rem(r + 4 - k, 4) * PIX, PIX), PIX)] = ref[0]
        prepare_back(mask, 1, False, lanes, kern_ref, (q_in.at[0], k_in.at[0], v_in.at[0]), up_ref, acc,
                     key_ref, query_ref, turned_ref, dv_ref)

        def size(n):
            attend_back(key_ref, query_ref, q_in.at[0], v_in.at[0], turned_ref.at[0], up_ref, at_in.at[0], lse_in.at[0],
                        0, delta_ref, dqt_ref, dq_ref, dk_ref, dv_ref, PIXELS, DOWN_BACK_GROUP, n)

        by_size(down_used(height), DOWN_SIZES, size)
        part_ref[...] = finish_back(x_ref, mask, lanes, weight_ref, gain_ref, shift_ref, acc, dq_ref, dk_ref, dv_ref)
        to_rows((pd0, pd1, pd2, pd3), r, part_ref)

    @pl.when(jnp.logical_not(live))
    def _():
        for ref in (pd0, pd1, pd2, pd3):
            ref[...] = jnp.zeros_like(ref)

    if not begin:

        @pl.when(step == pl.num_programs(0) - 1)
        def _():
            fetch(start, early, sem).wait()
            acc[...] += early[...]


def backward_across_kernel(count, first, begin, last, meta_ref, xa_keep, xa_recv, da_keep, da_recv,
                           q_in, k_in, v_in, at_in, lse_in, weight_ref, gain_ref, shift_ref, kern_ref,
                           *rest):
    if not begin:
        start, *rest = rest
        *rest, early, sem = rest
    if last:
        extra, *rest = rest
    (pa_keep, pa_send, acc_out,
                           acc, x_ref, up_ref, key_ref, query_ref, turned_ref, dq_ref, dk_ref, dv_ref, part_ref,
                           delta_ref, dqt_ref) = rest
    meta = Meta(meta_ref, count)
    step = pl.program_id(0)
    i = first + step
    r, c = meta.row(), meta.col()
    height, width = meta.height(i), meta.width(i)

    @pl.when(step == 0)
    def _():
        if not begin:
            fetch(start, early, sem).start()
        acc[...] = jnp.zeros_like(acc)

    stripe = 4 * r + pair_start(c)
    live = (meta.keep(i) > 0) & (STRIPE * stripe < height)

    @pl.when(live)
    def _():
        mask = across_mask(height, width, stripe).reshape(PIXELS, HALF)
        lanes = slice(0, HALF)
        for u in range(2):
            for xs, ds, side in ((xa_keep, da_keep, c), (xa_recv, da_recv, 1 - c)):
                x_ref[2 * u + side] = xs[0, u]
                up_ref[pl.ds(pl.multiple_of((2 * u + side) * PIX, PIX), PIX)] = ds[0, u]
        prepare_back(mask, 2, True, lanes, kern_ref, (q_in.at[0], k_in.at[0], v_in.at[0]), up_ref, acc,
                     key_ref, query_ref, turned_ref, dv_ref)
        half = PIXELS // 2
        dk_ref[half:] = jnp.zeros((half, HALF), F32)
        dq_ref[half:] = jnp.zeros((half, HALF), F32)

        def stripe_of(u, carry):
            def size(n):
                base = pl.multiple_of(u * half, half)
                attend_back(key_ref, query_ref, q_in.at[0], v_in.at[0], turned_ref.at[u], up_ref,
                            at_in.at[0, u], lse_in.at[0, u], base, delta_ref, dqt_ref, dq_ref, dk_ref, dv_ref,
                            half, HEADS, n)

            by_size(across_used(width), ACROSS_SIZES, size)
            return carry

        lax.fori_loop(0, live_stripes(height, stripe), stripe_of, 0)
        part_ref[...] = finish_back(x_ref, mask, lanes, weight_ref, gain_ref, shift_ref, acc, dq_ref, dk_ref, dv_ref)
        for u in range(2):
            pa_keep[0, u] = part_ref[2 * u + c]
            pa_send[0, u] = part_ref[2 * u + 1 - c]

    @pl.when(jnp.logical_not(live))
    def _():
        pa_keep[...] = jnp.zeros_like(pa_keep)
        pa_send[...] = jnp.zeros_like(pa_send)

    @pl.when(step == pl.num_programs(0) - 1)
    def _():
        if not begin:
            fetch(start, early, sem).wait()
            acc[...] += early[...]
        if last:
            acc_out[:, 0 : 3 * DIM] = acc[0:DIM].astype(BF16)
            vectors = []
            for source, count_rows in ((acc.at[VEC:, 0:DIM], 16), (extra, 8)):
                for k in range(count_rows):
                    vectors += [source[k : k + 1, 0:HALF], source[k : k + 1, HALF:DIM]]
            vectors.append(jnp.zeros((DIM - 48, HALF), F32))
            acc_out[:, 3 * DIM :] = jnp.concatenate(vectors, axis=0).astype(BF16)
        else:
            acc_out[...] = acc[...]


def finish_kernel(count, first, meta_ref, dm_ref, pd0, pd1, pd2, pd3, pa_keep, pa_recv, out_ref, total, wide):
    meta = Meta(meta_ref, count)
    r, c = meta.row(), meta.col()
    total[...] = dm_ref[0].astype(F32).reshape(4, ROWS, SLOT, DIM)
    for k, ref in enumerate((pd0, pd1, pd2, pd3)):
        total[lax.rem(r + 4 - k, 4)] += ref[0].astype(F32).reshape(ROWS, SLOT, DIM)
    for where, ref in own_stripes(pa_keep, pa_recv, c):
        total[:, where] += ref[...].astype(F32).reshape(4, STRIPE, SLOT, DIM)
    out_ref[0] = merge_cols(total, wide).astype(BF16)


def whole(shape):
    zeros = (0,) * len(shape)
    return pl.BlockSpec(shape, lambda i, *unused: zeros)


def per_image(shape, first=0):
    zeros = (0,) * len(shape)
    return pl.BlockSpec((1,) + shape, lambda i, *unused: (first + i,) + zeros)


def call(body, name, batch, scalars, inputs, outputs, scratch, micros, held=None, waits=()):
    in_specs = [spec for spec, unused in inputs]
    out_specs = [spec for spec, unused in outputs]
    moved = sum(value.size * value.dtype.itemsize for unused, value in inputs)
    aliases = {}
    held = held or {}
    inner, skipped, extra = body, len(scalars) + len(inputs), len(held) + len(waits)

    def body(*refs):
        inner(*refs[:skipped], *refs[skipped + extra :])

    for k, place in enumerate(held):
        aliases[skipped + k] = place
    in_specs = in_specs + [pl.BlockSpec(memory_space=pl.ANY)] * extra
    inputs = inputs + [(None, value) for value in list(held.values()) + list(waits)]
    return list(pl.pallas_call(
        body,
        out_shape=[shape for unused, shape in outputs],
        grid_spec=pltpu.PrefetchScalarGridSpec(
            num_scalar_prefetch=len(scalars),
            grid=(batch,),
            in_specs=in_specs,
            out_specs=out_specs,
            scratch_shapes=scratch,
        ),
        compiler_params=pltpu.CompilerParams(
            dimension_semantics=("arbitrary",), vmem_limit_bytes=VMEM_LIMIT
        ),
        input_output_aliases=aliases,
        cost_estimate=pl.CostEstimate(flops=micros * 10**9, bytes_accessed=moved, transcendentals=0),
        name=name,
    )(*scalars, *[value for unused, value in inputs]))


def struct(shape, dtype):
    return jax.ShapeDtypeStruct(shape, dtype)


def images_out(batch, shape, dtype):
    return per_image(shape), struct((batch,) + shape, dtype)


def whole_out(shape, dtype=F32):
    return whole(shape), struct(shape, dtype)


def row_exchange(parts):
    size = lax.axis_size("row")
    return [parts[0]] + [
        lax.ppermute(parts[k], "row", [(q, (q + k) % size) for q in range(size)]) for k in range(1, size)
    ]


def col_exchange(keep, send):
    return [keep, lax.ppermute(send, "col", [(0, 1), (1, 0)])]


def together(*values):
    return lax.optimization_barrier(values)


def bits_of(size):
    found = []
    bit = 1
    while bit < size:
        found.append(bit)
        bit *= 2
    return found


def kept_step(total, bit):
    size = lax.axis_size("batch")
    return total + lax.ppermute(total, "batch", [(q, q ^ bit) for q in range(size)])


ALL = ("batch", "row", "col")
NEAR = ("batch", "col")


def send_shares(rows, axes):
    places = lax.axis_size(axes)
    sent = rows.astype(BF16).reshape((places, -1) + rows.shape[1:])
    return lax.all_to_all(sent, axes, 0, 0)


def sum_shares(received):
    return jnp.sum(received.astype(F32), axis=0).astype(BF16)


def spread_share(share, axes):
    return jnp.broadcast_to(share[None], (lax.axis_size(axes),) + share.shape)


def gather_spread(sent, axes):
    return lax.all_to_all(sent, axes, 0, 0).reshape((-1,) + sent.shape[2:])


def send_rows(share):
    size = lax.axis_size("row")
    return [lax.ppermute(share, "row", [(q, (q + k) % size) for q in range(size)]) for k in range(1, size)]


def per_device(batch, devices, tokens, heights, widths, keep_flags, out_grad, first_gain, first_shift, triple_weight,
               query_value_bias, position_kernel, position_bias, mixing_weight, mixing_bias, second_gain, second_shift,
               expand_weight, expand_bias, reduce_weight, reduce_bias):
    count = tokens.shape[0]
    chunks = count // batch
    r, c = lax.axis_index("row"), lax.axis_index("col")
    meta = jnp.concatenate(
        [heights, widths, keep_flags[:, 0], keep_flags[:, 1], jnp.stack([r, c]).astype(jnp.int32)]
    )
    def full(value):
        return whole(value.shape), value

    def chunk_in(value):
        return per_image(value.shape[1:]), value

    def grid_out(first):
        return per_image((ROWS, ROWS, DIM), first), struct((count, ROWS, ROWS, DIM), BF16)

    pix = (PIX, DIM)
    half = (PIX, HALF)
    pair = (2, PIX, DIM)
    pair_half = (2, PIX, HALF)

    def all_images(shape, dtype, first):
        return per_image(shape, first), struct((count,) + shape, dtype)

    blocks = pltpu.VMEM((4, PIX, DIM), BF16)
    low = pltpu.VMEM((PIXELS, HALF), BF16)
    high = pltpu.VMEM((PIXELS, HALF), F32)
    pairs = pltpu.VMEM((PIXELS, DIM), BF16)
    low_blocks = pltpu.VMEM((4, PIX, HALF), BF16)
    parts_high = pltpu.VMEM((4, ROWS, SLOT, DIM), F32)
    wide = pltpu.VMEM((ROWS, 32, DIM), F32)

    def prepare(k, waits):
        first = k * batch
        outs = call(
            functools.partial(prep_kernel, count, first), "prep", batch, [meta],
            [(per_image((ROWS, ROWS, DIM), first), tokens)],
            [images_out(batch, pix, BF16)] * 4 + [images_out(batch, pair, BF16)] * 2,
            [wide, parts_high], 2 * batch, {}, waits)
        return outs[0:4], outs[4:6]

    flat = (PIXELS, HALF)
    save_scratch = [pltpu.VMEM((3, PIXELS, HALF), BF16), pltpu.SemaphoreType.DMA((3,))]

    def across_forward(k, taken, held, waits):
        first = k * batch
        shapes = [(pair_half, BF16)] * 2 + [(flat, BF16)] * 3 + [((2, HALF, PIXELS // 2), BF16), ((2, 8, PIXELS // 2), F32)]
        return call(
            functools.partial(forward_across_kernel, count, first), "across_forward", batch, [meta],
            [chunk_in(v) for v in taken] + [full(v) for v in (wa, ba, gain1, shift1, kern, pos)],
            [
                (pl.BlockSpec(memory_space=pl.ANY) if 2 <= k < 5 else per_image(shape, first), struct((count,) + shape, dtype))
                for k, (shape, dtype) in enumerate(shapes)
            ],
            [blocks, low, pairs, pltpu.VMEM((2, HEADS, SIZE + 16, PIXELS // 2), BF16), high, low_blocks,
             pltpu.VMEM((HALF, PIXELS // 2), F32)] + save_scratch,
            5 * batch, dict(enumerate(held)), waits)

    def down_forward(k, taken, waits):
        first = k * batch
        out = pl.BlockSpec(memory_space=pl.ANY), struct((batch,) + flat, BF16)
        outs = call(
            functools.partial(forward_down_kernel, count, first), "down_forward", batch, [meta],
            [chunk_in(v) for v in taken] + [full(v) for v in (wd, bd, gain1, shift1, kern, pos)],
            [images_out(batch, half, BF16)] * 4
            + [out, out, out, images_out(batch, (HALF, PIXELS), BF16), images_out(batch, (8, PIXELS), F32)],
            [blocks, low, pairs, pltpu.VMEM((1, HEADS, SIZE + 16, PIXELS), BF16), high, low_blocks,
             pltpu.VMEM((HALF, PIXELS), F32)] + save_scratch,
            6 * batch, {}, waits)
        return outs[0:4], outs[4:]

    own0, sent0 = prepare(0, [])
    own0, keep_flags, triple_weight, query_value_bias, position_kernel = together(
        own0, keep_flags, triple_weight, query_value_bias, position_kernel
    )
    kept = jnp.sum(keep_flags.astype(F32), axis=0)
    for step, bit in enumerate(bits_of(lax.axis_size("batch"))):
        kept = kept_step(kept, bit)
        if step == 0:
            own0, kept = together(own0, kept)
    share = kept / (count * lax.axis_size("batch"))
    factors = (keep_flags.astype(F32) / share).reshape(-1)

    def branch_weight(lo):
        return jnp.concatenate([triple_weight[:, DIM * k + lo : DIM * k + lo + HALF] for k in range(3)], axis=1)

    wa, wd = branch_weight(0), branch_weight(HALF)
    zeros = jnp.zeros((HALF,), F32)
    ba = jnp.concatenate([query_value_bias[0, :HALF], zeros, query_value_bias[1, :HALF]])[None]
    bd = jnp.concatenate([query_value_bias[0, HALF:], zeros, query_value_bias[1, HALF:]])[None]
    gain1, shift1 = first_gain[None], first_shift[None]
    gain2, shift2 = second_gain[None], second_shift[None]
    kern = jnp.pad(position_kernel.reshape(9, DIM), ((0, 7), (0, 0)))
    pos = position_bias[None]

    col0 = col_exchange(*sent0)
    row0 = row_exchange(own0)
    own1, sent1 = prepare(1, [factors])
    across0 = across_forward(0, col0, [], own1[0:1])
    own1, sent1, across_done = together(own1, sent1, across0[0])
    across0[0] = across_done
    col1 = col_exchange(*sent1)
    row1 = row_exchange(own1)
    joined0, saved0 = down_forward(0, row0, across0[0:1])
    across1 = across_forward(1, col1, across0, saved0[0:1])
    joined_across = col_exchange(*across1[0:2])
    joined1, saved1 = down_forward(1, row1, across1[2:3])
    row_joined0 = row_exchange(joined0)
    row_joined1 = row_exchange(joined1)

    def middle(k, own, row_joined, held, sums, waits):
        first = k * batch
        acc_shape = (DIM, 2 * HIDDEN + DIM)
        return call(
            functools.partial(middle_kernel, count, first), "middle", batch, [meta, factors],
            [chunk_in(v) for v in own + row_joined]
            + [(per_image(v.shape[1:], first), v) for v in joined_across + [out_grad]]
            + [full(v) for v in (mixing_weight, mixing_bias[None], gain2, shift2, expand_weight, expand_bias[None],
                                 reduce_weight, reduce_bias[None])]
            + ([(pl.BlockSpec(memory_space=pl.ANY), sums[0]), full(sums[1])] if sums else []),
            [all_images((ROWS, ROWS, DIM), BF16, first), all_images((4,) + pix, BF16, first)]
            + [images_out(batch, half, BF16)] * 4 + [images_out(batch, pair_half, BF16)] * 2
            + [whole_out(acc_shape, BF16), whole_out((8, DIM))],
            [pltpu.VMEM(acc_shape, F32), pltpu.VMEM((4,) + pix, BF16), parts_high,
             pltpu.VMEM((4, ROWS, SLOT, HALF), F32), pltpu.VMEM((4,) + pix, BF16), parts_high, parts_high, wide]
            + ([pltpu.VMEM(acc_shape, BF16), pltpu.SemaphoreType.DMA] if sums else []),
            8 * batch, held, waits)

    mid0 = middle(0, own0, row_joined0, {}, [], saved1[0:1])
    row_grad0 = row_exchange(mid0[2:6])
    col_grad0 = col_exchange(*mid0[6:8])
    mid1 = middle(1, own1, row_joined1, {0: mid0[0], 1: mid0[1]}, mid0[8:10], [])
    output, middles = mid1[0:2]
    feed, row_grad0, col_grad0 = together(mid1[8], row_grad0, col_grad0)
    row_grad1 = row_exchange(mid1[2:6])
    col_grad1 = col_exchange(*mid1[6:8])
    received = send_shares(feed, NEAR)

    back_scratch = [high, high, high, blocks, pltpu.VMEM((8, PIXELS), F32), pltpu.VMEM((HALF, PIXELS), F32)]
    back_shape = (VEC + 16, 3 * DIM)

    def early_scratch(sums):
        return [pltpu.VMEM(back_shape, F32), pltpu.SemaphoreType.DMA] if sums else []

    def down_backward(k, taken, row_grad, saved, sums, waits):
        first = k * batch
        outs = call(
            functools.partial(backward_down_kernel, count, first, not sums), "down_backward", batch, [meta],
            [chunk_in(v) for v in taken + row_grad + saved] + [full(v) for v in (wd, gain1, shift1, kern)]
            + [(pl.BlockSpec(memory_space=pl.ANY), v) for v in sums],
            [images_out(batch, pix, BF16)] * 4 + [whole_out(back_shape)],
            [blocks, low, low, pairs, pltpu.VMEM((1, HALF, PIXELS), BF16)] + back_scratch + early_scratch(sums),
            11 * batch, {}, waits)
        return outs[0:4], outs[4:]

    def across_backward(k, taken, col_grad, sums, waits):
        first = k * batch
        last = k == chunks - 1
        out = whole_out((DIM, PACKED), BF16) if last else whole_out(back_shape)
        outs = call(
            functools.partial(backward_across_kernel, count, first, not sums, last), "across_backward", batch, [meta],
            [chunk_in(v) for v in taken + col_grad] + [(per_image(v.shape[1:], first), v) for v in across1[2:]]
            + [full(v) for v in (wa, gain1, shift1, kern)]
            + [(pl.BlockSpec(memory_space=pl.ANY), v) for v in sums[:1]] + [full(v) for v in sums[1:]],
            [images_out(batch, pair, BF16)] * 2 + [out],
            [pltpu.VMEM(back_shape, F32), blocks, low, low, pairs, pltpu.VMEM((2, HALF, PIXELS // 2), BF16)]
            + back_scratch + early_scratch(sums), 9 * batch, {}, waits)
        return outs[0:2], outs[2]

    part0, sums = across_backward(0, col0, col_grad0, [], mid1[8:9] + row_grad0[1:])
    col_part0 = col_exchange(*part0)
    received, sums, row_grad1, col_grad1 = together(received, sums, row_grad1, col_grad1)
    share = sum_shares(received)
    others = send_rows(share)
    part0, sums = down_backward(0, row0, row_grad0, saved0, [sums], row_grad1[1:] + col_grad1[1:])
    row_part0 = row_exchange(part0)
    others, sums, col_part0 = together(others, sums, col_part0)
    feed = gather_spread(spread_share(sum_shares(jnp.stack([share] + others)), NEAR), NEAR)
    part1, sums = down_backward(1, row1, row_grad1, saved1, sums, col_part0[1:])
    row_part1 = row_exchange(part1)
    feed, sums = together(feed, sums)
    part1, back = across_backward(1, col1, col_grad1, sums + [mid1[9]], row_part0[1:])
    col_part1 = col_exchange(*part1)
    back, row_part1, col_part0 = together(back, row_part1, col_part0)
    received = send_shares(back, ALL)

    def finish(k, row_part, col_part, held, waits):
        first = k * batch
        return call(
            functools.partial(finish_kernel, count, first), "finish", batch, [meta],
            [(per_image(middles.shape[1:], first), middles)] + [chunk_in(v) for v in row_part + col_part],
            [grid_out(first)], [parts_high, wide], 2 * batch, held, waits)

    feed = feed.astype(F32)
    feed = [feed[:, 0:HIDDEN].T, feed[:, HIDDEN : 2 * HIDDEN], feed[:, 2 * HIDDEN :]]
    grad0 = finish(0, row_part0, col_part0, {}, [back])
    sent = spread_share(sum_shares(received), ALL)
    sent, feed, grad0, col_part1 = together(sent, feed, grad0, col_part1)
    rows = gather_spread(sent, ALL)
    tokens_grad = finish(1, row_part1, col_part1, {0: grad0[0]}, [])[0]
    back_rows = rows.astype(F32)

    triple_weight_grad = back_rows[:, 0 : 3 * DIM]
    vectors = back_rows[0:48, 3 * DIM :].reshape(24, DIM)
    rows = vectors[16:24]
    return (
        output,
        tokens_grad,
        vectors[0],
        vectors[1],
        triple_weight_grad,
        vectors[2:4],
        vectors[5:14].reshape(3, 3, DIM),
        vectors[4],
        feed[2],
        rows[7],
        rows[5],
        rows[6],
        feed[1],
        rows[0:4].reshape(HIDDEN),
        feed[0],
        rows[4],
    )


def solution(mesh):
    spread = P("batch", "row", "col", None)
    in_specs = (spread, P("batch"), P("batch"), P("batch", None), spread) + (P(),) * 14
    out_specs = (spread, spread) + (P(),) * 14
    devices = mesh.shape["batch"] * mesh.shape["row"] * mesh.shape["col"]
    return jax.shard_map(
        functools.partial(per_device, 2, devices),
        mesh=mesh, in_specs=in_specs, out_specs=out_specs, check_vma=False)
```
